32 devices in a mesh: ens: 2 (over y), row: 4 (over x, core), col: 4 (over z).
Axes of the slice: x: 2, y: 2, z: 4, core: 2. Of those that a mesh axis runs over, the one named last changes fastest.
Arguments:
- pair_state: bfloat16 [1024, 512, 128], P(('ens', 'row'), 'col'), parts along dimension 0, may hold values from -6 to 6
- pair_mask: int32 [1024, 512], P(('ens', 'row'), 'col'), parts along dimension 0, may hold values from 0 to 1, as said below
- norm_in_gain: float32 [2, 128], replicated, may hold values from 0.25 to 1.75
- norm_in_bias: float32 [2, 128], replicated, may hold values from -3 to 3
- proj_in: bfloat16 [2, 128, 256], replicated, may hold values from -0.5 to 0.5
- gate_in: bfloat16 [2, 128, 256], replicated, may hold values from -0.5 to 0.5
- norm_out_gain: float32 [2, 128], replicated, may hold values from 0.25 to 1.75
- norm_out_bias: float32 [2, 128], replicated, may hold values from -3 to 3
- proj_out: bfloat16 [2, 128, 128], replicated, may hold values from -0.5 to 0.5
- gate_out: bfloat16 [2, 128, 128], replicated, may hold values from -0.5 to 0.5
Outputs:
- pair_result: bfloat16 [1024, 512, 128], P(('ens', 'row'), 'col'), parts along dimension 0
The draws below stay inside these ranges and needn't reach their ends.
There are 2 independent parts, one for each index of `ens`. The reference program is written for one: setup_inputs(seed, part) draws one part's arguments, and reference() takes and returns one part's arrays. A program takes and returns all parts, laid end to end along the dimension named above; an argument that names none is the same for every part. Nothing has to cross between parts.
Inputs may be any that keep to these rules, and one draw needn't show every extreme that they name: pair_mask[i, j] = t[i] * t[j] for a 0/1 token validity t: every token at or above one valid length, which lies between 448 and 511, is invalid, and some tokens below it may be invalid too.
All inputs are finite; a program needn't handle non-finite values.
Results may differ from the reference program's by a relative error of at most 0.0055.
Values may be sent and summed in bfloat16 or wider, within the bound.
No kernel may reach another device: no remote copies, remote signals or barrier semaphores. Data moves between devices by JAX's collectives and lax.ppermute only.
A program may use at most 128 MiB of HBM per device.

```python
import jax
import jax.numpy as jnp
from jax import lax

C = 128
CH = 128
N = 512


def draw_pair_mask(key, part):
    key = jax.random.fold_in(key, 7)
    length_key = jax.random.fold_in(key, 1)
    token_key = jax.random.fold_in(key, 2)
    padding = jax.random.randint(length_key, (), 1, N // 8 + 1)
    valid_len = N - padding
    positions = jnp.arange(N, dtype=jnp.int32)
    resolved = jax.random.randint(token_key, (N,), 0, 16) != 0
    inside = jnp.logical_and(positions < valid_len, resolved)
    return jnp.logical_and(inside[:, None], inside[None, :]).astype(jnp.int32)


def steps_of(own_key, extent, cuts, low, top_value):
    factor_of = 1.0
    for dim, parts in cuts:
        steps = jax.random.uniform(jax.random.fold_in(jax.random.fold_in(own_key, 6), dim), (parts,), jnp.float32, low / len(cuts), top_value / len(cuts))
        factor_of = factor_of * jnp.repeat(jnp.exp(steps), extent[dim] // parts).reshape((-1,) + (1,) * (len(extent) - 1 - dim))
    return factor_of


def centred(key, shape, scale, limit, shards=(), held_as=jnp.bfloat16):
    array = jax.random.normal(key, shape, jnp.float32) * scale
    if len(shards) > 0:
        array = steps_of(key, shape, shards, -0.22, 0.18) * array
    return jnp.clip(array, min=-limit, max=limit).astype(held_as)


def setup_inputs(seed: int = 0, part: int = 0) -> dict:
    keys = jax.random.split(jax.random.key(seed), 11)
    part_keys = jax.random.split(jax.random.fold_in(keys[10], part), 11)
    pair_state = centred(part_keys[0], (N, N, C), 1.0, 6.0, ((0, 4), (1, 4)))
    pair_mask = draw_pair_mask(jax.random.fold_in(jax.random.fold_in(keys[10], part), 71), part)
    norm_in_gain = jnp.clip(1.0 + 0.15 * jax.random.normal(keys[2], (2, C), jnp.float32), 0.25, 1.75)
    norm_in_bias = centred(keys[3], (2, C), 0.5, 3.0, (), jnp.float32)
    proj_in = centred(keys[4], (2, C, 2 * CH), C ** -0.5, 0.5)
    gate_in = centred(keys[5], (2, C, 2 * CH), C ** -0.5, 0.5)
    norm_out_gain = jnp.clip(1.0 + 0.15 * jax.random.normal(keys[6], (2, CH), jnp.float32), 0.25, 1.75)
    norm_out_bias = centred(keys[7], (2, CH), 0.5, 3.0, (), jnp.float32)
    proj_out = centred(keys[8], (2, CH, C), CH ** -0.5, 0.5)
    gate_out = centred(keys[9], (2, C, C), C ** -0.5, 0.5)
    return dict(pair_state=pair_state, pair_mask=pair_mask, norm_in_gain=norm_in_gain, norm_in_bias=norm_in_bias, proj_in=proj_in, gate_in=gate_in, norm_out_gain=norm_out_gain, norm_out_bias=norm_out_bias, proj_out=proj_out, gate_out=gate_out)


epsilon = 1e-05

def norm_last(values, norm_gain, norm_bias):
    centre = lax.optimization_barrier(jnp.mean(values, axis=-1, keepdims=True))
    variance = lax.optimization_barrier(jnp.mean(jnp.square(values - centre), axis=-1, keepdims=True))
    return (values - centre) * lax.rsqrt(variance + epsilon) * norm_gain + norm_bias

def reference(pair_state, pair_mask, norm_in_gain, norm_in_bias, proj_in, gate_in, norm_out_gain, norm_out_bias, proj_out, gate_out):
    row_block = min(N, 128)
    groups = N // row_block
    chan_block = min(CH, 16)
    current = pair_state
    for update in range(2):

        def front_end(pieces):
            pair_rows, mask_rows = pieces
            normed = norm_last(pair_rows.astype(jnp.float32), norm_in_gain[update], norm_in_bias[update]).astype(jnp.bfloat16)
            flat_rows = normed.reshape(-1, C)
            projected = jnp.dot(flat_rows, proj_in[update], preferred_element_type=jnp.float32)
            gate_logit = jnp.dot(flat_rows, gate_in[update], preferred_element_type=jnp.float32)
            weights = mask_rows.reshape(-1, 1).astype(jnp.float32)
            paired = (projected * jax.nn.sigmoid(gate_logit) * weights).astype(jnp.bfloat16)
            return paired.reshape(row_block, N, 2 * CH)
        paired = lax.map(front_end, (current.reshape(groups, row_block, N, C), pair_mask.reshape(groups, row_block, N)))
        paired = paired.reshape(N, N, 2 * CH)
        left_side = jnp.moveaxis(paired[:, :, :CH], 2, 0).reshape(CH // chan_block, chan_block, N, N)
        right_side = jnp.moveaxis(paired[:, :, CH:], 2, 0).reshape(CH // chan_block, chan_block, N, N)
        pattern = 'dik,djk->dij' if update == 0 else 'dki,dkj->dij'

        def triangle(pieces):
            left_part, right_part = pieces
            summed = jnp.einsum(pattern, left_part.astype(jnp.float32), right_part.astype(jnp.float32))
            return summed.astype(jnp.bfloat16)
        triangle_out = lax.map(triangle, (left_side, right_side)).reshape(CH, N, N)
        triangle_out = jnp.moveaxis(triangle_out, 0, 2)

        def back_end(pieces):
            pair_rows, tri_rows = pieces
            normed = norm_last(pair_rows.astype(jnp.float32), norm_in_gain[update], norm_in_bias[update]).astype(jnp.bfloat16)
            gate_value = jax.nn.sigmoid(jnp.dot(normed.reshape(-1, C), gate_out[update], preferred_element_type=jnp.float32))
            normed_out = norm_last(tri_rows.astype(jnp.float32).reshape(-1, CH), norm_out_gain[update], norm_out_bias[update]).astype(jnp.bfloat16)
            change = jnp.dot(normed_out, proj_out[update], preferred_element_type=jnp.float32) * gate_value
            summed = pair_rows.reshape(-1, C).astype(jnp.float32) + change
            return summed.astype(jnp.bfloat16).reshape(row_block, N, C)
        current = lax.map(back_end, (current.reshape(groups, row_block, N, C), triangle_out.reshape(groups, row_block, N, CH)))
        current = current.reshape(N, N, C)
    return current
```

```python
import jax
import jax.numpy as jnp
from jax import lax
from jax.experimental import pallas as pl
from jax.experimental.pallas import tpu as pltpu
from jax.sharding import PartitionSpec as P

epsilon = 1e-05


def norm_last(values, norm_gain, norm_bias):
    centre = jnp.mean(values, axis=-1, keepdims=True)
    variance = jnp.mean(jnp.square(values - centre), axis=-1, keepdims=True)
    return (values - centre) * lax.rsqrt(variance + epsilon) * norm_gain + norm_bias


def norm_first(values, norm_gain, norm_bias):
    centre = jnp.mean(values, axis=0, keepdims=True)
    variance = jnp.mean(jnp.square(values - centre), axis=0, keepdims=True)
    return (values - centre) * lax.rsqrt(variance + epsilon) * norm_gain[:, None, None] + norm_bias[
        :, None, None
    ]


def alternate(matrix):
    in_width, out_width = matrix.shape
    half_width = out_width // 2
    return matrix.reshape(in_width, 2, half_width).transpose(0, 2, 1).reshape(in_width, out_width)


def spread(paired):
    arrived = lax.all_to_all(paired, ("row", "col"), split_axis=0, concat_axis=1, tiled=True)
    n_row = lax.axis_size("row")
    n_col = lax.axis_size("col")
    channels, stacked, tile_cols = arrived.shape
    tile_rows = stacked // (n_row * n_col)
    arrived = arrived.reshape(channels, n_row, n_col, tile_rows, tile_cols).transpose(0, 1, 3, 2, 4)
    return arrived.reshape(channels, n_row * tile_rows, n_col * tile_cols)


def gather_back(triangle_out):
    n_row = lax.axis_size("row")
    n_col = lax.axis_size("col")
    channels, total_rows, total_cols = triangle_out.shape
    tile_rows = total_rows // n_row
    tile_cols = total_cols // n_col
    pieces = triangle_out.reshape(channels, n_row, tile_rows, n_col, tile_cols).transpose(
        1, 3, 0, 2, 4
    )
    pieces = pieces.reshape(n_row * n_col * channels, tile_rows, tile_cols)
    return lax.all_to_all(pieces, ("row", "col"), split_axis=0, concat_axis=0, tiled=True)


TILE = 128
SUB = 16
BLOCKS = TILE // SUB
VMEM_LIMIT = 40 * 1024 * 1024
BOTH = ("row", "col")
NT = (((1,), (1,)), ((), ()))
TN = (((0,), (0,)), ((), ()))


def norm_rows(rows, gain, bias):
    average = jnp.full((TILE, TILE), 1.0 / TILE, jnp.bfloat16)
    centre = jnp.dot(rows, average, preferred_element_type=jnp.float32)
    apart = rows.astype(jnp.float32) - centre
    spread_out = jnp.dot(
        (apart * apart).astype(jnp.bfloat16), average, preferred_element_type=jnp.float32
    )
    return (apart * lax.rsqrt(spread_out + epsilon) * gain + bias).astype(jnp.bfloat16)


def gated_pairs(normed, weights, mask_rows):
    both = lax.dot_general(weights, normed, NT, preferred_element_type=jnp.float32)
    half = both.shape[0] // 2
    projected = both[:half]
    paired = projected * jnp.tanh(both[half:]) + projected
    mask_flat = jnp.concatenate([mask_rows[r : r + 1, :] for r in range(SUB)], axis=1)
    paired = (paired * mask_flat).astype(jnp.bfloat16)
    return paired.reshape(half, SUB, TILE)


def changed_state(triangle, rows, normed, gain, bias, proj, gate):
    centre = jnp.mean(triangle, axis=0, keepdims=True)
    apart = triangle - centre
    variance = jnp.mean(apart * apart, axis=0, keepdims=True)
    wide_gain = jnp.concatenate([gain] * SUB, axis=1)
    wide_bias = jnp.concatenate([bias] * SUB, axis=1)
    normed_out = (apart * lax.rsqrt(variance + epsilon) * wide_gain + wide_bias).astype(jnp.bfloat16)
    out = lax.dot_general(normed_out, proj, TN, preferred_element_type=jnp.float32)
    gate_value = jnp.tanh(jnp.dot(normed, gate, preferred_element_type=jnp.float32))
    return (rows.astype(jnp.float32) + (out * gate_value + out)).astype(jnp.bfloat16)


def enter_kernel(at, own, sib, mask, gain, bias, weights, *rest):
    state_out, left_out, right_out = rest[-3:]
    step = pl.program_id(0)
    use_own = (step == 1) == (at[4] == 1)
    picked = jnp.where(use_own, own[...], sib[...])
    rows = picked.reshape(SUB * TILE, TILE)
    normed = norm_rows(rows, gain[...], bias[...])
    paired = gated_pairs(normed, weights[...], mask[0, 0].astype(jnp.float32))
    half = paired.shape[0] // 2
    left_out[0] = paired[:half]
    right_out[0] = paired[half:]

    @pl.when(use_own)
    def _():
        state_out[0, 0] = picked


def enter(own, sib, first_block, at, mask, gain, bias, weights, held):
    n_block = own.shape[0] // SUB
    full = pl.BlockSpec(memory_space=pl.ANY)

    def core_of(step, at):
        return jnp.where(step == 1, at[2], 1 - at[2])

    def is_own(step, at):
        return (step == 1) == (at[4] == 1)

    def own_map(step, block, at):
        return (jnp.where(is_own(step, at), block, jnp.where(step == 0, 0, n_block - 1)), 0, 0)

    def sib_map(step, block, at):
        return (jnp.where(is_own(step, at), jnp.where(step == 0, 0, n_block - 1), block), 0, 0)

    def mask_map(step, block, at):
        return (2 * at[0] + core_of(step, at), at[1], first_block + block, 0)

    def state_map(step, block, at):
        kept = jnp.where(is_own(step, at), block, jnp.where(step == 0, 0, n_block - 1))
        return (at[0], at[1], first_block + kept, 0, 0)

    def left_map(step, block, at):
        return (at[1], 0, (2 * at[0] + core_of(step, at)) * BLOCKS + first_block + block, 0)

    def right_map(step, block, at):
        slot = jnp.where(at[3] == 1, core_of(step, at), 2)
        return (at[1], 0, slot * BLOCKS + first_block + block, 0)

    half = weights.shape[0] // 4
    same = lambda step, block, at: (0, 0)
    shapes = (
        jax.ShapeDtypeStruct((2, 4, TILE, TILE, TILE), jnp.bfloat16),
        jax.ShapeDtypeStruct((4, half, 4 * TILE, TILE), jnp.bfloat16),
        jax.ShapeDtypeStruct((4, half, 3 * TILE, TILE), jnp.bfloat16),
    )
    in_specs = [
        pl.BlockSpec((SUB, TILE, TILE), own_map),
        pl.BlockSpec((SUB, TILE, TILE), sib_map),
        pl.BlockSpec((1, 1, SUB, TILE), mask_map),
        pl.BlockSpec((1, TILE), same),
        pl.BlockSpec((1, TILE), same),
        pl.BlockSpec((4 * half, TILE), same),
    ]
    operands = [own, sib, mask, gain, bias, weights]
    aliases = {}
    if held is not None:
        aliases = {len(operands) + 1 + n: n for n in range(3)}
        operands += list(held)
        in_specs += [full] * 3
    pairs = 2 * own.shape[0] * TILE
    return pl.pallas_call(
        enter_kernel,
        grid_spec=pltpu.PrefetchScalarGridSpec(
            num_scalar_prefetch=1,
            grid=(2, n_block),
            in_specs=in_specs,
            out_specs=[
                pl.BlockSpec((1, 1, SUB, TILE, TILE), state_map),
                pl.BlockSpec((1, half, SUB, TILE), left_map),
                pl.BlockSpec((1, half, SUB, TILE), right_map),
            ],
        ),
        out_shape=shapes,
        input_output_aliases=aliases,
        compiler_params=pltpu.CompilerParams(
            dimension_semantics=("arbitrary", "arbitrary"), vmem_limit_bytes=VMEM_LIMIT
        ),
        cost_estimate=pl.CostEstimate(
            flops=pairs * TILE * 1024, bytes_accessed=pairs * 1024, transcendentals=pairs * TILE
        ),
        name="enter",
    )(at, *operands)


def outgoing_kernel(at, left, right, keep, send):
    core = at[0]
    third = pl.multiple_of(at[1] * TILE, TILE)

    def wide(ref, start, count):
        return jnp.concatenate([ref[k, 0, pl.ds(start, count), :] for k in range(4)], axis=1)

    near = wide(right, 0, 2 * TILE)
    far = wide(right, third, TILE)
    for out, which in ((keep, core), (send, 1 - core)):
        rows = jnp.concatenate(
            [wide(left, pl.multiple_of((2 * x + which) * TILE, TILE), TILE) for x in range(2)], axis=0
        )
        first = lax.dot_general(rows, near, NT, preferred_element_type=jnp.float32)
        out[0, 0] = first[:, :TILE].astype(jnp.bfloat16)
        out[1, 0] = first[:, TILE:].astype(jnp.bfloat16)
        out[2, 0] = lax.dot_general(rows, far, NT, preferred_element_type=jnp.float32).astype(
            jnp.bfloat16
        )


def outgoing(at, left, right):
    half = left.shape[1]
    out = jax.ShapeDtypeStruct((3, half, 2 * TILE, TILE), jnp.bfloat16)
    return pl.pallas_call(
        outgoing_kernel,
        grid_spec=pltpu.PrefetchScalarGridSpec(
            num_scalar_prefetch=1,
            grid=(half,),
            in_specs=[
                pl.BlockSpec((4, 1, 4 * TILE, TILE), lambda d, at: (0, d, 0, 0)),
                pl.BlockSpec((4, 1, 3 * TILE, TILE), lambda d, at: (0, d, 0, 0)),
            ],
            out_specs=[pl.BlockSpec((3, 1, 2 * TILE, TILE), lambda d, at: (0, d, 0, 0))] * 2,
        ),
        out_shape=(out, out),
        compiler_params=pltpu.CompilerParams(
            dimension_semantics=("arbitrary",), vmem_limit_bytes=VMEM_LIMIT
        ),
        cost_estimate=pl.CostEstimate(
            flops=half * 512 * 384 * 1024, bytes_accessed=half * 1300 * 1024, transcendentals=0
        ),
        name="outgoing",
    )(at, left, right)


def middle_kernel(
    at, kept, got, state, mask, gain0, bias0, gain_out, bias_out, proj, gate, gain1, bias1, weights,
    pairs_out, state_out,
):
    rows = state[0, 0].reshape(SUB * TILE, TILE)
    normed = norm_rows(rows, gain0[...], bias0[...])
    triangle = jnp.concatenate([kept[0], got[0]], axis=0).reshape(TILE, SUB * TILE)
    changed = changed_state(
        triangle.astype(jnp.float32), rows, normed, gain_out[...], bias_out[...], proj[...], gate[...]
    )
    normed1 = norm_rows(changed, gain1[...], bias1[...])
    pairs_out[0] = gated_pairs(normed1, weights[0], mask[0, 0].astype(jnp.float32))
    state_out[...] = changed.reshape(SUB, TILE, TILE)


def middle(at, kept, got, states, mask, gain0, bias0, gain_out, bias_out, proj, gate, gain1, bias1, weights):
    half = kept.shape[1]

    def column(slot, at):
        return jnp.where(slot == 2, at[2], 2 * at[1] + slot)

    same = lambda slot, x, block, at: (0, 0)
    row = pl.BlockSpec((1, TILE), same)
    square = pl.BlockSpec((TILE, TILE), same)
    tri = pl.BlockSpec((1, half, SUB, TILE), lambda slot, x, block, at: (slot, 0, x * BLOCKS + block, 0))
    pairs = 6 * TILE * TILE
    return pl.pallas_call(
        middle_kernel,
        grid_spec=pltpu.PrefetchScalarGridSpec(
            num_scalar_prefetch=1,
            grid=(3, 2, BLOCKS),
            in_specs=[
                tri,
                tri,
                pl.BlockSpec(
                    (1, 1, SUB, TILE, TILE),
                    lambda slot, x, block, at: (x, column(slot, at), block, 0, 0),
                ),
                pl.BlockSpec(
                    (1, 1, SUB, TILE),
                    lambda slot, x, block, at: (2 * x + at[0], column(slot, at), block, 0),
                ),
                row,
                row,
                square,
                square,
                square,
                square,
                row,
                row,
                pl.BlockSpec(
                    (1, 2 * TILE, TILE),
                    lambda slot, x, block, at: (jnp.where(slot == 2, 1, 0), 0, 0),
                ),
            ],
            out_specs=[
                pl.BlockSpec(
                    (1, TILE, SUB, TILE), lambda slot, x, block, at: (slot, 0, x * BLOCKS + block, 0)
                ),
                pl.BlockSpec(
                    (SUB, TILE, TILE),
                    lambda slot, x, block, at: (
                        jnp.where(slot == 2, x * BLOCKS + block, 2 * BLOCKS), 0, 0,
                    ),
                ),
            ],
        ),
        out_shape=(
            jax.ShapeDtypeStruct((3, TILE, 2 * TILE, TILE), jnp.bfloat16),
            jax.ShapeDtypeStruct(((2 * BLOCKS + 1) * SUB, TILE, TILE), jnp.bfloat16),
        ),
        compiler_params=pltpu.CompilerParams(
            dimension_semantics=("arbitrary",) * 3, vmem_limit_bytes=VMEM_LIMIT
        ),
        cost_estimate=pl.CostEstimate(
            flops=pairs * TILE * 1024, bytes_accessed=pairs * 1024, transcendentals=pairs * TILE * 2
        ),
        name="middle",
    )(at, kept, got, states, mask, gain0, bias0, gain_out, bias_out, proj, gate, gain1, bias1, weights)


CHANNELS = 8


def incoming_kernel(at, pairs, keep, send):
    core = at[0]
    for d in range(CHANNELS):
        right = pairs[2, d]
        keep[d] = lax.dot_general(pairs[core, d], right, TN, preferred_element_type=jnp.float32)
        send[d] = lax.dot_general(
            pairs[1 - core, d], right, TN, preferred_element_type=jnp.float32
        ).astype(jnp.bfloat16)


def incoming(at, pairs):
    out_spec = pl.BlockSpec((CHANNELS, TILE, TILE), lambda d, at: (d, 0, 0))
    return pl.pallas_call(
        incoming_kernel,
        grid_spec=pltpu.PrefetchScalarGridSpec(
            num_scalar_prefetch=1,
            grid=(TILE // CHANNELS,),
            in_specs=[pl.BlockSpec((3, CHANNELS, 2 * TILE, TILE), lambda d, at: (0, d, 0, 0))],
            out_specs=[out_spec, out_spec],
        ),
        out_shape=(
            jax.ShapeDtypeStruct((TILE, TILE, TILE), jnp.float32),
            jax.ShapeDtypeStruct((TILE, TILE, TILE), jnp.bfloat16),
        ),
        compiler_params=pltpu.CompilerParams(
            dimension_semantics=("arbitrary",), vmem_limit_bytes=VMEM_LIMIT
        ),
        cost_estimate=pl.CostEstimate(
            flops=TILE * 512 * 256 * TILE, bytes_accessed=36 * 2**20, transcendentals=0
        ),
        name="incoming",
    )(at, pairs)


def leave_kernel(at, kept, got, state, gain1, bias1, gain_out, bias_out, proj, gate, result):
    rows = state[...].reshape(SUB * TILE, TILE)
    normed = norm_rows(rows, gain1[...], bias1[...])
    summed = (kept[...] + got[...].astype(jnp.float32)).astype(jnp.bfloat16)
    triangle = summed.reshape(TILE, SUB * TILE).astype(jnp.float32)
    changed = changed_state(triangle, rows, normed, gain_out[...], bias_out[...], proj[...], gate[...])
    result[...] = changed.reshape(SUB, TILE, TILE)


def leave(at, kept, got, states, gain1, bias1, gain_out, bias_out, proj, gate):
    same = lambda block, at: (0, 0)
    row = pl.BlockSpec((1, TILE), same)
    square = pl.BlockSpec((TILE, TILE), same)
    tri = pl.BlockSpec((TILE, SUB, TILE), lambda block, at: (0, block, 0))
    return pl.pallas_call(
        leave_kernel,
        grid_spec=pltpu.PrefetchScalarGridSpec(
            num_scalar_prefetch=1,
            grid=(BLOCKS,),
            in_specs=[
                tri,
                tri,
                pl.BlockSpec((SUB, TILE, TILE), lambda block, at: (at[1] * BLOCKS + block, 0, 0)),
                row,
                row,
                square,
                square,
                square,
                square,
            ],
            out_specs=pl.BlockSpec((SUB, TILE, TILE), lambda block, at: (block, 0, 0)),
        ),
        out_shape=jax.ShapeDtypeStruct((TILE, TILE, TILE), jnp.bfloat16),
        compiler_params=pltpu.CompilerParams(
            dimension_semantics=("arbitrary",), vmem_limit_bytes=VMEM_LIMIT
        ),
        cost_estimate=pl.CostEstimate(
            flops=TILE**3 * 512, bytes_accessed=20 * 2**20, transcendentals=TILE**3
        ),
        name="leave",
    )(at, kept, got, states, gain1, bias1, gain_out, bias_out, proj, gate)


def on_device_ring(
    pair_state,
    pair_mask,
    norm_in_gain,
    norm_in_bias,
    proj_in,
    gate_in,
    norm_out_gain,
    norm_out_bias,
    proj_out,
    gate_out,
):
    row = lax.axis_index("row")
    z = lax.axis_index("col")
    x, core = row // 2, row % 2
    place = jnp.where(x == 0, z, 7 - z)

    def device(position, which):
        on_x, on_z = (0, position) if position < 4 else (1, 7 - position)
        return (2 * on_x + which) * 4 + on_z

    up = [(device(p, w), device((p + 1) % 8, w)) for p in range(8) for w in range(2)]
    down = [(target, source) for source, target in up]
    swap = [(device(p, w), device(p, 1 - w)) for p in range(8) for w in range(2)]

    mask = lax.all_gather(pair_mask.astype(jnp.bfloat16), BOTH).reshape(4, 4, TILE, TILE)

    half = TILE // 2
    ours = core * half
    theirs = half - ours

    def halved(matrix, start, width):
        return (0.5 * lax.dynamic_slice_in_dim(matrix, start, width, axis=1)).T

    enter_weights = jnp.concatenate(
        [halved(m[0], side + ours, half) for m in (proj_in, gate_in) for side in (0, TILE)], axis=0
    )
    middle_weights = jnp.stack(
        [
            jnp.concatenate([halved(m[1], side, TILE) for m in (proj_in, gate_in)], axis=0)
            for side in (0, TILE)
        ]
    )
    gain_in = [norm_in_gain[u].reshape(1, TILE) for u in range(2)]
    bias_in = [norm_in_bias[u].reshape(1, TILE) for u in range(2)]

    def reordered(values):
        return jnp.concatenate(
            [lax.dynamic_slice_in_dim(values, start, half, axis=0) for start in (ours, theirs)], axis=0
        )

    def columns(values):
        return jnp.broadcast_to(values[:, None], (TILE, TILE))

    def project(held, offset, own, sib, first_block):
        there = lax.rem(place + offset, 8)
        there_x = there // 4
        there_z = jnp.where(there_x == 0, there, 7 - there)
        last = lax.rem(z, 2)
        at = jnp.stack(
            [there_x, there_z, last, (there_x == x).astype(jnp.int32), (last == core).astype(jnp.int32)]
        ).astype(jnp.int32)
        return enter(own, sib, first_block, at, mask, gain_in[0], bias_in[0], enter_weights, held)

    held = project(None, 0, pair_state, lax.ppermute(pair_state, BOTH, swap), 0)
    from_below = lax.ppermute(pair_state, BOTH, up)
    from_above = lax.ppermute(pair_state, BOTH, down)
    for step in range(1, 4):
        from_below, from_above, held = lax.optimization_barrier((from_below, from_above, held))
        now_below, now_above = from_below, from_above
        if step < 3:
            from_below = lax.ppermute(now_below, BOTH, up)
            from_above = lax.ppermute(now_above, BOTH, down)
        else:
            part = TILE // 2
            from_below = lax.ppermute(now_below[:part], BOTH, up)
            from_above = lax.ppermute(now_above[part:], BOTH, down)
        held = project(held, 8 - step, now_below, lax.ppermute(now_below, BOTH, swap), 0)
        held = project(held, step, now_above, lax.ppermute(now_above, BOTH, swap), 0)
    from_below, from_above, held = lax.optimization_barrier((from_below, from_above, held))
    held = project(held, 4, from_below, lax.ppermute(from_below, BOTH, swap), 0)
    held = project(held, 4, from_above, lax.ppermute(from_above, BOTH, swap), part // SUB)
    states, left, right = held

    third = jnp.where(z // 2 == x, lax.rem(z, 2), 2)
    kept, sent = outgoing(jnp.stack([core, third]).astype(jnp.int32), left, right)
    got = lax.ppermute(sent, BOTH, swap)
    at = jnp.stack([core, x, z]).astype(jnp.int32)
    pairs, states1 = middle(
        at,
        kept,
        got,
        states,
        mask,
        gain_in[0],
        bias_in[0],
        columns(reordered(norm_out_gain[0])),
        columns(reordered(norm_out_bias[0])),
        0.5 * reordered(proj_out[0]),
        0.5 * gate_out[0],
        gain_in[1],
        bias_in[1],
        middle_weights,
    )
    kept1, sent1 = incoming(at, pairs)
    got1 = lax.ppermute(sent1, BOTH, swap)
    return leave(
        at,
        kept1,
        got1,
        states1,
        gain_in[1],
        bias_in[1],
        columns(norm_out_gain[1]),
        columns(norm_out_bias[1]),
        0.5 * proj_out[1],
        0.5 * gate_out[1],
    )


def on_device_exchange(
    pair_state,
    pair_mask,
    norm_in_gain,
    norm_in_bias,
    proj_in,
    gate_in,
    norm_out_gain,
    norm_out_bias,
    proj_out,
    gate_out,
):
    mask_weight = pair_mask.astype(jnp.float32)[None]
    current = pair_state
    for update in range(2):
        normed = norm_last(
            current.astype(jnp.float32), norm_in_gain[update], norm_in_bias[update]
        ).astype(jnp.bfloat16)
        projected = jnp.einsum(
            "rcd,de->erc", normed, alternate(proj_in[update]), preferred_element_type=jnp.float32
        )
        gate_logit = jnp.einsum(
            "rcd,de->erc", normed, alternate(gate_in[update]), preferred_element_type=jnp.float32
        )
        paired = (projected * jax.nn.sigmoid(gate_logit) * mask_weight).astype(jnp.bfloat16)
        arrived = spread(paired)
        doubled, total_rows, total_cols = arrived.shape
        pair_count = doubled // 2
        arrived = arrived.reshape(pair_count, 2, total_rows, total_cols)
        left_side = arrived[:, 0]
        right_side = arrived[:, 1]
        pattern = "dik,djk->dij" if update == 0 else "dki,dkj->dij"
        triangle_out = jnp.einsum(
            pattern, left_side, right_side, preferred_element_type=jnp.float32
        ).astype(jnp.bfloat16)
        returned = gather_back(triangle_out)
        normed_out = norm_first(
            returned.astype(jnp.float32), norm_out_gain[update], norm_out_bias[update]
        ).astype(jnp.bfloat16)
        gate_value = jax.nn.sigmoid(
            jnp.einsum("rcd,df->rcf", normed, gate_out[update], preferred_element_type=jnp.float32)
        )
        change = (
            jnp.einsum(
                "erc,ef->rcf", normed_out, proj_out[update], preferred_element_type=jnp.float32
            )
            * gate_value
        )
        current = (current.astype(jnp.float32) + change).astype(jnp.bfloat16)
    return current


def on_device(pair_state, *others):
    square = pair_state.shape == (TILE, TILE, TILE)
    if square and lax.axis_size("row") == 4 and lax.axis_size("col") == 4:
        return on_device_ring(pair_state, *others)
    return on_device_exchange(pair_state, *others)


def solution(mesh):
    return jax.shard_map(
        on_device,
        mesh=mesh,
        in_specs=(
            P(("ens", "row"), "col", None),
            P(("ens", "row"), "col"),
            P(),
            P(),
            P(),
            P(),
            P(),
            P(),
            P(),
            P(),
        ),
        out_specs=P(("ens", "row"), "col", None),
        check_vma=False,
    )
```

```python
import jax
import jax.numpy as jnp
from jax import lax
from jax.experimental import pallas as pl
from jax.experimental.pallas import tpu as pltpu
from jax.sharding import PartitionSpec as P

epsilon = 1e-05


def norm_last(values, norm_gain, norm_bias):
    centre = jnp.mean(values, axis=-1, keepdims=True)
    variance = jnp.mean(jnp.square(values - centre), axis=-1, keepdims=True)
    return (values - centre) * lax.rsqrt(variance + epsilon) * norm_gain + norm_bias


def norm_first(values, norm_gain, norm_bias):
    centre = jnp.mean(values, axis=0, keepdims=True)
    variance = jnp.mean(jnp.square(values - centre), axis=0, keepdims=True)
    return (values - centre) * lax.rsqrt(variance + epsilon) * norm_gain[:, None, None] + norm_bias[
        :, None, None
    ]


def alternate(matrix):
    in_width, out_width = matrix.shape
    half_width = out_width // 2
    return matrix.reshape(in_width, 2, half_width).transpose(0, 2, 1).reshape(in_width, out_width)


def spread(paired):
    arrived = lax.all_to_all(paired, ("row", "col"), split_axis=0, concat_axis=1, tiled=True)
    n_row = lax.axis_size("row")
    n_col = lax.axis_size("col")
    channels, stacked, tile_cols = arrived.shape
    tile_rows = stacked // (n_row * n_col)
    arrived = arrived.reshape(channels, n_row, n_col, tile_rows, tile_cols).transpose(0, 1, 3, 2, 4)
    return arrived.reshape(channels, n_row * tile_rows, n_col * tile_cols)


def gather_back(triangle_out):
    n_row = lax.axis_size("row")
    n_col = lax.axis_size("col")
    channels, total_rows, total_cols = triangle_out.shape
    tile_rows = total_rows // n_row
    tile_cols = total_cols // n_col
    pieces = triangle_out.reshape(channels, n_row, tile_rows, n_col, tile_cols).transpose(
        1, 3, 0, 2, 4
    )
    pieces = pieces.reshape(n_row * n_col * channels, tile_rows, tile_cols)
    return lax.all_to_all(pieces, ("row", "col"), split_axis=0, concat_axis=0, tiled=True)


TILE = 128
SUB = 16
BLOCKS = TILE // SUB
VMEM_LIMIT = 40 * 1024 * 1024
BOTH = ("row", "col")
NT = (((1,), (1,)), ((), ()))
TN = (((0,), (0,)), ((), ()))


def channels_first(rows, matrix):
    return lax.dot_general(matrix, rows, NT, preferred_element_type=jnp.float32)


def norm_apart(apart, gain, bias):
    variance = jnp.mean(apart * apart, axis=0, keepdims=True)
    wide_gain = jnp.concatenate([gain] * SUB, axis=1)
    wide_bias = jnp.concatenate([bias] * SUB, axis=1)
    return (apart * lax.rsqrt(variance + epsilon) * wide_gain + wide_bias).astype(jnp.bfloat16)


def norm_channels(values, gain, bias):
    return norm_apart(values - jnp.mean(values, axis=0, keepdims=True), gain, bias)


def gated(weights, normed):
    both = jnp.dot(weights, normed, preferred_element_type=jnp.float32)
    half = both.shape[0] // 2
    return both[:half] * jnp.tanh(both[half:]) + both[:half]


def masked_tiles(paired, mask_rows, turn):
    channels = paired.shape[0]
    for r in range(SUB):
        turn[pl.ds(r, channels, stride=SUB), :] = (
            paired[:, r * TILE : (r + 1) * TILE] * mask_rows[r : r + 1, :]
        )
    return turn[...].astype(jnp.bfloat16).reshape(channels, SUB, TILE)


def flat_channels(turn):
    return jnp.concatenate([turn[pl.ds(r, TILE, stride=SUB), :] for r in range(SUB)], axis=1)


def enter_kernel(at, own, sib, mask, centre, gain, bias, weights, *rest):
    state_out, left_out, right_out, mask_out, turn = rest[-5:]
    step = pl.program_id(0)
    use_own = (step == 1) == (at[4] == 1)
    picked = jnp.where(use_own, own[...], sib[...])
    apart = channels_first(picked.reshape(SUB * TILE, TILE), centre[...])
    normed = norm_apart(apart, gain[...], bias[...])
    paired = masked_tiles(gated(weights[...], normed), mask[0].astype(jnp.float32), turn)
    half = paired.shape[0] // 2
    left_out[0] = paired[:half]
    right_out[0] = paired[half:]
    mask_out[0, 0] = mask[0]

    @pl.when(use_own)
    def _():
        state_out[0, 0] = picked


def enter(own, sib, first_block, at, mask, centre, gain, bias, weights, held):
    n_block = own.shape[0] // SUB
    full = pl.BlockSpec(memory_space=pl.ANY)

    def core_of(step, at):
        return jnp.where(step == 1, at[2], 1 - at[2])

    def is_own(step, at):
        return (step == 1) == (at[4] == 1)

    def own_map(step, block, at):
        return (jnp.where(is_own(step, at), block, jnp.where(step == 0, 0, n_block - 1)), 0, 0)

    def sib_map(step, block, at):
        return (jnp.where(is_own(step, at), jnp.where(step == 0, 0, n_block - 1), block), 0, 0)

    def mask_map(step, block, at):
        return (core_of(step, at), first_block + block, 0)

    def mask_out_map(step, block, at):
        return (2 * at[0] + core_of(step, at), at[1], first_block + block, 0)

    def state_map(step, block, at):
        kept = jnp.where(is_own(step, at), block, jnp.where(step == 0, 0, n_block - 1))
        return (at[0], at[1], first_block + kept, 0, 0)

    def left_map(step, block, at):
        return (at[1], 0, (2 * at[0] + core_of(step, at)) * BLOCKS + first_block + block, 0)

    def right_map(step, block, at):
        slot = jnp.where(at[3] == 1, core_of(step, at), 2)
        return (at[1], 0, slot * BLOCKS + first_block + block, 0)

    half = weights.shape[0] // 4
    same = lambda step, block, at: (0, 0)
    shapes = (
        jax.ShapeDtypeStruct((2, 4, TILE, TILE, TILE), jnp.bfloat16),
        jax.ShapeDtypeStruct((4, half, 4 * TILE, TILE), jnp.bfloat16),
        jax.ShapeDtypeStruct((4, half, 3 * TILE, TILE), jnp.bfloat16),
        jax.ShapeDtypeStruct((4, 4, TILE, TILE), jnp.bfloat16),
    )
    in_specs = [
        pl.BlockSpec((SUB, TILE, TILE), own_map),
        pl.BlockSpec((SUB, TILE, TILE), sib_map),
        pl.BlockSpec((1, SUB, TILE), mask_map),
        pl.BlockSpec((TILE, TILE), same),
        pl.BlockSpec((TILE, TILE), same),
        pl.BlockSpec((TILE, TILE), same),
        pl.BlockSpec((4 * half, TILE), same),
    ]
    operands = [own, sib, mask, centre, gain, bias, weights]
    aliases = {}
    if held is not None:
        aliases = {len(operands) + 1 + n: n for n in range(4)}
        operands += list(held)
        in_specs += [full] * 4
    pairs = 2 * own.shape[0] * TILE
    return pl.pallas_call(
        enter_kernel,
        grid_spec=pltpu.PrefetchScalarGridSpec(
            num_scalar_prefetch=1,
            grid=(2, n_block),
            in_specs=in_specs,
            out_specs=[
                pl.BlockSpec((1, 1, SUB, TILE, TILE), state_map),
                pl.BlockSpec((1, half, SUB, TILE), left_map),
                pl.BlockSpec((1, half, SUB, TILE), right_map),
                pl.BlockSpec((1, 1, SUB, TILE), mask_out_map),
            ],
            scratch_shapes=[pltpu.VMEM((2 * half * SUB, TILE), jnp.float32)],
        ),
        out_shape=shapes,
        input_output_aliases=aliases,
        compiler_params=pltpu.CompilerParams(
            dimension_semantics=("arbitrary", "arbitrary"), vmem_limit_bytes=VMEM_LIMIT
        ),
        cost_estimate=pl.CostEstimate(
            flops=pairs * TILE * 1024, bytes_accessed=pairs * 1024, transcendentals=pairs * TILE
        ),
        name="enter",
    )(at, *operands)


def outgoing_kernel(at, left, right, keep, send):
    core = at[0]
    third = pl.multiple_of(at[1] * TILE, TILE)

    def wide(ref, start, count):
        return jnp.concatenate([ref[k, 0, pl.ds(start, count), :] for k in range(4)], axis=1)

    columns = jnp.concatenate([wide(right, 0, 2 * TILE), wide(right, third, TILE)], axis=0)
    blocks = [2 * x + which for which in (core, 1 - core) for x in range(2)]
    rows = jnp.concatenate(
        [wide(left, pl.multiple_of(block * TILE, TILE), TILE) for block in blocks], axis=0
    )
    sums = lax.dot_general(rows, columns, NT, preferred_element_type=jnp.float32).astype(jnp.bfloat16)
    for slot in range(3):
        keep[slot, 0] = sums[: 2 * TILE, slot * TILE : (slot + 1) * TILE]
        send[slot, 0] = sums[2 * TILE :, slot * TILE : (slot + 1) * TILE]


PARTS = 4


def outgoing(at, left, right, part):
    count = left.shape[1] // PARTS
    first = part * count
    out = jax.ShapeDtypeStruct((3, count, 2 * TILE, TILE), jnp.bfloat16)
    return pl.pallas_call(
        outgoing_kernel,
        grid_spec=pltpu.PrefetchScalarGridSpec(
            num_scalar_prefetch=1,
            grid=(count,),
            in_specs=[
                pl.BlockSpec((4, 1, 4 * TILE, TILE), lambda d, at: (0, first + d, 0, 0)),
                pl.BlockSpec((4, 1, 3 * TILE, TILE), lambda d, at: (0, first + d, 0, 0)),
            ],
            out_specs=[pl.BlockSpec((3, 1, 2 * TILE, TILE), lambda d, at: (0, d, 0, 0))] * 2,
        ),
        out_shape=(out, out),
        compiler_params=pltpu.CompilerParams(
            dimension_semantics=("arbitrary",), vmem_limit_bytes=VMEM_LIMIT
        ),
        cost_estimate=pl.CostEstimate(
            flops=count * 512 * 384 * 1024, bytes_accessed=count * 1300 * 1024, transcendentals=0
        ),
        name="outgoing",
    )(at, left, right)


def middle_kernel(
    at, state, mask, both, gain0, bias0, gain_out, bias_out, proj, gate, gain1, bias1, weights, *rest
):
    parts, (pairs_out, state_out, turn) = rest[:-3], rest[-3:]
    turned = channels_first(state[0, 0].reshape(SUB * TILE, TILE), both[...])
    normed = norm_apart(turned[:TILE], gain0[...], bias0[...])
    height = TILE * SUB // len(parts)
    for n, part in enumerate(parts):
        turn[n * height : (n + 1) * height, :] = part[0].reshape(height, TILE).astype(jnp.float32)
    normed_out = norm_channels(flat_channels(turn), gain_out[...], bias_out[...])
    out = jnp.dot(proj[...], normed_out, preferred_element_type=jnp.float32)
    gate_value = jnp.tanh(jnp.dot(gate[...], normed, preferred_element_type=jnp.float32))
    changed = (turned[TILE:] + (out * gate_value + out)).astype(jnp.bfloat16)
    state_out[0] = changed
    normed1 = norm_channels(changed.astype(jnp.float32), gain1[...], bias1[...])
    pairs_out[0] = masked_tiles(gated(weights[0], normed1), mask[0, 0].astype(jnp.float32), turn)


def middle(at, states, mask, both, gain0, bias0, gain_out, bias_out, proj, gate, gain1, bias1, weights, parts):
    def column(slot, at):
        return jnp.where(slot == 2, at[2], 2 * at[1] + slot)

    square = pl.BlockSpec((TILE, TILE), lambda slot, x, block, at: (0, 0))
    tri = pl.BlockSpec(
        (1, parts[0].shape[1], SUB, TILE), lambda slot, x, block, at: (slot, 0, x * BLOCKS + block, 0)
    )
    pairs = 6 * TILE * TILE
    return pl.pallas_call(
        middle_kernel,
        grid_spec=pltpu.PrefetchScalarGridSpec(
            num_scalar_prefetch=1,
            grid=(3, 2, BLOCKS),
            in_specs=[
                pl.BlockSpec(
                    (1, 1, SUB, TILE, TILE),
                    lambda slot, x, block, at: (x, column(slot, at), block, 0, 0),
                ),
                pl.BlockSpec(
                    (1, 1, SUB, TILE),
                    lambda slot, x, block, at: (2 * x + at[0], column(slot, at), block, 0),
                ),
                pl.BlockSpec((2 * TILE, TILE), lambda slot, x, block, at: (0, 0)),
            ]
            + [square] * 8
            + [
                pl.BlockSpec(
                    (1, 2 * TILE, TILE),
                    lambda slot, x, block, at: (jnp.where(slot == 2, 1, 0), 0, 0),
                )
            ]
            + [tri] * len(parts),
            out_specs=[
                pl.BlockSpec(
                    (1, TILE, SUB, TILE), lambda slot, x, block, at: (slot, 0, x * BLOCKS + block, 0)
                ),
                pl.BlockSpec(
                    (1, TILE, SUB * TILE),
                    lambda slot, x, block, at: (
                        jnp.where(slot == 2, x * BLOCKS + block, 2 * BLOCKS), 0, 0,
                    ),
                ),
            ],
            scratch_shapes=[pltpu.VMEM((TILE * SUB, TILE), jnp.float32)],
        ),
        out_shape=(
            jax.ShapeDtypeStruct((3, TILE, 2 * TILE, TILE), jnp.bfloat16),
            jax.ShapeDtypeStruct((2 * BLOCKS + 1, TILE, SUB * TILE), jnp.bfloat16),
        ),
        compiler_params=pltpu.CompilerParams(
            dimension_semantics=("arbitrary",) * 3, vmem_limit_bytes=VMEM_LIMIT
        ),
        cost_estimate=pl.CostEstimate(
            flops=pairs * TILE * 1024, bytes_accessed=pairs * 1024, transcendentals=pairs * TILE * 2
        ),
        name="middle",
    )(at, states, mask, both, gain0, bias0, gain_out, bias_out, proj, gate, gain1, bias1, weights, *parts)


CHANNELS = 8


def incoming_kernel(at, pairs, keep, send):
    core = at[0]
    for d in range(CHANNELS):
        right = pairs[2, d]
        keep[d] = lax.dot_general(pairs[core, d], right, TN, preferred_element_type=jnp.float32)
        send[d] = lax.dot_general(
            pairs[1 - core, d], right, TN, preferred_element_type=jnp.float32
        ).astype(jnp.bfloat16)


def incoming(at, pairs):
    out_spec = pl.BlockSpec((CHANNELS, TILE, TILE), lambda d, at: (d, 0, 0))
    return pl.pallas_call(
        incoming_kernel,
        grid_spec=pltpu.PrefetchScalarGridSpec(
            num_scalar_prefetch=1,
            grid=(TILE // CHANNELS,),
            in_specs=[pl.BlockSpec((3, CHANNELS, 2 * TILE, TILE), lambda d, at: (0, d, 0, 0))],
            out_specs=[out_spec, out_spec],
        ),
        out_shape=(
            jax.ShapeDtypeStruct((TILE, TILE, TILE), jnp.float32),
            jax.ShapeDtypeStruct((TILE, TILE, TILE), jnp.bfloat16),
        ),
        compiler_params=pltpu.CompilerParams(
            dimension_semantics=("arbitrary",), vmem_limit_bytes=VMEM_LIMIT
        ),
        cost_estimate=pl.CostEstimate(
            flops=TILE * 512 * 256 * TILE, bytes_accessed=36 * 2**20, transcendentals=0
        ),
        name="incoming",
    )(at, pairs)


def leave_kernel(at, kept, got, state, gain1, bias1, gain_out, bias_out, proj, gate, result, turn):
    rows = state[0].astype(jnp.float32)
    normed = norm_channels(rows, gain1[...], bias1[...])
    summed = (kept[...] + got[...].astype(jnp.float32)).astype(jnp.bfloat16)
    turn[...] = summed.astype(jnp.float32).reshape(TILE * SUB, TILE)
    normed_out = norm_channels(flat_channels(turn), gain_out[...], bias_out[...])
    out = jnp.dot(proj[...], normed_out, preferred_element_type=jnp.float32)
    gate_value = jnp.tanh(jnp.dot(gate[...], normed, preferred_element_type=jnp.float32))
    changed = (rows + (out * gate_value + out)).astype(jnp.bfloat16)
    result[...] = changed.T.reshape(SUB, TILE, TILE)


def leave(at, kept, got, states, *fixed):
    square = pl.BlockSpec((TILE, TILE), lambda block, at: (0, 0))
    tri = pl.BlockSpec((TILE, SUB, TILE), lambda block, at: (0, block, 0))
    return pl.pallas_call(
        leave_kernel,
        grid_spec=pltpu.PrefetchScalarGridSpec(
            num_scalar_prefetch=1,
            grid=(BLOCKS,),
            in_specs=[
                tri,
                tri,
                pl.BlockSpec((1, TILE, SUB * TILE), lambda block, at: (at[1] * BLOCKS + block, 0, 0)),
            ]
            + [square] * 6,
            out_specs=pl.BlockSpec((SUB, TILE, TILE), lambda block, at: (block, 0, 0)),
            scratch_shapes=[pltpu.VMEM((TILE * SUB, TILE), jnp.float32)],
        ),
        out_shape=jax.ShapeDtypeStruct((TILE, TILE, TILE), jnp.bfloat16),
        compiler_params=pltpu.CompilerParams(
            dimension_semantics=("arbitrary",), vmem_limit_bytes=VMEM_LIMIT
        ),
        cost_estimate=pl.CostEstimate(
            flops=TILE**3 * 512, bytes_accessed=20 * 2**20, transcendentals=TILE**3
        ),
        name="leave",
    )(at, kept, got, states, *fixed)


def on_device_ring(
    pair_state,
    pair_mask,
    norm_in_gain,
    norm_in_bias,
    proj_in,
    gate_in,
    norm_out_gain,
    norm_out_bias,
    proj_out,
    gate_out,
):
    row = lax.axis_index("row")
    z = lax.axis_index("col")
    x, core = row // 2, row % 2
    place = jnp.where(x == 0, z, 7 - z)

    def device(position, which):
        on_x, on_z = (0, position) if position < 4 else (1, 7 - position)
        return (2 * on_x + which) * 4 + on_z

    up = [(device(p, w), device((p + 1) % 8, w)) for p in range(8) for w in range(2)]
    down = [(target, source) for source, target in up]
    swap = [(device(p, w), device(p, 1 - w)) for p in range(8) for w in range(2)]

    own_mask = pair_mask.astype(jnp.bfloat16)
    sib_mask = lax.ppermute(own_mask, BOTH, swap)
    masks = jnp.where(core == 0, jnp.stack([own_mask, sib_mask]), jnp.stack([sib_mask, own_mask]))

    half = TILE // 2
    ours = core * half
    theirs = half - ours

    def halved(matrix, start, width):
        return (0.5 * lax.dynamic_slice_in_dim(matrix, start, width, axis=1)).T

    enter_weights = jnp.concatenate(
        [halved(m[0], side + ours, half) for m in (proj_in, gate_in) for side in (0, TILE)], axis=0
    )
    middle_weights = jnp.stack(
        [
            jnp.concatenate([halved(m[1], side, TILE) for m in (proj_in, gate_in)], axis=0)
            for side in (0, TILE)
        ]
    )
    identity = jnp.eye(TILE, dtype=jnp.bfloat16)
    centre = identity - jnp.bfloat16(1.0 / TILE)
    def reordered(values):
        return jnp.concatenate(
            [lax.dynamic_slice_in_dim(values, start, half, axis=0) for start in (ours, theirs)], axis=0
        )

    def columns(values):
        return jnp.broadcast_to(values[:, None], (TILE, TILE))

    gain_in = [columns(norm_in_gain[u]) for u in range(2)]
    bias_in = [columns(norm_in_bias[u]) for u in range(2)]

    def project(held, offset, own, sib, mask, first_block):
        there = lax.rem(place + offset, 8)
        there_x = there // 4
        there_z = jnp.where(there_x == 0, there, 7 - there)
        last = lax.rem(z, 2)
        at = jnp.stack(
            [there_x, there_z, last, (there_x == x).astype(jnp.int32), (last == core).astype(jnp.int32)]
        ).astype(jnp.int32)
        return enter(own, sib, first_block, at, mask, centre, gain_in[0], bias_in[0], enter_weights, held)

    def hop(values, pairs):
        return [lax.ppermute(value, BOTH, pairs) for value in values]

    held = project(None, 0, pair_state, lax.ppermute(pair_state, BOTH, swap), masks, 0)
    below = hop([masks, pair_state], up)
    above = hop([masks, pair_state], down)
    part = TILE // 2
    middle_fixed = [
        jnp.concatenate([centre, identity], axis=0),
        gain_in[0],
        bias_in[0],
        columns(reordered(norm_out_gain[0])),
        columns(reordered(norm_out_bias[0])),
        0.5 * reordered(proj_out[0]).T,
        0.5 * gate_out[0].T,
        gain_in[1],
        bias_in[1],
        middle_weights,
    ]
    leave_fixed = [
        gain_in[1],
        bias_in[1],
        columns(norm_out_gain[1]),
        columns(norm_out_bias[1]),
        0.5 * proj_out[1].T,
        0.5 * gate_out[1].T,
    ]
    for step in range(1, 4):
        below, above, held, middle_fixed, leave_fixed = lax.optimization_barrier(
            (below, above, held, middle_fixed, leave_fixed)
        )
        now_below, now_above = below, above
        if step < 3:
            below = hop(now_below, up)
            above = hop(now_above, down)
        else:
            below = hop([now_below[0], now_below[1][:part]], up)
            above = hop([now_above[1][part:]], down)
        for offset, (mask, tile) in ((8 - step, now_below), (step, now_above)):
            held = project(held, offset, tile, lax.ppermute(tile, BOTH, swap), mask, 0)
    below, above, held = lax.optimization_barrier((below, above, held))
    held = project(held, 4, below[1], lax.ppermute(below[1], BOTH, swap), below[0], 0)
    held = project(held, 4, above[0], lax.ppermute(above[0], BOTH, swap), below[0], part // SUB)
    states, left, right, mask = held

    third = jnp.where(z // 2 == x, lax.rem(z, 2), 2)
    at_tri = jnp.stack([core, third]).astype(jnp.int32)
    kept, got = [], []
    for n in range(PARTS):
        if n >= 2:
            at_tri, got[n - 2] = lax.optimization_barrier((at_tri, got[n - 2]))
        stays, leaves = outgoing(at_tri, left, right, n)
        kept.append(stays)
        got.append(lax.ppermute(leaves, BOTH, swap))
    parts = kept + got
    at = jnp.stack([core, x, z]).astype(jnp.int32)
    pairs, states1 = middle(at, states, mask, *middle_fixed, parts)
    kept1, sent1 = incoming(at, pairs)
    got1 = lax.ppermute(sent1, BOTH, swap)
    return leave(at, kept1, got1, states1, *leave_fixed)


def on_device_exchange(
    pair_state,
    pair_mask,
    norm_in_gain,
    norm_in_bias,
    proj_in,
    gate_in,
    norm_out_gain,
    norm_out_bias,
    proj_out,
    gate_out,
):
    mask_weight = pair_mask.astype(jnp.float32)[None]
    current = pair_state
    for update in range(2):
        normed = norm_last(
            current.astype(jnp.float32), norm_in_gain[update], norm_in_bias[update]
        ).astype(jnp.bfloat16)
        projected = jnp.einsum(
            "rcd,de->erc", normed, alternate(proj_in[update]), preferred_element_type=jnp.float32
        )
        gate_logit = jnp.einsum(
            "rcd,de->erc", normed, alternate(gate_in[update]), preferred_element_type=jnp.float32
        )
        paired = (projected * jax.nn.sigmoid(gate_logit) * mask_weight).astype(jnp.bfloat16)
        arrived = spread(paired)
        doubled, total_rows, total_cols = arrived.shape
        pair_count = doubled // 2
        arrived = arrived.reshape(pair_count, 2, total_rows, total_cols)
        left_side = arrived[:, 0]
        right_side = arrived[:, 1]
        pattern = "dik,djk->dij" if update == 0 else "dki,dkj->dij"
        triangle_out = jnp.einsum(
            pattern, left_side, right_side, preferred_element_type=jnp.float32
        ).astype(jnp.bfloat16)
        returned = gather_back(triangle_out)
        normed_out = norm_first(
            returned.astype(jnp.float32), norm_out_gain[update], norm_out_bias[update]
        ).astype(jnp.bfloat16)
        gate_value = jax.nn.sigmoid(
            jnp.einsum("rcd,df->rcf", normed, gate_out[update], preferred_element_type=jnp.float32)
        )
        change = (
            jnp.einsum(
                "erc,ef->rcf", normed_out, proj_out[update], preferred_element_type=jnp.float32
            )
            * gate_value
        )
        current = (current.astype(jnp.float32) + change).astype(jnp.bfloat16)
    return current


def on_device(pair_state, *others):
    square = pair_state.shape == (TILE, TILE, TILE)
    if square and lax.axis_size("row") == 4 and lax.axis_size("col") == 4:
        return on_device_ring(pair_state, *others)
    return on_device_exchange(pair_state, *others)


def solution(mesh):
    return jax.shard_map(
        on_device,
        mesh=mesh,
        in_specs=(
            P(("ens", "row"), "col", None),
            P(("ens", "row"), "col"),
            P(),
            P(),
            P(),
            P(),
            P(),
            P(),
            P(),
            P(),
        ),
        out_specs=P(("ens", "row"), "col", None),
        check_vma=False,
    )
```

```python
import jax
import jax.numpy as jnp
from jax import lax
from jax.experimental import pallas as pl
from jax.experimental.pallas import tpu as pltpu
from jax.sharding import PartitionSpec as P

epsilon = 1e-05


def norm_last(values, norm_gain, norm_bias):
    centre = jnp.mean(values, axis=-1, keepdims=True)
    variance = jnp.mean(jnp.square(values - centre), axis=-1, keepdims=True)
    return (values - centre) * lax.rsqrt(variance + epsilon) * norm_gain + norm_bias


def norm_first(values, norm_gain, norm_bias):
    centre = jnp.mean(values, axis=0, keepdims=True)
    variance = jnp.mean(jnp.square(values - centre), axis=0, keepdims=True)
    return (values - centre) * lax.rsqrt(variance + epsilon) * norm_gain[:, None, None] + norm_bias[
        :, None, None
    ]


def alternate(matrix):
    in_width, out_width = matrix.shape
    half_width = out_width // 2
    return matrix.reshape(in_width, 2, half_width).transpose(0, 2, 1).reshape(in_width, out_width)


def spread(paired):
    arrived = lax.all_to_all(paired, ("row", "col"), split_axis=0, concat_axis=1, tiled=True)
    n_row = lax.axis_size("row")
    n_col = lax.axis_size("col")
    channels, stacked, tile_cols = arrived.shape
    tile_rows = stacked // (n_row * n_col)
    arrived = arrived.reshape(channels, n_row, n_col, tile_rows, tile_cols).transpose(0, 1, 3, 2, 4)
    return arrived.reshape(channels, n_row * tile_rows, n_col * tile_cols)


def gather_back(triangle_out):
    n_row = lax.axis_size("row")
    n_col = lax.axis_size("col")
    channels, total_rows, total_cols = triangle_out.shape
    tile_rows = total_rows // n_row
    tile_cols = total_cols // n_col
    pieces = triangle_out.reshape(channels, n_row, tile_rows, n_col, tile_cols).transpose(
        1, 3, 0, 2, 4
    )
    pieces = pieces.reshape(n_row * n_col * channels, tile_rows, tile_cols)
    return lax.all_to_all(pieces, ("row", "col"), split_axis=0, concat_axis=0, tiled=True)


TILE = 128
SUB = 16
BLOCKS = TILE // SUB
CHUNK = 2
STATE_BLOCKS = 6 * BLOCKS
VMEM_LIMIT = 40 * 1024 * 1024
BOTH = ("row", "col")
NT = (((1,), (1,)), ((), ()))
TN = (((0,), (0,)), ((), ()))


def channels_first(rows, matrix):
    return lax.dot_general(matrix, rows, NT, preferred_element_type=jnp.float32)


def norm_apart(apart, gain, bias):
    variance = jnp.mean(apart * apart, axis=0, keepdims=True)
    wide_gain = jnp.concatenate([gain[...]] * CHUNK, axis=1)
    wide_bias = jnp.concatenate([bias[...]] * CHUNK, axis=1)
    return (apart * lax.rsqrt(variance + epsilon) * wide_gain + wide_bias).astype(jnp.bfloat16)


def norm_channels(values, gain, bias):
    return norm_apart(values - jnp.mean(values, axis=0, keepdims=True), gain, bias)


def product(matrix, values):
    return jnp.dot(matrix, values, preferred_element_type=jnp.float32)


def gated_store(weights, normed, mask_rows, first, turn):
    both = product(weights, normed)
    half = both.shape[0] // 2
    paired = both[:half] * jnp.tanh(both[half:]) + both[:half]
    for r in range(CHUNK):
        turn[pl.ds(first + r, half, stride=SUB), :] = (
            paired[:, r * TILE : (r + 1) * TILE] * mask_rows[first + r : first + r + 1, :]
        )


def chunk_of(turn, first):
    return jnp.concatenate([turn[pl.ds(first + r, TILE, stride=SUB), :] for r in range(CHUNK)], axis=1)


def enter_kernel(at, own, sib, mask, both, gain, bias, weights, *rest):
    state_out, left_low, left_high, right_out, mask_out, turn = rest[-6:]
    step = pl.program_id(0)
    use_own = (step == 1) == (at[4] == 1)
    mask_rows = mask[0].astype(jnp.float32)
    mask_out[0, 0] = mask[0]

    @pl.when(use_own)
    def _():
        for first in range(0, SUB, CHUNK):
            turned = channels_first(own[first : first + CHUNK].reshape(CHUNK * TILE, TILE), both[...])
            normed = norm_apart(turned[:TILE], gain, bias)
            lanes = slice(first * TILE, (first + CHUNK) * TILE)
            state_out[0, :, lanes] = turned[TILE:].astype(jnp.bfloat16)
            gated_store(weights[...], normed, mask_rows, first, turn)

    @pl.when(jnp.logical_not(use_own))
    def _():
        for first in range(0, SUB, CHUNK):
            apart = channels_first(sib[first : first + CHUNK].reshape(CHUNK * TILE, TILE), both[:TILE])
            gated_store(weights[...], norm_apart(apart, gain, bias), mask_rows, first, turn)

    start = 0
    for out in (left_low, left_high, right_out):
        stop = start + out.shape[1] * SUB
        out[0] = turn[start:stop, :].astype(jnp.bfloat16).reshape(out.shape[1], SUB, TILE)
        start = stop


def enter(own, sib, first_block, at, mask, both, gain, bias, weights, held):
    n_block = own.shape[0] // SUB
    full = pl.BlockSpec(memory_space=pl.ANY)

    def core_of(step, at):
        return jnp.where(step == 1, at[2], 1 - at[2])

    def is_own(step, at):
        return (step == 1) == (at[4] == 1)

    def own_map(step, block, at):
        return (jnp.where(is_own(step, at), block, jnp.where(step == 0, 0, n_block - 1)), 0, 0)

    def sib_map(step, block, at):
        return (jnp.where(is_own(step, at), jnp.where(step == 0, 0, n_block - 1), block), 0, 0)

    def mask_map(step, block, at):
        return (core_of(step, at), first_block + block, 0)

    def mask_out_map(step, block, at):
        return (2 * at[0] + core_of(step, at), at[1], first_block + block, 0)

    def state_map(step, block, at):
        kept = jnp.where(is_own(step, at), block, jnp.where(step == 0, 0, n_block - 1))
        return (jnp.where(at[5] < 0, STATE_BLOCKS, at[5] + first_block + kept), 0, 0)

    def left_map(step, block, at):
        return (at[1], 0, (2 * at[0] + core_of(step, at)) * BLOCKS + first_block + block, 0)

    def right_map(step, block, at):
        slot = jnp.where(at[3] == 1, core_of(step, at), 2)
        return (at[1], 0, slot * BLOCKS + first_block + block, 0)

    half = weights.shape[0] // 4
    same = lambda step, block, at: (0, 0)
    shapes = (
        jax.ShapeDtypeStruct((STATE_BLOCKS + 1, TILE, SUB * TILE), jnp.bfloat16),
        jax.ShapeDtypeStruct((4, half // 2, 4 * TILE, TILE), jnp.bfloat16),
        jax.ShapeDtypeStruct((4, half // 2, 4 * TILE, TILE), jnp.bfloat16),
        jax.ShapeDtypeStruct((4, half, 3 * TILE, TILE), jnp.bfloat16),
        jax.ShapeDtypeStruct((4, 4, TILE, TILE), jnp.bfloat16),
    )
    in_specs = [
        pl.BlockSpec((SUB, TILE, TILE), own_map),
        pl.BlockSpec((SUB, TILE, TILE), sib_map),
        pl.BlockSpec((1, SUB, TILE), mask_map),
        pl.BlockSpec((2 * TILE, TILE), same),
        pl.BlockSpec((TILE, TILE), same),
        pl.BlockSpec((TILE, TILE), same),
        pl.BlockSpec((4 * half, TILE), same),
    ]
    operands = [own, sib, mask, both, gain, bias, weights]
    aliases = {}
    if held is not None:
        aliases = {len(operands) + 1 + n: n for n in range(5)}
        operands += list(held)
        in_specs += [full] * 5
    pairs = 2 * own.shape[0] * TILE
    return pl.pallas_call(
        enter_kernel,
        grid_spec=pltpu.PrefetchScalarGridSpec(
            num_scalar_prefetch=1,
            grid=(2, n_block),
            in_specs=in_specs,
            out_specs=[
                pl.BlockSpec((1, TILE, SUB * TILE), state_map),
                pl.BlockSpec((1, half // 2, SUB, TILE), left_map),
                pl.BlockSpec((1, half // 2, SUB, TILE), left_map),
                pl.BlockSpec((1, half, SUB, TILE), right_map),
                pl.BlockSpec((1, 1, SUB, TILE), mask_out_map),
            ],
            scratch_shapes=[pltpu.VMEM((2 * half * SUB, TILE), jnp.float32)],
        ),
        out_shape=shapes,
        input_output_aliases=aliases,
        compiler_params=pltpu.CompilerParams(
            dimension_semantics=("arbitrary", "arbitrary"), vmem_limit_bytes=VMEM_LIMIT
        ),
        cost_estimate=pl.CostEstimate(
            flops=pairs * TILE * 1024, bytes_accessed=pairs * 1024, transcendentals=pairs * TILE
        ),
        name="enter",
    )(at, *operands)


def outgoing_kernel(at, left, right, keep, send):
    core = at[0]
    third = pl.multiple_of(at[1] * TILE, TILE)

    def wide(ref, d, start, count):
        return jnp.concatenate([ref[k, d, pl.ds(start, count), :] for k in range(4)], axis=1)

    blocks = [2 * x + which for which in (core, 1 - core) for x in range(2)]
    for d in range(TOGETHER):
        columns = jnp.concatenate(
            [wide(right, d, 0, 2 * TILE), wide(right, d, third, TILE)], axis=0
        )
        rows = jnp.concatenate(
            [wide(left, d, pl.multiple_of(block * TILE, TILE), TILE) for block in blocks], axis=0
        )
        sums = lax.dot_general(rows, columns, NT, preferred_element_type=jnp.float32)
        for slot in range(3):
            lanes = slice(slot * TILE, (slot + 1) * TILE)
            keep[slot, d] = sums[: 2 * TILE, lanes].astype(jnp.bfloat16)
            send[slot, d] = sums[2 * TILE :, lanes].astype(jnp.bfloat16)


TOGETHER = 2
PARTS = 4


def outgoing(at, lefts, right, part):
    count = right.shape[1] // PARTS
    steps = count // TOGETHER
    first = part * steps
    left = lefts[part * len(lefts) // PARTS]
    left_first = part % (PARTS // len(lefts)) * steps
    out = jax.ShapeDtypeStruct((3, count, 2 * TILE, TILE), jnp.bfloat16)
    return pl.pallas_call(
        outgoing_kernel,
        grid_spec=pltpu.PrefetchScalarGridSpec(
            num_scalar_prefetch=1,
            grid=(steps,),
            in_specs=[
                pl.BlockSpec((4, TOGETHER, 4 * TILE, TILE), lambda d, at: (0, left_first + d, 0, 0)),
                pl.BlockSpec((4, TOGETHER, 3 * TILE, TILE), lambda d, at: (0, first + d, 0, 0)),
            ],
            out_specs=[pl.BlockSpec((3, TOGETHER, 2 * TILE, TILE), lambda d, at: (0, d, 0, 0))] * 2,
        ),
        out_shape=(out, out),
        compiler_params=pltpu.CompilerParams(
            dimension_semantics=("arbitrary",), vmem_limit_bytes=VMEM_LIMIT
        ),
        cost_estimate=pl.CostEstimate(
            flops=count * 512 * 384 * 1024, bytes_accessed=count * 1300 * 1024, transcendentals=0
        ),
        name="outgoing",
    )(at, left, right)


def middle_kernel(
    at, state, mask, gain0, bias0, gain_out, bias_out, proj, gate, gain1, bias1, weights, *rest
):
    parts, (pairs_out, state_out, turn, turn_out) = rest[:-4], rest[-4:]
    height = TILE * SUB // len(parts)
    for n, part in enumerate(parts):
        turn[n * height : (n + 1) * height, :] = part[0].reshape(height, TILE).astype(jnp.float32)
    mask_rows = mask[0, 0].astype(jnp.float32)
    for first in range(0, SUB, CHUNK):
        lanes = slice(first * TILE, (first + CHUNK) * TILE)
        normed_out = norm_channels(chunk_of(turn, first), gain_out, bias_out)
        out = product(proj[...], normed_out)
        before = state[0, :, lanes].astype(jnp.float32)
        gate_value = jnp.tanh(product(gate[...], norm_channels(before, gain0, bias0)))
        changed = (before + (out * gate_value + out)).astype(jnp.bfloat16)
        state_out[0, :, lanes] = changed
        normed1 = norm_channels(changed.astype(jnp.float32), gain1, bias1)
        gated_store(weights[0], normed1, mask_rows, first, turn_out)
    pairs_out[0] = turn_out[...].astype(jnp.bfloat16).reshape(TILE, SUB, TILE)


def middle(at, states, mask, fixed, parts):
    def column(slot, at):
        return jnp.where(slot == 2, at[2], 2 * at[1] + slot)

    square = pl.BlockSpec((TILE, TILE), lambda slot, x, block, at: (0, 0))
    tri = pl.BlockSpec(
        (1, parts[0].shape[1], SUB, TILE), lambda slot, x, block, at: (slot, 0, x * BLOCKS + block, 0)
    )
    state_spec = pl.BlockSpec(
        (1, TILE, SUB * TILE),
        lambda slot, x, block, at: ((x * 3 + jnp.where(slot == 2, at[3], slot)) * BLOCKS + block, 0, 0),
    )
    pairs = 6 * TILE * TILE
    return pl.pallas_call(
        middle_kernel,
        grid_spec=pltpu.PrefetchScalarGridSpec(
            num_scalar_prefetch=1,
            grid=(3, 2, BLOCKS),
            in_specs=[
                state_spec,
                pl.BlockSpec(
                    (1, 1, SUB, TILE),
                    lambda slot, x, block, at: (2 * x + at[0], column(slot, at), block, 0),
                ),
            ]
            + [square] * 8
            + [
                pl.BlockSpec(
                    (1, 2 * TILE, TILE),
                    lambda slot, x, block, at: (jnp.where(slot == 2, 1, 0), 0, 0),
                )
            ]
            + [tri] * len(parts),
            out_specs=[
                pl.BlockSpec(
                    (1, TILE, SUB, TILE), lambda slot, x, block, at: (slot, 0, x * BLOCKS + block, 0)
                ),
                pl.BlockSpec(
                    (1, TILE, SUB * TILE),
                    lambda slot, x, block, at: (
                        jnp.where(slot == 2, x * BLOCKS + block, 2 * BLOCKS), 0, 0,
                    ),
                ),
            ],
            scratch_shapes=[pltpu.VMEM((TILE * SUB, TILE), jnp.float32)] * 2,
        ),
        out_shape=(
            jax.ShapeDtypeStruct((3, TILE, 2 * TILE, TILE), jnp.bfloat16),
            jax.ShapeDtypeStruct((2 * BLOCKS + 1, TILE, SUB * TILE), jnp.bfloat16),
        ),
        compiler_params=pltpu.CompilerParams(
            dimension_semantics=("arbitrary",) * 3, vmem_limit_bytes=VMEM_LIMIT
        ),
        cost_estimate=pl.CostEstimate(
            flops=pairs * TILE * 1024, bytes_accessed=pairs * 1024, transcendentals=pairs * TILE * 2
        ),
        name="middle",
    )(at, states, mask, *fixed, *parts)


CHANNELS = 8


def incoming_kernel(at, pairs, keep, send):
    core = at[0]
    for d in range(CHANNELS):
        right = pairs[2, d]
        keep[d] = lax.dot_general(pairs[core, d], right, TN, preferred_element_type=jnp.float32)
        send[d] = lax.dot_general(
            pairs[1 - core, d], right, TN, preferred_element_type=jnp.float32
        ).astype(jnp.bfloat16)


def incoming(at, pairs):
    out_spec = pl.BlockSpec((CHANNELS, TILE, TILE), lambda d, at: (d, 0, 0))
    return pl.pallas_call(
        incoming_kernel,
        grid_spec=pltpu.PrefetchScalarGridSpec(
            num_scalar_prefetch=1,
            grid=(TILE // CHANNELS,),
            in_specs=[pl.BlockSpec((3, CHANNELS, 2 * TILE, TILE), lambda d, at: (0, d, 0, 0))],
            out_specs=[out_spec, out_spec],
        ),
        out_shape=(
            jax.ShapeDtypeStruct((TILE, TILE, TILE), jnp.float32),
            jax.ShapeDtypeStruct((TILE, TILE, TILE), jnp.bfloat16),
        ),
        compiler_params=pltpu.CompilerParams(
            dimension_semantics=("arbitrary",), vmem_limit_bytes=VMEM_LIMIT
        ),
        cost_estimate=pl.CostEstimate(
            flops=TILE * 512 * 256 * TILE, bytes_accessed=36 * 2**20, transcendentals=0
        ),
        name="incoming",
    )(at, pairs)


def leave_kernel(at, kept, got, state, gain1, bias1, gain_out, bias_out, proj, gate, result, turn):
    summed = (kept[...] + got[...].astype(jnp.float32)).astype(jnp.bfloat16)
    turn[...] = summed.astype(jnp.float32).reshape(TILE * SUB, TILE)
    for first in range(0, SUB, CHUNK):
        before = state[0, :, first * TILE : (first + CHUNK) * TILE].astype(jnp.float32)
        normed = norm_channels(before, gain1, bias1)
        out = product(proj[...], norm_channels(chunk_of(turn, first), gain_out, bias_out))
        gate_value = jnp.tanh(product(gate[...], normed))
        changed = (before + (out * gate_value + out)).astype(jnp.bfloat16)
        result[first : first + CHUNK] = changed.T.reshape(CHUNK, TILE, TILE)


def leave(at, kept, got, states, *fixed):
    square = pl.BlockSpec((TILE, TILE), lambda block, at: (0, 0))
    tri = pl.BlockSpec((TILE, SUB, TILE), lambda block, at: (0, block, 0))
    return pl.pallas_call(
        leave_kernel,
        grid_spec=pltpu.PrefetchScalarGridSpec(
            num_scalar_prefetch=1,
            grid=(BLOCKS,),
            in_specs=[
                tri,
                tri,
                pl.BlockSpec((1, TILE, SUB * TILE), lambda block, at: (at[1] * BLOCKS + block, 0, 0)),
            ]
            + [square] * 6,
            out_specs=pl.BlockSpec((SUB, TILE, TILE), lambda block, at: (block, 0, 0)),
            scratch_shapes=[pltpu.VMEM((TILE * SUB, TILE), jnp.float32)],
        ),
        out_shape=jax.ShapeDtypeStruct((TILE, TILE, TILE), jnp.bfloat16),
        compiler_params=pltpu.CompilerParams(
            dimension_semantics=("arbitrary",), vmem_limit_bytes=VMEM_LIMIT
        ),
        cost_estimate=pl.CostEstimate(
            flops=TILE**3 * 512, bytes_accessed=20 * 2**20, transcendentals=TILE**3
        ),
        name="leave",
    )(at, kept, got, states, *fixed)


def on_device_ring(
    pair_state,
    pair_mask,
    norm_in_gain,
    norm_in_bias,
    proj_in,
    gate_in,
    norm_out_gain,
    norm_out_bias,
    proj_out,
    gate_out,
):
    row = lax.axis_index("row")
    z = lax.axis_index("col")
    x, core = row // 2, row % 2
    place = jnp.where(x == 0, z, 7 - z)

    def device(position, which):
        on_x, on_z = (0, position) if position < 4 else (1, 7 - position)
        return (2 * on_x + which) * 4 + on_z

    up = [(device(p, w), device((p + 1) % 8, w)) for p in range(8) for w in range(2)]
    down = [(target, source) for source, target in up]
    swap = [(device(p, w), device(p, 1 - w)) for p in range(8) for w in range(2)]

    own_mask = pair_mask.astype(jnp.bfloat16)
    sib_mask = lax.ppermute(own_mask, BOTH, swap)
    masks = jnp.where(core == 0, jnp.stack([own_mask, sib_mask]), jnp.stack([sib_mask, own_mask]))

    half = TILE // 2
    ours = core * half
    theirs = half - ours

    def halved(matrix, start, width):
        return (0.5 * lax.dynamic_slice_in_dim(matrix, start, width, axis=1)).T

    enter_weights = jnp.concatenate(
        [halved(m[0], side + ours, half) for m in (proj_in, gate_in) for side in (0, TILE)], axis=0
    )
    middle_weights = jnp.stack(
        [
            jnp.concatenate([halved(m[1], side, TILE) for m in (proj_in, gate_in)], axis=0)
            for side in (0, TILE)
        ]
    )
    identity = jnp.eye(TILE, dtype=jnp.bfloat16)
    both = jnp.concatenate([identity - jnp.bfloat16(1.0 / TILE), identity], axis=0)
    def reordered(values):
        return jnp.concatenate(
            [lax.dynamic_slice_in_dim(values, start, half, axis=0) for start in (ours, theirs)], axis=0
        )

    def columns(values):
        return jnp.broadcast_to(values[:, None], (TILE, TILE))

    gain_in = [columns(norm_in_gain[u]) for u in range(2)]
    bias_in = [columns(norm_in_bias[u]) for u in range(2)]

    def project(held, offset, own, sib, mask, first_block):
        there = lax.rem(place + offset, 8)
        there_x = there // 4
        there_z = jnp.where(there_x == 0, there, 7 - there)
        last = lax.rem(z, 2)
        slot = jnp.where(there_z // 2 == x, lax.rem(there_z, 2), jnp.where(there_z == z, 2, -1))
        at = jnp.stack(
            [
                there_x,
                there_z,
                last,
                (there_x == x).astype(jnp.int32),
                (last == core).astype(jnp.int32),
                jnp.where(slot < 0, -1, (3 * there_x + slot) * BLOCKS),
            ]
        ).astype(jnp.int32)
        fixed = (both, gain_in[0], bias_in[0], enter_weights)
        return enter(own, sib, first_block, at, mask, *fixed, held)

    def hop(values, pairs):
        return [lax.ppermute(value, BOTH, pairs) for value in values]

    held = project(None, 0, pair_state, lax.ppermute(pair_state, BOTH, swap), masks, 0)
    below = hop([masks, pair_state], up)
    above = hop([masks, pair_state], down)
    part = TILE // 2
    middle_fixed = [
        gain_in[0],
        bias_in[0],
        columns(reordered(norm_out_gain[0])),
        columns(reordered(norm_out_bias[0])),
        0.5 * reordered(proj_out[0]).T,
        0.5 * gate_out[0].T,
        gain_in[1],
        bias_in[1],
        middle_weights,
    ]
    leave_fixed = [
        gain_in[1],
        bias_in[1],
        columns(norm_out_gain[1]),
        columns(norm_out_bias[1]),
        0.5 * proj_out[1].T,
        0.5 * gate_out[1].T,
    ]
    for step in range(1, 4):
        below, above, held, middle_fixed, leave_fixed = lax.optimization_barrier(
            (below, above, held, middle_fixed, leave_fixed)
        )
        now_below, now_above = below, above
        if step < 3:
            below = hop(now_below, up)
            above = hop(now_above, down)
        else:
            below = hop([now_below[0], now_below[1][:part]], up)
            above = hop([now_above[1][part:]], down)
        for offset, (mask, tile) in ((8 - step, now_below), (step, now_above)):
            held = project(held, offset, tile, lax.ppermute(tile, BOTH, swap), mask, 0)
    below, above, held = lax.optimization_barrier((below, above, held))
    held = project(held, 4, below[1], lax.ppermute(below[1], BOTH, swap), below[0], 0)
    held = project(held, 4, above[0], lax.ppermute(above[0], BOTH, swap), below[0], part // SUB)
    states, *lefts, right, mask = held

    third = jnp.where(z // 2 == x, lax.rem(z, 2), 2)
    at_tri = jnp.stack([core, third]).astype(jnp.int32)
    kept, got = [], []
    for n in range(PARTS):
        if n >= 2:
            at_tri, got[n - 2] = lax.optimization_barrier((at_tri, got[n - 2]))
        stays, leaves = outgoing(at_tri, lefts, right, n)
        kept.append(stays)
        got.append(lax.ppermute(leaves, BOTH, swap))
    parts = kept + got
    at = jnp.stack([core, x, z, third]).astype(jnp.int32)
    pairs, states1 = middle(at, states, mask, middle_fixed, parts)
    kept1, sent1 = incoming(at, pairs)
    got1 = lax.ppermute(sent1, BOTH, swap)
    return leave(at, kept1, got1, states1, *leave_fixed)


def on_device_exchange(
    pair_state,
    pair_mask,
    norm_in_gain,
    norm_in_bias,
    proj_in,
    gate_in,
    norm_out_gain,
    norm_out_bias,
    proj_out,
    gate_out,
):
    mask_weight = pair_mask.astype(jnp.float32)[None]
    current = pair_state
    for update in range(2):
        normed = norm_last(
            current.astype(jnp.float32), norm_in_gain[update], norm_in_bias[update]
        ).astype(jnp.bfloat16)
        projected = jnp.einsum(
            "rcd,de->erc", normed, alternate(proj_in[update]), preferred_element_type=jnp.float32
        )
        gate_logit = jnp.einsum(
            "rcd,de->erc", normed, alternate(gate_in[update]), preferred_element_type=jnp.float32
        )
        paired = (projected * jax.nn.sigmoid(gate_logit) * mask_weight).astype(jnp.bfloat16)
        arrived = spread(paired)
        doubled, total_rows, total_cols = arrived.shape
        pair_count = doubled // 2
        arrived = arrived.reshape(pair_count, 2, total_rows, total_cols)
        left_side = arrived[:, 0]
        right_side = arrived[:, 1]
        pattern = "dik,djk->dij" if update == 0 else "dki,dkj->dij"
        triangle_out = jnp.einsum(
            pattern, left_side, right_side, preferred_element_type=jnp.float32
        ).astype(jnp.bfloat16)
        returned = gather_back(triangle_out)
        normed_out = norm_first(
            returned.astype(jnp.float32), norm_out_gain[update], norm_out_bias[update]
        ).astype(jnp.bfloat16)
        gate_value = jax.nn.sigmoid(
            jnp.einsum("rcd,df->rcf", normed, gate_out[update], preferred_element_type=jnp.float32)
        )
        change = (
            jnp.einsum(
                "erc,ef->rcf", normed_out, proj_out[update], preferred_element_type=jnp.float32
            )
            * gate_value
        )
        current = (current.astype(jnp.float32) + change).astype(jnp.bfloat16)
    return current


def on_device(pair_state, *others):
    square = pair_state.shape == (TILE, TILE, TILE)
    if square and lax.axis_size("row") == 4 and lax.axis_size("col") == 4:
        return on_device_ring(pair_state, *others)
    return on_device_exchange(pair_state, *others)


def solution(mesh):
    return jax.shard_map(
        on_device,
        mesh=mesh,
        in_specs=(
            P(("ens", "row"), "col", None),
            P(("ens", "row"), "col"),
            P(),
            P(),
            P(),
            P(),
            P(),
            P(),
            P(),
            P(),
        ),
        out_specs=P(("ens", "row"), "col", None),
        check_vma=False,
    )
```

```python
import jax
import jax.numpy as jnp
from jax import lax
from jax.experimental import pallas as pl
from jax.experimental.pallas import tpu as pltpu
from jax.sharding import PartitionSpec as P

epsilon = 1e-05


def norm_last(values, norm_gain, norm_bias):
    centre = jnp.mean(values, axis=-1, keepdims=True)
    variance = jnp.mean(jnp.square(values - centre), axis=-1, keepdims=True)
    return (values - centre) * lax.rsqrt(variance + epsilon) * norm_gain + norm_bias


def norm_first(values, norm_gain, norm_bias):
    centre = jnp.mean(values, axis=0, keepdims=True)
    variance = jnp.mean(jnp.square(values - centre), axis=0, keepdims=True)
    return (values - centre) * lax.rsqrt(variance + epsilon) * norm_gain[:, None, None] + norm_bias[
        :, None, None
    ]


def alternate(matrix):
    in_width, out_width = matrix.shape
    half_width = out_width // 2
    return matrix.reshape(in_width, 2, half_width).transpose(0, 2, 1).reshape(in_width, out_width)


def spread(paired):
    arrived = lax.all_to_all(paired, ("row", "col"), split_axis=0, concat_axis=1, tiled=True)
    n_row = lax.axis_size("row")
    n_col = lax.axis_size("col")
    channels, stacked, tile_cols = arrived.shape
    tile_rows = stacked // (n_row * n_col)
    arrived = arrived.reshape(channels, n_row, n_col, tile_rows, tile_cols).transpose(0, 1, 3, 2, 4)
    return arrived.reshape(channels, n_row * tile_rows, n_col * tile_cols)


def gather_back(triangle_out):
    n_row = lax.axis_size("row")
    n_col = lax.axis_size("col")
    channels, total_rows, total_cols = triangle_out.shape
    tile_rows = total_rows // n_row
    tile_cols = total_cols // n_col
    pieces = triangle_out.reshape(channels, n_row, tile_rows, n_col, tile_cols).transpose(
        1, 3, 0, 2, 4
    )
    pieces = pieces.reshape(n_row * n_col * channels, tile_rows, tile_cols)
    return lax.all_to_all(pieces, ("row", "col"), split_axis=0, concat_axis=0, tiled=True)


TILE = 128
SUB = 16
BLOCKS = TILE // SUB
CHUNK = 2
GROUPS = 2
MIDDLE_GROUPS = 4
VMEM_LIMIT = 40 * 1024 * 1024
BOTH = ("row", "col")
NT = (((1,), (1,)), ((), ()))
TN = (((0,), (0,)), ((), ()))


def channels_first(rows, matrix):
    return lax.dot_general(matrix, rows, NT, preferred_element_type=jnp.float32)


def norm_apart(apart, gain, bias):
    variance = jnp.mean(apart * apart, axis=0, keepdims=True)
    wide_gain = jnp.concatenate([gain[...]] * CHUNK, axis=1)
    wide_bias = jnp.concatenate([bias[...]] * CHUNK, axis=1)
    return (apart * lax.rsqrt(variance + epsilon) * wide_gain + wide_bias).astype(jnp.bfloat16)


def norm_channels(values, gain, bias):
    return norm_apart(values - jnp.mean(values, axis=0, keepdims=True), gain, bias)


def product(matrix, values):
    return jnp.dot(matrix, values, preferred_element_type=jnp.float32)


def gated(weights, normed):
    both = product(weights, normed)
    half = both.shape[0] // 2
    return both[:half] * jnp.tanh(both[half:]) + both[:half]


def turn_masked(chunks, mask_rows, turn):
    count = chunks[0].shape[0]
    for r in range(SUB):
        lanes = slice(r % CHUNK * TILE, (r % CHUNK + 1) * TILE)
        turn[pl.ds(r, count, stride=SUB), :] = chunks[r // CHUNK][:, lanes] * mask_rows[r : r + 1, :]


def chunk_of(turn, first):
    return jnp.concatenate([turn[pl.ds(first + r, TILE, stride=SUB), :] for r in range(CHUNK)], axis=1)


def rows_of(group):
    return pl.ds(pl.multiple_of(group * SUB, SUB), SUB)


def enter_kernel(at, own, sib, mask, both, gain, bias, weights, *rest):
    state_out, left_low, left_high, right_out, mask_out, turn = rest[-6:]
    step = pl.program_id(0)
    use_own = (step == 1) == (at[4] == 1)
    mask_out[0, 0] = mask[0]

    def finish(group, paired):
        turn_masked(paired, mask[0, rows_of(group), :].astype(jnp.float32), turn)
        start = 0
        for out in (left_low, left_high, right_out):
            stop = start + out.shape[1] * SUB
            out[0, :, rows_of(group), :] = (
                turn[start:stop, :].astype(jnp.bfloat16).reshape(out.shape[1], SUB, TILE)
            )
            start = stop

    def turned_chunks(tile, group, matrix):
        rows = tile[rows_of(group)].reshape(SUB * TILE, TILE)
        size = CHUNK * TILE
        return [channels_first(rows[n * size : (n + 1) * size], matrix) for n in range(SUB // CHUNK)]

    @pl.when(use_own)
    def _():
        @pl.loop(0, GROUPS)
        def _(group):
            chunks = turned_chunks(own, group, both[...])
            paired = [gated(weights[...], norm_apart(chunk[:TILE], gain, bias)) for chunk in chunks]
            state_out[group] = jnp.concatenate(
                [chunk[TILE:].astype(jnp.bfloat16) for chunk in chunks], axis=1
            )
            finish(group, paired)

    @pl.when(jnp.logical_not(use_own))
    def _():
        @pl.loop(0, GROUPS)
        def _(group):
            chunks = turned_chunks(sib, group, both[:TILE])
            finish(group, [gated(weights[...], norm_apart(chunk, gain, bias)) for chunk in chunks])


def enter(own, sib, first_block, at, mask, both, gain, bias, weights, held):
    n_block = own.shape[0] // (GROUPS * SUB)
    blocks = TILE // (GROUPS * SUB)
    high = GROUPS * SUB
    full = pl.BlockSpec(memory_space=pl.ANY)

    def core_of(step, at):
        return jnp.where(step == 1, at[2], 1 - at[2])

    def is_own(step, at):
        return (step == 1) == (at[4] == 1)

    def own_map(step, block, at):
        return (jnp.where(is_own(step, at), block, jnp.where(step == 0, 0, n_block - 1)), 0, 0)

    def sib_map(step, block, at):
        return (jnp.where(is_own(step, at), jnp.where(step == 0, 0, n_block - 1), block), 0, 0)

    def mask_map(step, block, at):
        return (core_of(step, at), first_block + block, 0)

    def mask_out_map(step, block, at):
        return (2 * at[0] + core_of(step, at), at[1], first_block + block, 0)

    def state_map(step, block, at):
        kept = jnp.where(is_own(step, at), block, jnp.where(step == 0, 0, n_block - 1))
        return (jnp.where(at[5] < 0, 6 * blocks, at[5] * blocks + first_block + kept), 0, 0)

    def left_map(step, block, at):
        return (at[1], 0, (2 * at[0] + core_of(step, at)) * blocks + first_block + block, 0)

    def right_map(step, block, at):
        slot = jnp.where(at[3] == 1, core_of(step, at), 2)
        return (at[1], 0, slot * blocks + first_block + block, 0)

    half = weights.shape[0] // 4
    same = lambda step, block, at: (0, 0)
    shapes = (
        jax.ShapeDtypeStruct((6 * BLOCKS + GROUPS, TILE, SUB * TILE), jnp.bfloat16),
        jax.ShapeDtypeStruct((4, half // 2, 4 * TILE, TILE), jnp.bfloat16),
        jax.ShapeDtypeStruct((4, half // 2, 4 * TILE, TILE), jnp.bfloat16),
        jax.ShapeDtypeStruct((4, half, 3 * TILE, TILE), jnp.bfloat16),
        jax.ShapeDtypeStruct((4, 4, TILE, TILE), jnp.bfloat16),
    )
    in_specs = [
        pl.BlockSpec((high, TILE, TILE), own_map),
        pl.BlockSpec((high, TILE, TILE), sib_map),
        pl.BlockSpec((1, high, TILE), mask_map),
        pl.BlockSpec((2 * TILE, TILE), same),
        pl.BlockSpec((TILE, TILE), same),
        pl.BlockSpec((TILE, TILE), same),
        pl.BlockSpec((4 * half, TILE), same),
    ]
    operands = [own, sib, mask, both, gain, bias, weights]
    aliases = {}
    if held is not None:
        aliases = {len(operands) + 1 + n: n for n in range(5)}
        operands += list(held)
        in_specs += [full] * 5
    pairs = 2 * own.shape[0] * TILE
    return pl.pallas_call(
        enter_kernel,
        grid_spec=pltpu.PrefetchScalarGridSpec(
            num_scalar_prefetch=1,
            grid=(2, n_block),
            in_specs=in_specs,
            out_specs=[
                pl.BlockSpec((GROUPS, TILE, SUB * TILE), state_map),
                pl.BlockSpec((1, half // 2, high, TILE), left_map),
                pl.BlockSpec((1, half // 2, high, TILE), left_map),
                pl.BlockSpec((1, half, high, TILE), right_map),
                pl.BlockSpec((1, 1, high, TILE), mask_out_map),
            ],
            scratch_shapes=[pltpu.VMEM((2 * half * SUB, TILE), jnp.float32)],
        ),
        out_shape=shapes,
        input_output_aliases=aliases,
        compiler_params=pltpu.CompilerParams(
            dimension_semantics=("arbitrary", "arbitrary"), vmem_limit_bytes=VMEM_LIMIT
        ),
        cost_estimate=pl.CostEstimate(
            flops=pairs * TILE * 1024, bytes_accessed=pairs * 1024, transcendentals=pairs * TILE
        ),
        name="enter",
    )(at, *operands)


def outgoing_kernel(at, left, right, keep, send):
    core = at[0]
    third = pl.multiple_of(at[1] * TILE, TILE)

    def wide(ref, d, start, count):
        return jnp.concatenate([ref[k, d, pl.ds(start, count), :] for k in range(4)], axis=1)

    blocks = [2 * x + which for which in (core, 1 - core) for x in range(2)]
    for d in range(TOGETHER):
        columns = jnp.concatenate(
            [wide(right, d, 0, 2 * TILE), wide(right, d, third, TILE)], axis=0
        )
        rows = jnp.concatenate(
            [wide(left, d, pl.multiple_of(block * TILE, TILE), TILE) for block in blocks], axis=0
        )
        sums = lax.dot_general(rows, columns, NT, preferred_element_type=jnp.float32)
        for slot in range(3):
            lanes = slice(slot * TILE, (slot + 1) * TILE)
            keep[slot, d] = sums[: 2 * TILE, lanes].astype(jnp.bfloat16)
            send[slot, d] = sums[2 * TILE :, lanes].astype(jnp.bfloat16)


TOGETHER = 2
PARTS = 4


def outgoing(at, lefts, right, part):
    count = right.shape[1] // PARTS
    steps = count // TOGETHER
    first = part * steps
    left = lefts[part * len(lefts) // PARTS]
    left_first = part % (PARTS // len(lefts)) * steps
    out = jax.ShapeDtypeStruct((3, count, 2 * TILE, TILE), jnp.bfloat16)
    return pl.pallas_call(
        outgoing_kernel,
        grid_spec=pltpu.PrefetchScalarGridSpec(
            num_scalar_prefetch=1,
            grid=(steps,),
            in_specs=[
                pl.BlockSpec((4, TOGETHER, 4 * TILE, TILE), lambda d, at: (0, left_first + d, 0, 0)),
                pl.BlockSpec((4, TOGETHER, 3 * TILE, TILE), lambda d, at: (0, first + d, 0, 0)),
            ],
            out_specs=[pl.BlockSpec((3, TOGETHER, 2 * TILE, TILE), lambda d, at: (0, d, 0, 0))] * 2,
        ),
        out_shape=(out, out),
        compiler_params=pltpu.CompilerParams(
            dimension_semantics=("arbitrary",), vmem_limit_bytes=VMEM_LIMIT
        ),
        cost_estimate=pl.CostEstimate(
            flops=count * 512 * 384 * 1024, bytes_accessed=count * 1300 * 1024, transcendentals=0
        ),
        name="outgoing",
    )(at, left, right)


def middle_kernel(
    at, state, mask, gain0, bias0, gain_out, bias_out, proj, gate, gain1, bias1, weights, *rest
):
    parts, (pairs_out, state_out, turn, turn_out) = rest[:-4], rest[-4:]
    height = TILE * SUB // len(parts)

    @pl.loop(0, MIDDLE_GROUPS)
    def _(group):
        for n, part in enumerate(parts):
            turn[n * height : (n + 1) * height, :] = (
                part[0, :, rows_of(group), :].reshape(height, TILE).astype(jnp.float32)
            )
        changed, paired = [], []
        for first in range(0, SUB, CHUNK):
            before = state[group, :, first * TILE : (first + CHUNK) * TILE].astype(jnp.float32)
            gate_value = jnp.tanh(product(gate[...], norm_channels(before, gain0, bias0)))
            out = product(proj[...], norm_channels(chunk_of(turn, first), gain_out, bias_out))
            changed.append((before + (out * gate_value + out)).astype(jnp.bfloat16))
            normed1 = norm_channels(changed[-1].astype(jnp.float32), gain1, bias1)
            paired.append(gated(weights[0], normed1))
        state_out[group] = jnp.concatenate(changed, axis=1)
        turn_masked(paired, mask[0, 0, rows_of(group), :].astype(jnp.float32), turn_out)
        pairs_out[0, :, rows_of(group), :] = (
            turn_out[...].astype(jnp.bfloat16).reshape(TILE, SUB, TILE)
        )


def middle(at, states, mask, fixed, parts):
    def column(slot, at):
        return jnp.where(slot == 2, at[2], 2 * at[1] + slot)

    blocks = BLOCKS // MIDDLE_GROUPS
    high = MIDDLE_GROUPS * SUB
    square = pl.BlockSpec((TILE, TILE), lambda slot, x, block, at: (0, 0))
    tri = pl.BlockSpec(
        (1, parts[0].shape[1], high, TILE), lambda slot, x, block, at: (slot, 0, x * blocks + block, 0)
    )
    state_spec = pl.BlockSpec(
        (MIDDLE_GROUPS, TILE, SUB * TILE),
        lambda slot, x, block, at: ((x * 3 + jnp.where(slot == 2, at[3], slot)) * blocks + block, 0, 0),
    )
    pairs = 6 * TILE * TILE
    return pl.pallas_call(
        middle_kernel,
        grid_spec=pltpu.PrefetchScalarGridSpec(
            num_scalar_prefetch=1,
            grid=(3, 2, blocks),
            in_specs=[
                state_spec,
                pl.BlockSpec(
                    (1, 1, high, TILE),
                    lambda slot, x, block, at: (2 * x + at[0], column(slot, at), block, 0),
                ),
            ]
            + [square] * 8
            + [
                pl.BlockSpec(
                    (1, 2 * TILE, TILE),
                    lambda slot, x, block, at: (jnp.where(slot == 2, 1, 0), 0, 0),
                )
            ]
            + [tri] * len(parts),
            out_specs=[
                pl.BlockSpec(
                    (1, TILE, high, TILE), lambda slot, x, block, at: (slot, 0, x * blocks + block, 0)
                ),
                pl.BlockSpec(
                    (MIDDLE_GROUPS, TILE, SUB * TILE),
                    lambda slot, x, block, at: (
                        jnp.where(slot == 2, x * blocks + block, 2 * blocks), 0, 0,
                    ),
                ),
            ],
            scratch_shapes=[pltpu.VMEM((TILE * SUB, TILE), jnp.float32)] * 2,
        ),
        out_shape=(
            jax.ShapeDtypeStruct((3, TILE, 2 * TILE, TILE), jnp.bfloat16),
            jax.ShapeDtypeStruct((2 * BLOCKS + MIDDLE_GROUPS, TILE, SUB * TILE), jnp.bfloat16),
        ),
        compiler_params=pltpu.CompilerParams(
            dimension_semantics=("arbitrary",) * 3, vmem_limit_bytes=VMEM_LIMIT
        ),
        cost_estimate=pl.CostEstimate(
            flops=pairs * TILE * 1024, bytes_accessed=pairs * 1024, transcendentals=pairs * TILE * 2
        ),
        name="middle",
    )(at, states, mask, *fixed, *parts)


CHANNELS = 8


def incoming_kernel(at, pairs, keep, send):
    core = at[0]
    for d in range(CHANNELS):
        right = pairs[2, d]
        keep[d] = lax.dot_general(pairs[core, d], right, TN, preferred_element_type=jnp.float32)
        send[d] = lax.dot_general(
            pairs[1 - core, d], right, TN, preferred_element_type=jnp.float32
        ).astype(jnp.bfloat16)


def incoming(at, pairs):
    out_spec = pl.BlockSpec((CHANNELS, TILE, TILE), lambda d, at: (d, 0, 0))
    return pl.pallas_call(
        incoming_kernel,
        grid_spec=pltpu.PrefetchScalarGridSpec(
            num_scalar_prefetch=1,
            grid=(TILE // CHANNELS,),
            in_specs=[pl.BlockSpec((3, CHANNELS, 2 * TILE, TILE), lambda d, at: (0, d, 0, 0))],
            out_specs=[out_spec, out_spec],
        ),
        out_shape=(
            jax.ShapeDtypeStruct((TILE, TILE, TILE), jnp.float32),
            jax.ShapeDtypeStruct((TILE, TILE, TILE), jnp.bfloat16),
        ),
        compiler_params=pltpu.CompilerParams(
            dimension_semantics=("arbitrary",), vmem_limit_bytes=VMEM_LIMIT
        ),
        cost_estimate=pl.CostEstimate(
            flops=TILE * 512 * 256 * TILE, bytes_accessed=36 * 2**20, transcendentals=0
        ),
        name="incoming",
    )(at, pairs)


def leave_kernel(at, kept, got, state, gain1, bias1, gain_out, bias_out, proj, gate, result, turn):
    @pl.loop(0, GROUPS)
    def _(group):
        summed = kept[:, rows_of(group), :] + got[:, rows_of(group), :].astype(jnp.float32)
        turn[...] = summed.astype(jnp.bfloat16).astype(jnp.float32).reshape(TILE * SUB, TILE)
        changed = []
        for first in range(0, SUB, CHUNK):
            before = state[group, :, first * TILE : (first + CHUNK) * TILE].astype(jnp.float32)
            gate_value = jnp.tanh(product(gate[...], norm_channels(before, gain1, bias1)))
            out = product(proj[...], norm_channels(chunk_of(turn, first), gain_out, bias_out))
            changed.append((before + (out * gate_value + out)).astype(jnp.bfloat16))
        result[rows_of(group)] = jnp.concatenate([chunk.T for chunk in changed], axis=0).reshape(
            SUB, TILE, TILE
        )


def leave(at, kept, got, states, *fixed):
    blocks = BLOCKS // GROUPS
    square = pl.BlockSpec((TILE, TILE), lambda block, at: (0, 0))
    tri = pl.BlockSpec((TILE, GROUPS * SUB, TILE), lambda block, at: (0, block, 0))
    return pl.pallas_call(
        leave_kernel,
        grid_spec=pltpu.PrefetchScalarGridSpec(
            num_scalar_prefetch=1,
            grid=(blocks,),
            in_specs=[
                tri,
                tri,
                pl.BlockSpec((GROUPS, TILE, SUB * TILE), lambda block, at: (at[1] * blocks + block, 0, 0)),
            ]
            + [square] * 6,
            out_specs=pl.BlockSpec((GROUPS * SUB, TILE, TILE), lambda block, at: (block, 0, 0)),
            scratch_shapes=[pltpu.VMEM((TILE * SUB, TILE), jnp.float32)],
        ),
        out_shape=jax.ShapeDtypeStruct((TILE, TILE, TILE), jnp.bfloat16),
        compiler_params=pltpu.CompilerParams(
            dimension_semantics=("arbitrary",), vmem_limit_bytes=VMEM_LIMIT
        ),
        cost_estimate=pl.CostEstimate(
            flops=TILE**3 * 512, bytes_accessed=20 * 2**20, transcendentals=TILE**3
        ),
        name="leave",
    )(at, kept, got, states, *fixed)


def on_device_ring(
    pair_state,
    pair_mask,
    norm_in_gain,
    norm_in_bias,
    proj_in,
    gate_in,
    norm_out_gain,
    norm_out_bias,
    proj_out,
    gate_out,
):
    row = lax.axis_index("row")
    z = lax.axis_index("col")
    x, core = row // 2, row % 2
    place = jnp.where(x == 0, z, 7 - z)

    def device(position, which):
        on_x, on_z = (0, position) if position < 4 else (1, 7 - position)
        return (2 * on_x + which) * 4 + on_z

    up = [(device(p, w), device((p + 1) % 8, w)) for p in range(8) for w in range(2)]
    down = [(target, source) for source, target in up]
    swap = [(device(p, w), device(p, 1 - w)) for p in range(8) for w in range(2)]

    own_mask = pair_mask.astype(jnp.bfloat16)
    sib_mask = lax.ppermute(own_mask, BOTH, swap)
    masks = jnp.where(core == 0, jnp.stack([own_mask, sib_mask]), jnp.stack([sib_mask, own_mask]))

    half = TILE // 2
    ours = core * half
    theirs = half - ours

    def halved(matrix, start, width):
        return (0.5 * lax.dynamic_slice_in_dim(matrix, start, width, axis=1)).T

    enter_weights = jnp.concatenate(
        [halved(m[0], side + ours, half) for m in (proj_in, gate_in) for side in (0, TILE)], axis=0
    )
    middle_weights = jnp.stack(
        [
            jnp.concatenate([halved(m[1], side, TILE) for m in (proj_in, gate_in)], axis=0)
            for side in (0, TILE)
        ]
    )
    identity = jnp.eye(TILE, dtype=jnp.bfloat16)
    both = jnp.concatenate([identity - jnp.bfloat16(1.0 / TILE), identity], axis=0)
    def reordered(values):
        return jnp.concatenate(
            [lax.dynamic_slice_in_dim(values, start, half, axis=0) for start in (ours, theirs)], axis=0
        )

    def columns(values):
        return jnp.broadcast_to(values[:, None], (TILE, TILE))

    gain_in = [columns(norm_in_gain[u]) for u in range(2)]
    bias_in = [columns(norm_in_bias[u]) for u in range(2)]

    def project(held, offset, own, sib, mask, first_block):
        there = lax.rem(place + offset, 8)
        there_x = there // 4
        there_z = jnp.where(there_x == 0, there, 7 - there)
        last = lax.rem(z, 2)
        slot = jnp.where(there_z // 2 == x, lax.rem(there_z, 2), jnp.where(there_z == z, 2, -1))
        at = jnp.stack(
            [
                there_x,
                there_z,
                last,
                (there_x == x).astype(jnp.int32),
                (last == core).astype(jnp.int32),
                jnp.where(slot < 0, -1, 3 * there_x + slot),
            ]
        ).astype(jnp.int32)
        fixed = (both, gain_in[0], bias_in[0], enter_weights)
        return enter(own, sib, first_block, at, mask, *fixed, held)

    def hop(values, pairs):
        return [lax.ppermute(value, BOTH, pairs) for value in values]

    held = project(None, 0, pair_state, lax.ppermute(pair_state, BOTH, swap), masks, 0)
    below = hop([masks, pair_state], up)
    above = hop([masks, pair_state], down)
    part = TILE // 2
    middle_fixed = [
        gain_in[0],
        bias_in[0],
        columns(reordered(norm_out_gain[0])),
        columns(reordered(norm_out_bias[0])),
        0.5 * reordered(proj_out[0]).T,
        0.5 * gate_out[0].T,
        gain_in[1],
        bias_in[1],
        middle_weights,
    ]
    leave_fixed = [
        gain_in[1],
        bias_in[1],
        columns(norm_out_gain[1]),
        columns(norm_out_bias[1]),
        0.5 * proj_out[1].T,
        0.5 * gate_out[1].T,
    ]
    for step in range(1, 4):
        below, above, held, middle_fixed, leave_fixed = lax.optimization_barrier(
            (below, above, held, middle_fixed, leave_fixed)
        )
        now_below, now_above = below, above
        if step < 3:
            below = hop(now_below, up)
            above = hop(now_above, down)
        else:
            below = hop([now_below[0], now_below[1][:part]], up)
            above = hop([now_above[1][part:]], down)
        for offset, (mask, tile) in ((8 - step, now_below), (step, now_above)):
            held = project(held, offset, tile, lax.ppermute(tile, BOTH, swap), mask, 0)
    below, above, held = lax.optimization_barrier((below, above, held))
    held = project(held, 4, below[1], lax.ppermute(below[1], BOTH, swap), below[0], 0)
    held = project(held, 4, above[0], lax.ppermute(above[0], BOTH, swap), below[0], part // (GROUPS * SUB))
    states, *lefts, right, mask = held

    third = jnp.where(z // 2 == x, lax.rem(z, 2), 2)
    at_tri = jnp.stack([core, third]).astype(jnp.int32)
    kept, got = [], []
    for n in range(PARTS):
        if n >= 2:
            at_tri, got[n - 2] = lax.optimization_barrier((at_tri, got[n - 2]))
        stays, leaves = outgoing(at_tri, lefts, right, n)
        kept.append(stays)
        got.append(lax.ppermute(leaves, BOTH, swap))
    parts = kept + got
    at = jnp.stack([core, x, z, third]).astype(jnp.int32)
    pairs, states1 = middle(at, states, mask, middle_fixed, parts)
    kept1, sent1 = incoming(at, pairs)
    got1 = lax.ppermute(sent1, BOTH, swap)
    return leave(at, kept1, got1, states1, *leave_fixed)


def on_device_exchange(
    pair_state,
    pair_mask,
    norm_in_gain,
    norm_in_bias,
    proj_in,
    gate_in,
    norm_out_gain,
    norm_out_bias,
    proj_out,
    gate_out,
):
    mask_weight = pair_mask.astype(jnp.float32)[None]
    current = pair_state
    for update in range(2):
        normed = norm_last(
            current.astype(jnp.float32), norm_in_gain[update], norm_in_bias[update]
        ).astype(jnp.bfloat16)
        projected = jnp.einsum(
            "rcd,de->erc", normed, alternate(proj_in[update]), preferred_element_type=jnp.float32
        )
        gate_logit = jnp.einsum(
            "rcd,de->erc", normed, alternate(gate_in[update]), preferred_element_type=jnp.float32
        )
        paired = (projected * jax.nn.sigmoid(gate_logit) * mask_weight).astype(jnp.bfloat16)
        arrived = spread(paired)
        doubled, total_rows, total_cols = arrived.shape
        pair_count = doubled // 2
        arrived = arrived.reshape(pair_count, 2, total_rows, total_cols)
        left_side = arrived[:, 0]
        right_side = arrived[:, 1]
        pattern = "dik,djk->dij" if update == 0 else "dki,dkj->dij"
        triangle_out = jnp.einsum(
            pattern, left_side, right_side, preferred_element_type=jnp.float32
        ).astype(jnp.bfloat16)
        returned = gather_back(triangle_out)
        normed_out = norm_first(
            returned.astype(jnp.float32), norm_out_gain[update], norm_out_bias[update]
        ).astype(jnp.bfloat16)
        gate_value = jax.nn.sigmoid(
            jnp.einsum("rcd,df->rcf", normed, gate_out[update], preferred_element_type=jnp.float32)
        )
        change = (
            jnp.einsum(
                "erc,ef->rcf", normed_out, proj_out[update], preferred_element_type=jnp.float32
            )
            * gate_value
        )
        current = (current.astype(jnp.float32) + change).astype(jnp.bfloat16)
    return current


def on_device(pair_state, *others):
    square = pair_state.shape == (TILE, TILE, TILE)
    if square and lax.axis_size("row") == 4 and lax.axis_size("col") == 4:
        return on_device_ring(pair_state, *others)
    return on_device_exchange(pair_state, *others)


def solution(mesh):
    return jax.shard_map(
        on_device,
        mesh=mesh,
        in_specs=(
            P(("ens", "row"), "col", None),
            P(("ens", "row"), "col"),
            P(),
            P(),
            P(),
            P(),
            P(),
            P(),
            P(),
            P(),
        ),
        out_specs=P(("ens", "row"), "col", None),
        check_vma=False,
    )
```

```python
import jax
import jax.numpy as jnp
from jax import lax
from jax.experimental import pallas as pl
from jax.experimental.pallas import tpu as pltpu
from jax.sharding import PartitionSpec as P

epsilon = 1e-05


def norm_last(values, norm_gain, norm_bias):
    centre = jnp.mean(values, axis=-1, keepdims=True)
    variance = jnp.mean(jnp.square(values - centre), axis=-1, keepdims=True)
    return (values - centre) * lax.rsqrt(variance + epsilon) * norm_gain + norm_bias


def norm_first(values, norm_gain, norm_bias):
    centre = jnp.mean(values, axis=0, keepdims=True)
    variance = jnp.mean(jnp.square(values - centre), axis=0, keepdims=True)
    return (values - centre) * lax.rsqrt(variance + epsilon) * norm_gain[:, None, None] + norm_bias[
        :, None, None
    ]


def alternate(matrix):
    in_width, out_width = matrix.shape
    half_width = out_width // 2
    return matrix.reshape(in_width, 2, half_width).transpose(0, 2, 1).reshape(in_width, out_width)


def spread(paired):
    arrived = lax.all_to_all(paired, ("row", "col"), split_axis=0, concat_axis=1, tiled=True)
    n_row = lax.axis_size("row")
    n_col = lax.axis_size("col")
    channels, stacked, tile_cols = arrived.shape
    tile_rows = stacked // (n_row * n_col)
    arrived = arrived.reshape(channels, n_row, n_col, tile_rows, tile_cols).transpose(0, 1, 3, 2, 4)
    return arrived.reshape(channels, n_row * tile_rows, n_col * tile_cols)


def gather_back(triangle_out):
    n_row = lax.axis_size("row")
    n_col = lax.axis_size("col")
    channels, total_rows, total_cols = triangle_out.shape
    tile_rows = total_rows // n_row
    tile_cols = total_cols // n_col
    pieces = triangle_out.reshape(channels, n_row, tile_rows, n_col, tile_cols).transpose(
        1, 3, 0, 2, 4
    )
    pieces = pieces.reshape(n_row * n_col * channels, tile_rows, tile_cols)
    return lax.all_to_all(pieces, ("row", "col"), split_axis=0, concat_axis=0, tiled=True)


TILE = 128
SUB = 16
BLOCKS = TILE // SUB
CHUNK = 2
PITCH = SUB + 1
GROUPS = 2
MIDDLE_GROUPS = 4
VMEM_LIMIT = 40 * 1024 * 1024
BOTH = ("row", "col")
NT = (((1,), (1,)), ((), ()))
TN = (((0,), (0,)), ((), ()))


def channels_first(rows, matrix):
    return lax.dot_general(matrix, rows, NT, preferred_element_type=jnp.float32)


def norm_apart(apart, gain, bias):
    variance = jnp.mean(apart * apart, axis=0, keepdims=True)
    wide_gain = jnp.concatenate([gain[...]] * CHUNK, axis=1)
    wide_bias = jnp.concatenate([bias[...]] * CHUNK, axis=1)
    return (apart * lax.rsqrt(variance + epsilon) * wide_gain + wide_bias).astype(jnp.bfloat16)


def norm_channels(values, gain, bias):
    return norm_apart(values - jnp.mean(values, axis=0, keepdims=True), gain, bias)


def product(matrix, values):
    return jnp.dot(matrix, values, preferred_element_type=jnp.float32)


def gated(weights, normed):
    both = product(weights, normed)
    half = both.shape[0] // 2
    return both[:half] * jnp.tanh(both[half:]) + both[:half]


def turn_masked(chunks, mask_rows, turn):
    count = chunks[0].shape[0]
    for r in range(SUB):
        lanes = slice(r % CHUNK * TILE, (r % CHUNK + 1) * TILE)
        turn[pl.ds(r, count, stride=PITCH), :] = chunks[r // CHUNK][:, lanes] * mask_rows[r : r + 1, :]


def chunk_of(turn, first):
    return jnp.concatenate([turn[pl.ds(first + r, TILE, stride=PITCH), :] for r in range(CHUNK)], axis=1)


def rows_of(group):
    return pl.ds(pl.multiple_of(group * SUB, SUB), SUB)


def unturn(turn, places, group):
    for n, (out, d) in enumerate(places):
        out[0, d, rows_of(group), :] = turn[n * PITCH : n * PITCH + SUB, :].astype(jnp.bfloat16)


def enter_kernel(at, own, sib, mask, both, gain, bias, weights, *rest):
    state_out, left_low, left_high, right_out, mask_out, turn = rest[-6:]
    step = pl.program_id(0)
    use_own = (step == 1) == (at[4] == 1)
    mask_out[0, 0] = mask[0]

    def finish(group, paired):
        turn_masked(paired, mask[0, rows_of(group), :].astype(jnp.float32), turn)
        unturn(turn, [(out, d) for out in (left_low, left_high, right_out) for d in range(out.shape[1])], group)

    def turned_chunks(tile, group, matrix):
        rows = tile[rows_of(group)].reshape(SUB * TILE, TILE)
        size = CHUNK * TILE
        return [channels_first(rows[n * size : (n + 1) * size], matrix) for n in range(SUB // CHUNK)]

    @pl.when(use_own)
    def _():
        @pl.loop(0, GROUPS)
        def _(group):
            chunks = turned_chunks(own, group, both[...])
            paired = [gated(weights[...], norm_apart(chunk[:TILE], gain, bias)) for chunk in chunks]
            state_out[group] = jnp.concatenate(
                [chunk[TILE:].astype(jnp.bfloat16) for chunk in chunks], axis=1
            )
            finish(group, paired)

    @pl.when(jnp.logical_not(use_own))
    def _():
        @pl.loop(0, GROUPS)
        def _(group):
            chunks = turned_chunks(sib, group, both[:TILE])
            finish(group, [gated(weights[...], norm_apart(chunk, gain, bias)) for chunk in chunks])


def enter(own, sib, first_block, at, mask, both, gain, bias, weights, held):
    n_block = own.shape[0] // (GROUPS * SUB)
    blocks = TILE // (GROUPS * SUB)
    high = GROUPS * SUB
    full = pl.BlockSpec(memory_space=pl.ANY)

    def core_of(step, at):
        return jnp.where(step == 1, at[2], 1 - at[2])

    def is_own(step, at):
        return (step == 1) == (at[4] == 1)

    def own_map(step, block, at):
        return (jnp.where(is_own(step, at), block, jnp.where(step == 0, 0, n_block - 1)), 0, 0)

    def sib_map(step, block, at):
        return (jnp.where(is_own(step, at), jnp.where(step == 0, 0, n_block - 1), block), 0, 0)

    def mask_map(step, block, at):
        return (core_of(step, at), first_block + block, 0)

    def mask_out_map(step, block, at):
        return (2 * at[0] + core_of(step, at), at[1], first_block + block, 0)

    def state_map(step, block, at):
        kept = jnp.where(is_own(step, at), block, jnp.where(step == 0, 0, n_block - 1))
        return (jnp.where(at[5] < 0, 6 * blocks, at[5] * blocks + first_block + kept), 0, 0)

    def left_map(step, block, at):
        return (at[1], 0, (2 * at[0] + core_of(step, at)) * blocks + first_block + block, 0)

    def right_map(step, block, at):
        slot = jnp.where(at[3] == 1, core_of(step, at), 2)
        return (at[1], 0, slot * blocks + first_block + block, 0)

    half = weights.shape[0] // 4
    same = lambda step, block, at: (0, 0)
    shapes = (
        jax.ShapeDtypeStruct((6 * BLOCKS + GROUPS, TILE, SUB * TILE), jnp.bfloat16),
        jax.ShapeDtypeStruct((4, half // 2, 4 * TILE, TILE), jnp.bfloat16),
        jax.ShapeDtypeStruct((4, half // 2, 4 * TILE, TILE), jnp.bfloat16),
        jax.ShapeDtypeStruct((4, half, 3 * TILE, TILE), jnp.bfloat16),
        jax.ShapeDtypeStruct((4, 4, TILE, TILE), jnp.bfloat16),
    )
    in_specs = [
        pl.BlockSpec((high, TILE, TILE), own_map),
        pl.BlockSpec((high, TILE, TILE), sib_map),
        pl.BlockSpec((1, high, TILE), mask_map),
        pl.BlockSpec((2 * TILE, TILE), same),
        pl.BlockSpec((TILE, TILE), same),
        pl.BlockSpec((TILE, TILE), same),
        pl.BlockSpec((4 * half, TILE), same),
    ]
    operands = [own, sib, mask, both, gain, bias, weights]
    aliases = {}
    if held is not None:
        aliases = {len(operands) + 1 + n: n for n in range(5)}
        operands += list(held)
        in_specs += [full] * 5
    pairs = 2 * own.shape[0] * TILE
    return pl.pallas_call(
        enter_kernel,
        grid_spec=pltpu.PrefetchScalarGridSpec(
            num_scalar_prefetch=1,
            grid=(2, n_block),
            in_specs=in_specs,
            out_specs=[
                pl.BlockSpec((GROUPS, TILE, SUB * TILE), state_map),
                pl.BlockSpec((1, half // 2, high, TILE), left_map),
                pl.BlockSpec((1, half // 2, high, TILE), left_map),
                pl.BlockSpec((1, half, high, TILE), right_map),
                pl.BlockSpec((1, 1, high, TILE), mask_out_map),
            ],
            scratch_shapes=[pltpu.VMEM((2 * half * PITCH, TILE), jnp.float32)],
        ),
        out_shape=shapes,
        input_output_aliases=aliases,
        compiler_params=pltpu.CompilerParams(
            dimension_semantics=("arbitrary", "arbitrary"), vmem_limit_bytes=VMEM_LIMIT
        ),
        cost_estimate=pl.CostEstimate(
            flops=pairs * TILE * 1024, bytes_accessed=pairs * 1024, transcendentals=pairs * TILE
        ),
        name="enter",
    )(at, *operands)


def outgoing_kernel(at, left, right, keep, send):
    core = at[0]
    third = pl.multiple_of(at[1] * TILE, TILE)

    def wide(ref, d, start, count):
        return jnp.concatenate([ref[k, d, pl.ds(start, count), :] for k in range(4)], axis=1)

    blocks = [2 * x + which for which in (core, 1 - core) for x in range(2)]
    for d in range(TOGETHER):
        columns = jnp.concatenate(
            [wide(right, d, 0, 2 * TILE), wide(right, d, third, TILE)], axis=0
        )
        rows = jnp.concatenate(
            [wide(left, d, pl.multiple_of(block * TILE, TILE), TILE) for block in blocks], axis=0
        )
        sums = lax.dot_general(rows, columns, NT, preferred_element_type=jnp.float32)
        for slot in range(3):
            lanes = slice(slot * TILE, (slot + 1) * TILE)
            keep[slot, d] = sums[: 2 * TILE, lanes].astype(jnp.bfloat16)
            send[slot, d] = sums[2 * TILE :, lanes].astype(jnp.bfloat16)


TOGETHER = 2
PARTS = 2


def outgoing(at, lefts, right, part):
    count = right.shape[1] // PARTS
    steps = count // TOGETHER
    first = part * steps
    left = lefts[part * len(lefts) // PARTS]
    left_first = part % (PARTS // len(lefts)) * steps
    out = jax.ShapeDtypeStruct((3, count, 2 * TILE, TILE), jnp.bfloat16)
    return pl.pallas_call(
        outgoing_kernel,
        grid_spec=pltpu.PrefetchScalarGridSpec(
            num_scalar_prefetch=1,
            grid=(steps,),
            in_specs=[
                pl.BlockSpec((4, TOGETHER, 4 * TILE, TILE), lambda d, at: (0, left_first + d, 0, 0)),
                pl.BlockSpec((4, TOGETHER, 3 * TILE, TILE), lambda d, at: (0, first + d, 0, 0)),
            ],
            out_specs=[pl.BlockSpec((3, TOGETHER, 2 * TILE, TILE), lambda d, at: (0, d, 0, 0))] * 2,
        ),
        out_shape=(out, out),
        compiler_params=pltpu.CompilerParams(
            dimension_semantics=("arbitrary",), vmem_limit_bytes=VMEM_LIMIT
        ),
        cost_estimate=pl.CostEstimate(
            flops=count * 512 * 384 * 1024, bytes_accessed=count * 1300 * 1024, transcendentals=0
        ),
        name="outgoing",
    )(at, left, right)


def middle_kernel(
    at, state, mask, gain0, bias0, gain_out, bias_out, proj, gate, gain1, bias1, weights, *rest
):
    parts, (pairs_out, state_out, turn, turn_out) = rest[:-4], rest[-4:]

    @pl.loop(0, MIDDLE_GROUPS)
    def _(group):
        for n, (part, d) in enumerate((part, d) for part in parts for d in range(part.shape[1])):
            turn[n * PITCH : n * PITCH + SUB, :] = part[0, d, rows_of(group), :].astype(jnp.float32)
        changed, paired = [], []
        for first in range(0, SUB, CHUNK):
            before = state[group, :, first * TILE : (first + CHUNK) * TILE].astype(jnp.float32)
            gate_value = jnp.tanh(product(gate[...], norm_channels(before, gain0, bias0)))
            out = product(proj[...], norm_channels(chunk_of(turn, first), gain_out, bias_out))
            changed.append((before + (out * gate_value + out)).astype(jnp.bfloat16))
            normed1 = norm_channels(changed[-1].astype(jnp.float32), gain1, bias1)
            paired.append(gated(weights[0], normed1))
        state_out[group] = jnp.concatenate(changed, axis=1)
        turn_masked(paired, mask[0, 0, rows_of(group), :].astype(jnp.float32), turn_out)
        unturn(turn_out, [(pairs_out, d) for d in range(TILE)], group)


def middle(at, states, mask, fixed, parts):
    def column(slot, at):
        return jnp.where(slot == 2, at[2], 2 * at[1] + slot)

    blocks = BLOCKS // MIDDLE_GROUPS
    high = MIDDLE_GROUPS * SUB
    square = pl.BlockSpec((TILE, TILE), lambda slot, x, block, at: (0, 0))
    tri = pl.BlockSpec(
        (1, parts[0].shape[1], high, TILE), lambda slot, x, block, at: (slot, 0, x * blocks + block, 0)
    )
    state_spec = pl.BlockSpec(
        (MIDDLE_GROUPS, TILE, SUB * TILE),
        lambda slot, x, block, at: ((x * 3 + jnp.where(slot == 2, at[3], slot)) * blocks + block, 0, 0),
    )
    pairs = 6 * TILE * TILE
    return pl.pallas_call(
        middle_kernel,
        grid_spec=pltpu.PrefetchScalarGridSpec(
            num_scalar_prefetch=1,
            grid=(3, 2, blocks),
            in_specs=[
                state_spec,
                pl.BlockSpec(
                    (1, 1, high, TILE),
                    lambda slot, x, block, at: (2 * x + at[0], column(slot, at), block, 0),
                ),
            ]
            + [square] * 8
            + [
                pl.BlockSpec(
                    (1, 2 * TILE, TILE),
                    lambda slot, x, block, at: (jnp.where(slot == 2, 1, 0), 0, 0),
                )
            ]
            + [tri] * len(parts),
            out_specs=[
                pl.BlockSpec(
                    (1, TILE, high, TILE), lambda slot, x, block, at: (slot, 0, x * blocks + block, 0)
                ),
                pl.BlockSpec(
                    (MIDDLE_GROUPS, TILE, SUB * TILE),
                    lambda slot, x, block, at: (
                        jnp.where(slot == 2, x * blocks + block, 2 * blocks), 0, 0,
                    ),
                ),
            ],
            scratch_shapes=[pltpu.VMEM((TILE * PITCH, TILE), jnp.float32)] * 2,
        ),
        out_shape=(
            jax.ShapeDtypeStruct((3, TILE, 2 * TILE, TILE), jnp.bfloat16),
            jax.ShapeDtypeStruct((2 * BLOCKS + MIDDLE_GROUPS, TILE, SUB * TILE), jnp.bfloat16),
        ),
        compiler_params=pltpu.CompilerParams(
            dimension_semantics=("arbitrary",) * 3, vmem_limit_bytes=VMEM_LIMIT
        ),
        cost_estimate=pl.CostEstimate(
            flops=pairs * TILE * 1024, bytes_accessed=pairs * 1024, transcendentals=pairs * TILE * 2
        ),
        name="middle",
    )(at, states, mask, *fixed, *parts)


CHANNELS = 8


def incoming_kernel(at, pairs, keep, send):
    core = at[0]
    for d in range(CHANNELS):
        right = pairs[2, d]
        keep[d] = lax.dot_general(
            pairs[core, d], right, TN, preferred_element_type=jnp.float32
        ).astype(jnp.bfloat16)
        send[d] = lax.dot_general(
            pairs[1 - core, d], right, TN, preferred_element_type=jnp.float32
        ).astype(jnp.bfloat16)


def incoming(at, pairs):
    out_spec = pl.BlockSpec((CHANNELS, TILE, TILE), lambda d, at: (d, 0, 0))
    return pl.pallas_call(
        incoming_kernel,
        grid_spec=pltpu.PrefetchScalarGridSpec(
            num_scalar_prefetch=1,
            grid=(TILE // CHANNELS,),
            in_specs=[pl.BlockSpec((3, CHANNELS, 2 * TILE, TILE), lambda d, at: (0, d, 0, 0))],
            out_specs=[out_spec, out_spec],
        ),
        out_shape=(
            jax.ShapeDtypeStruct((TILE, TILE, TILE), jnp.bfloat16),
            jax.ShapeDtypeStruct((TILE, TILE, TILE), jnp.bfloat16),
        ),
        compiler_params=pltpu.CompilerParams(
            dimension_semantics=("arbitrary",), vmem_limit_bytes=VMEM_LIMIT
        ),
        cost_estimate=pl.CostEstimate(
            flops=TILE * 512 * 256 * TILE, bytes_accessed=36 * 2**20, transcendentals=0
        ),
        name="incoming",
    )(at, pairs)


def leave_kernel(at, kept, got, state, gain1, bias1, gain_out, bias_out, proj, gate, result, turn):
    @pl.loop(0, GROUPS)
    def _(group):
        for d in range(TILE):
            turn[d * PITCH : d * PITCH + SUB, :] = kept[d, rows_of(group), :].astype(jnp.float32) + got[
                d, rows_of(group), :
            ].astype(jnp.float32)
        changed = []
        for first in range(0, SUB, CHUNK):
            before = state[group, :, first * TILE : (first + CHUNK) * TILE].astype(jnp.float32)
            gate_value = jnp.tanh(product(gate[...], norm_channels(before, gain1, bias1)))
            out = product(proj[...], norm_channels(chunk_of(turn, first), gain_out, bias_out))
            changed.append((before + (out * gate_value + out)).astype(jnp.bfloat16))
        result[rows_of(group)] = jnp.concatenate([chunk.T for chunk in changed], axis=0).reshape(
            SUB, TILE, TILE
        )


def leave(at, kept, got, states, *fixed):
    blocks = BLOCKS // GROUPS
    square = pl.BlockSpec((TILE, TILE), lambda block, at: (0, 0))
    tri = pl.BlockSpec((TILE, GROUPS * SUB, TILE), lambda block, at: (0, block, 0))
    return pl.pallas_call(
        leave_kernel,
        grid_spec=pltpu.PrefetchScalarGridSpec(
            num_scalar_prefetch=1,
            grid=(blocks,),
            in_specs=[
                tri,
                tri,
                pl.BlockSpec((GROUPS, TILE, SUB * TILE), lambda block, at: (at[1] * blocks + block, 0, 0)),
            ]
            + [square] * 6,
            out_specs=pl.BlockSpec((GROUPS * SUB, TILE, TILE), lambda block, at: (block, 0, 0)),
            scratch_shapes=[pltpu.VMEM((TILE * PITCH, TILE), jnp.float32)],
        ),
        out_shape=jax.ShapeDtypeStruct((TILE, TILE, TILE), jnp.bfloat16),
        compiler_params=pltpu.CompilerParams(
            dimension_semantics=("arbitrary",), vmem_limit_bytes=VMEM_LIMIT
        ),
        cost_estimate=pl.CostEstimate(
            flops=TILE**3 * 512, bytes_accessed=20 * 2**20, transcendentals=TILE**3
        ),
        name="leave",
    )(at, kept, got, states, *fixed)


def on_device_ring(
    pair_state,
    pair_mask,
    norm_in_gain,
    norm_in_bias,
    proj_in,
    gate_in,
    norm_out_gain,
    norm_out_bias,
    proj_out,
    gate_out,
):
    row = lax.axis_index("row")
    z = lax.axis_index("col")
    x, core = row // 2, row % 2
    place = jnp.where(x == 0, z, 7 - z)

    def device(position, which):
        on_x, on_z = (0, position) if position < 4 else (1, 7 - position)
        return (2 * on_x + which) * 4 + on_z

    up = [(device(p, w), device((p + 1) % 8, w)) for p in range(8) for w in range(2)]
    down = [(target, source) for source, target in up]
    swap = [(device(p, w), device(p, 1 - w)) for p in range(8) for w in range(2)]

    own_mask = pair_mask.astype(jnp.bfloat16)
    sib_mask = lax.ppermute(own_mask, BOTH, swap)
    masks = jnp.where(core == 0, jnp.stack([own_mask, sib_mask]), jnp.stack([sib_mask, own_mask]))

    half = TILE // 2
    ours = core * half
    theirs = half - ours

    def halved(matrix, start, width):
        return (0.5 * lax.dynamic_slice_in_dim(matrix, start, width, axis=1)).T

    enter_weights = jnp.concatenate(
        [halved(m[0], side + ours, half) for m in (proj_in, gate_in) for side in (0, TILE)], axis=0
    )
    middle_weights = jnp.stack(
        [
            jnp.concatenate([halved(m[1], side, TILE) for m in (proj_in, gate_in)], axis=0)
            for side in (0, TILE)
        ]
    )
    identity = jnp.eye(TILE, dtype=jnp.bfloat16)
    both = jnp.concatenate([identity - jnp.bfloat16(1.0 / TILE), identity], axis=0)
    def reordered(values):
        return jnp.concatenate(
            [lax.dynamic_slice_in_dim(values, start, half, axis=0) for start in (ours, theirs)], axis=0
        )

    def columns(values):
        return jnp.broadcast_to(values[:, None], (TILE, TILE))

    gain_in = [columns(norm_in_gain[u]) for u in range(2)]
    bias_in = [columns(norm_in_bias[u]) for u in range(2)]

    def project(held, offset, own, sib, mask, first_block):
        there = lax.rem(place + offset, 8)
        there_x = there // 4
        there_z = jnp.where(there_x == 0, there, 7 - there)
        last = lax.rem(z, 2)
        slot = jnp.where(there_z // 2 == x, lax.rem(there_z, 2), jnp.where(there_z == z, 2, -1))
        at = jnp.stack(
            [
                there_x,
                there_z,
                last,
                (there_x == x).astype(jnp.int32),
                (last == core).astype(jnp.int32),
                jnp.where(slot < 0, -1, 3 * there_x + slot),
            ]
        ).astype(jnp.int32)
        fixed = (both, gain_in[0], bias_in[0], enter_weights)
        return enter(own, sib, first_block, at, mask, *fixed, held)

    def hop(values, pairs):
        return [lax.ppermute(value, BOTH, pairs) for value in values]

    held = project(None, 0, pair_state, lax.ppermute(pair_state, BOTH, swap), masks, 0)
    below = hop([masks, pair_state], up)
    above = hop([masks, pair_state], down)
    part = TILE // 2
    middle_fixed = [
        gain_in[0],
        bias_in[0],
        columns(reordered(norm_out_gain[0])),
        columns(reordered(norm_out_bias[0])),
        0.5 * reordered(proj_out[0]).T,
        0.5 * gate_out[0].T,
        gain_in[1],
        bias_in[1],
        middle_weights,
    ]
    leave_fixed = [
        gain_in[1],
        bias_in[1],
        columns(norm_out_gain[1]),
        columns(norm_out_bias[1]),
        0.5 * proj_out[1].T,
        0.5 * gate_out[1].T,
    ]
    for step in range(1, 4):
        below, above, held, middle_fixed, leave_fixed = lax.optimization_barrier(
            (below, above, held, middle_fixed, leave_fixed)
        )
        now_below, now_above = below, above
        if step < 3:
            below = hop(now_below, up)
            above = hop(now_above, down)
        else:
            below = hop([now_below[0], now_below[1][:part]], up)
            above = hop([now_above[1][part:]], down)
        for offset, (mask, tile) in ((8 - step, now_below), (step, now_above)):
            held = project(held, offset, tile, lax.ppermute(tile, BOTH, swap), mask, 0)
    below, above, held = lax.optimization_barrier((below, above, held))
    held = project(held, 4, below[1], lax.ppermute(below[1], BOTH, swap), below[0], 0)
    held = project(held, 4, above[0], lax.ppermute(above[0], BOTH, swap), below[0], part // (GROUPS * SUB))
    states, *lefts, right, mask = held

    third = jnp.where(z // 2 == x, lax.rem(z, 2), 2)
    at_tri = jnp.stack([core, third]).astype(jnp.int32)
    kept, got = [], []
    for n in range(PARTS):
        if n >= 2:
            at_tri, got[n - 2] = lax.optimization_barrier((at_tri, got[n - 2]))
        stays, leaves = outgoing(at_tri, lefts, right, n)
        kept.append(stays)
        got.append(lax.ppermute(leaves, BOTH, swap))
    parts = kept + got
    at = jnp.stack([core, x, z, third]).astype(jnp.int32)
    pairs, states1 = middle(at, states, mask, middle_fixed, parts)
    kept1, sent1 = incoming(at, pairs)
    got1 = lax.ppermute(sent1, BOTH, swap)
    return leave(at, kept1, got1, states1, *leave_fixed)


def on_device_exchange(
    pair_state,
    pair_mask,
    norm_in_gain,
    norm_in_bias,
    proj_in,
    gate_in,
    norm_out_gain,
    norm_out_bias,
    proj_out,
    gate_out,
):
    mask_weight = pair_mask.astype(jnp.float32)[None]
    current = pair_state
    for update in range(2):
        normed = norm_last(
            current.astype(jnp.float32), norm_in_gain[update], norm_in_bias[update]
        ).astype(jnp.bfloat16)
        projected = jnp.einsum(
            "rcd,de->erc", normed, alternate(proj_in[update]), preferred_element_type=jnp.float32
        )
        gate_logit = jnp.einsum(
            "rcd,de->erc", normed, alternate(gate_in[update]), preferred_element_type=jnp.float32
        )
        paired = (projected * jax.nn.sigmoid(gate_logit) * mask_weight).astype(jnp.bfloat16)
        arrived = spread(paired)
        doubled, total_rows, total_cols = arrived.shape
        pair_count = doubled // 2
        arrived = arrived.reshape(pair_count, 2, total_rows, total_cols)
        left_side = arrived[:, 0]
        right_side = arrived[:, 1]
        pattern = "dik,djk->dij" if update == 0 else "dki,dkj->dij"
        triangle_out = jnp.einsum(
            pattern, left_side, right_side, preferred_element_type=jnp.float32
        ).astype(jnp.bfloat16)
        returned = gather_back(triangle_out)
        normed_out = norm_first(
            returned.astype(jnp.float32), norm_out_gain[update], norm_out_bias[update]
        ).astype(jnp.bfloat16)
        gate_value = jax.nn.sigmoid(
            jnp.einsum("rcd,df->rcf", normed, gate_out[update], preferred_element_type=jnp.float32)
        )
        change = (
            jnp.einsum(
                "erc,ef->rcf", normed_out, proj_out[update], preferred_element_type=jnp.float32
            )
            * gate_value
        )
        current = (current.astype(jnp.float32) + change).astype(jnp.bfloat16)
    return current


def on_device(pair_state, *others):
    square = pair_state.shape == (TILE, TILE, TILE)
    if square and lax.axis_size("row") == 4 and lax.axis_size("col") == 4:
        return on_device_ring(pair_state, *others)
    return on_device_exchange(pair_state, *others)


def solution(mesh):
    return jax.shard_map(
        on_device,
        mesh=mesh,
        in_specs=(
            P(("ens", "row"), "col", None),
            P(("ens", "row"), "col"),
            P(),
            P(),
            P(),
            P(),
            P(),
            P(),
            P(),
            P(),
        ),
        out_specs=P(("ens", "row"), "col", None),
        check_vma=False,
    )
```

```python
import jax
import jax.numpy as jnp
from jax import lax
from jax.experimental import pallas as pl
from jax.experimental.pallas import tpu as pltpu
from jax.sharding import PartitionSpec as P

epsilon = 1e-05


def norm_last(values, norm_gain, norm_bias):
    centre = jnp.mean(values, axis=-1, keepdims=True)
    variance = jnp.mean(jnp.square(values - centre), axis=-1, keepdims=True)
    return (values - centre) * lax.rsqrt(variance + epsilon) * norm_gain + norm_bias


def norm_first(values, norm_gain, norm_bias):
    centre = jnp.mean(values, axis=0, keepdims=True)
    variance = jnp.mean(jnp.square(values - centre), axis=0, keepdims=True)
    return (values - centre) * lax.rsqrt(variance + epsilon) * norm_gain[:, None, None] + norm_bias[
        :, None, None
    ]


def alternate(matrix):
    in_width, out_width = matrix.shape
    half_width = out_width // 2
    return matrix.reshape(in_width, 2, half_width).transpose(0, 2, 1).reshape(in_width, out_width)


def spread(paired):
    arrived = lax.all_to_all(paired, ("row", "col"), split_axis=0, concat_axis=1, tiled=True)
    n_row = lax.axis_size("row")
    n_col = lax.axis_size("col")
    channels, stacked, tile_cols = arrived.shape
    tile_rows = stacked // (n_row * n_col)
    arrived = arrived.reshape(channels, n_row, n_col, tile_rows, tile_cols).transpose(0, 1, 3, 2, 4)
    return arrived.reshape(channels, n_row * tile_rows, n_col * tile_cols)


def gather_back(triangle_out):
    n_row = lax.axis_size("row")
    n_col = lax.axis_size("col")
    channels, total_rows, total_cols = triangle_out.shape
    tile_rows = total_rows // n_row
    tile_cols = total_cols // n_col
    pieces = triangle_out.reshape(channels, n_row, tile_rows, n_col, tile_cols).transpose(
        1, 3, 0, 2, 4
    )
    pieces = pieces.reshape(n_row * n_col * channels, tile_rows, tile_cols)
    return lax.all_to_all(pieces, ("row", "col"), split_axis=0, concat_axis=0, tiled=True)


TILE = 128
SUB = 16
BLOCKS = TILE // SUB
CHUNK = 2
PITCH = SUB + 1
GROUPS = 2
MIDDLE_GROUPS = 4
VMEM_LIMIT = 40 * 1024 * 1024
BOTH = ("row", "col")
NT = (((1,), (1,)), ((), ()))
TN = (((0,), (0,)), ((), ()))


def channels_first(rows, matrix):
    return lax.dot_general(matrix, rows, NT, preferred_element_type=jnp.float32)


def norm_apart(apart, gain, bias):
    variance = jnp.mean(apart * apart, axis=0, keepdims=True)
    wide_gain = jnp.concatenate([gain[...]] * CHUNK, axis=1)
    wide_bias = jnp.concatenate([bias[...]] * CHUNK, axis=1)
    return (apart * lax.rsqrt(variance + epsilon) * wide_gain + wide_bias).astype(jnp.bfloat16)


def norm_channels(values, centre, gain, bias):
    return norm_apart(product(centre[...], values), gain, bias)


def product(matrix, values):
    return jnp.dot(matrix, values, preferred_element_type=jnp.float32)


def gated(weights, normed):
    both = product(weights, normed)
    half = both.shape[0] // 2
    return both[:half] * jnp.tanh(both[half:]) + both[:half]


def turn_masked(chunks, mask_rows, turn):
    count = chunks[0].shape[0]
    for r in range(SUB):
        lanes = slice(r % CHUNK * TILE, (r % CHUNK + 1) * TILE)
        turn[pl.ds(r, count, stride=PITCH), :] = chunks[r // CHUNK][:, lanes] * mask_rows[r : r + 1, :]


def chunk_of(turn, first):
    return jnp.concatenate([turn[pl.ds(first + r, TILE, stride=PITCH), :] for r in range(CHUNK)], axis=1)


def rows_of(group):
    return pl.ds(pl.multiple_of(group * SUB, SUB), SUB)


def unturn(turn, places, group):
    for n, (out, d) in enumerate(places):
        out[0, d, rows_of(group), :] = turn[n * PITCH : n * PITCH + SUB, :].astype(jnp.bfloat16)


def enter_kernel(at, own, sib, mask, both, gain, bias, weights, *rest):
    state_out, left_low, left_high, right_out, mask_out, turn = rest[-6:]
    step = pl.program_id(0)
    use_own = (step == 1) == (at[4] == 1)
    mask_out[0, 0] = mask[0]

    def finish(group, paired):
        turn_masked(paired, mask[0, rows_of(group), :].astype(jnp.float32), turn)
        unturn(turn, [(out, d) for out in (left_low, left_high, right_out) for d in range(out.shape[1])], group)

    def turned_chunks(tile, group, matrix):
        rows = tile[rows_of(group)].reshape(SUB * TILE, TILE)
        size = CHUNK * TILE
        return [channels_first(rows[n * size : (n + 1) * size], matrix) for n in range(SUB // CHUNK)]

    @pl.when(use_own)
    def _():
        @pl.loop(0, GROUPS)
        def _(group):
            chunks = turned_chunks(own, group, both[...])
            paired = [gated(weights[...], norm_apart(chunk[:TILE], gain, bias)) for chunk in chunks]
            state_out[group] = jnp.concatenate(
                [chunk[TILE:].astype(jnp.bfloat16) for chunk in chunks], axis=1
            )
            finish(group, paired)

    @pl.when(jnp.logical_not(use_own))
    def _():
        @pl.loop(0, GROUPS)
        def _(group):
            chunks = turned_chunks(sib, group, both[:TILE])
            finish(group, [gated(weights[...], norm_apart(chunk, gain, bias)) for chunk in chunks])


def enter(own, sib, first_block, at, mask, both, gain, bias, weights, held):
    n_block = own.shape[0] // (GROUPS * SUB)
    blocks = TILE // (GROUPS * SUB)
    high = GROUPS * SUB
    full = pl.BlockSpec(memory_space=pl.ANY)

    def core_of(step, at):
        return jnp.where(step == 1, at[2], 1 - at[2])

    def is_own(step, at):
        return (step == 1) == (at[4] == 1)

    def own_map(step, block, at):
        return (jnp.where(is_own(step, at), block, jnp.where(step == 0, 0, n_block - 1)), 0, 0)

    def sib_map(step, block, at):
        return (jnp.where(is_own(step, at), jnp.where(step == 0, 0, n_block - 1), block), 0, 0)

    def mask_map(step, block, at):
        return (core_of(step, at), first_block + block, 0)

    def mask_out_map(step, block, at):
        return (2 * at[0] + core_of(step, at), at[1], first_block + block, 0)

    def state_map(step, block, at):
        kept = jnp.where(is_own(step, at), block, jnp.where(step == 0, 0, n_block - 1))
        return (jnp.where(at[5] < 0, 6 * blocks, at[5] * blocks + first_block + kept), 0, 0)

    def left_map(step, block, at):
        return (at[1], 0, (2 * at[0] + core_of(step, at)) * blocks + first_block + block, 0)

    def right_map(step, block, at):
        slot = jnp.where(at[3] == 1, core_of(step, at), 2)
        return (at[1], 0, slot * blocks + first_block + block, 0)

    half = weights.shape[0] // 4
    same = lambda step, block, at: (0, 0)
    shapes = (
        jax.ShapeDtypeStruct((6 * BLOCKS + GROUPS, TILE, SUB * TILE), jnp.bfloat16),
        jax.ShapeDtypeStruct((4, half // 2, 4 * TILE, TILE), jnp.bfloat16),
        jax.ShapeDtypeStruct((4, half // 2, 4 * TILE, TILE), jnp.bfloat16),
        jax.ShapeDtypeStruct((4, half, 3 * TILE, TILE), jnp.bfloat16),
        jax.ShapeDtypeStruct((4, 4, TILE, TILE), jnp.bfloat16),
    )
    in_specs = [
        pl.BlockSpec((high, TILE, TILE), own_map),
        pl.BlockSpec((high, TILE, TILE), sib_map),
        pl.BlockSpec((1, high, TILE), mask_map),
        pl.BlockSpec((2 * TILE, TILE), same),
        pl.BlockSpec((TILE, TILE), same),
        pl.BlockSpec((TILE, TILE), same),
        pl.BlockSpec((4 * half, TILE), same),
    ]
    operands = [own, sib, mask, both, gain, bias, weights]
    aliases = {}
    if held is not None:
        aliases = {len(operands) + 1 + n: n for n in range(5)}
        operands += list(held)
        in_specs += [full] * 5
    pairs = 2 * own.shape[0] * TILE
    return pl.pallas_call(
        enter_kernel,
        grid_spec=pltpu.PrefetchScalarGridSpec(
            num_scalar_prefetch=1,
            grid=(2, n_block),
            in_specs=in_specs,
            out_specs=[
                pl.BlockSpec((GROUPS, TILE, SUB * TILE), state_map),
                pl.BlockSpec((1, half // 2, high, TILE), left_map),
                pl.BlockSpec((1, half // 2, high, TILE), left_map),
                pl.BlockSpec((1, half, high, TILE), right_map),
                pl.BlockSpec((1, 1, high, TILE), mask_out_map),
            ],
            scratch_shapes=[pltpu.VMEM((2 * half * PITCH, TILE), jnp.float32)],
        ),
        out_shape=shapes,
        input_output_aliases=aliases,
        compiler_params=pltpu.CompilerParams(
            dimension_semantics=("arbitrary", "arbitrary"), vmem_limit_bytes=VMEM_LIMIT
        ),
        cost_estimate=pl.CostEstimate(
            flops=pairs * TILE * 1024, bytes_accessed=pairs * 1024, transcendentals=pairs * TILE
        ),
        name="enter",
    )(at, *operands)


def outgoing_kernel(at, left, right, keep, send):
    core = at[0]
    third = pl.multiple_of(at[1] * TILE, TILE)

    def wide(ref, d, start, count):
        return jnp.concatenate([ref[k, d, pl.ds(start, count), :] for k in range(4)], axis=1)

    blocks = [2 * x + which for which in (core, 1 - core) for x in range(2)]
    for d in range(TOGETHER):
        columns = jnp.concatenate(
            [wide(right, d, 0, 2 * TILE), wide(right, d, third, TILE)], axis=0
        )
        rows = jnp.concatenate(
            [wide(left, d, pl.multiple_of(block * TILE, TILE), TILE) for block in blocks], axis=0
        )
        sums = lax.dot_general(rows, columns, NT, preferred_element_type=jnp.float32)
        for slot in range(3):
            lanes = slice(slot * TILE, (slot + 1) * TILE)
            keep[slot, d] = sums[: 2 * TILE, lanes].astype(jnp.bfloat16)
            send[slot, d] = sums[2 * TILE :, lanes].astype(jnp.bfloat16)


TOGETHER = 2
PARTS = 2


def outgoing(at, lefts, right, part):
    count = right.shape[1] // PARTS
    steps = count // TOGETHER
    first = part * steps
    left = lefts[part * len(lefts) // PARTS]
    left_first = part % (PARTS // len(lefts)) * steps
    out = jax.ShapeDtypeStruct((3, count, 2 * TILE, TILE), jnp.bfloat16)
    return pl.pallas_call(
        outgoing_kernel,
        grid_spec=pltpu.PrefetchScalarGridSpec(
            num_scalar_prefetch=1,
            grid=(steps,),
            in_specs=[
                pl.BlockSpec((4, TOGETHER, 4 * TILE, TILE), lambda d, at: (0, left_first + d, 0, 0)),
                pl.BlockSpec((4, TOGETHER, 3 * TILE, TILE), lambda d, at: (0, first + d, 0, 0)),
            ],
            out_specs=[pl.BlockSpec((3, TOGETHER, 2 * TILE, TILE), lambda d, at: (0, d, 0, 0))] * 2,
        ),
        out_shape=(out, out),
        compiler_params=pltpu.CompilerParams(
            dimension_semantics=("arbitrary",), vmem_limit_bytes=VMEM_LIMIT
        ),
        cost_estimate=pl.CostEstimate(
            flops=count * 512 * 384 * 1024, bytes_accessed=count * 1300 * 1024, transcendentals=0
        ),
        name="outgoing",
    )(at, left, right)


def middle_kernel(
    at, state, mask, centre, gain0, bias0, gain_out, bias_out, proj, gate, gain1, bias1, weights, *rest
):
    parts, (pairs_out, state_out, turn, turn_out) = rest[:-4], rest[-4:]

    @pl.loop(0, MIDDLE_GROUPS)
    def _(group):
        for n, (part, d) in enumerate((part, d) for part in parts for d in range(part.shape[1])):
            turn[n * PITCH : n * PITCH + SUB, :] = part[0, d, rows_of(group), :].astype(jnp.float32)
        changed, paired = [], []
        for first in range(0, SUB, CHUNK):
            before = state[group, :, first * TILE : (first + CHUNK) * TILE]
            gate_value = jnp.tanh(product(gate[...], norm_channels(before, centre, gain0, bias0)))
            triangle = chunk_of(turn, first).astype(jnp.bfloat16)
            out = product(proj[...], norm_channels(triangle, centre, gain_out, bias_out))
            changed.append(
                (before.astype(jnp.float32) + (out * gate_value + out)).astype(jnp.bfloat16)
            )
            normed1 = norm_channels(changed[-1], centre, gain1, bias1)
            paired.append(gated(weights[0], normed1))
        state_out[group] = jnp.concatenate(changed, axis=1)
        turn_masked(paired, mask[0, 0, rows_of(group), :].astype(jnp.float32), turn_out)
        unturn(turn_out, [(pairs_out, d) for d in range(TILE)], group)


def middle(at, states, mask, fixed, parts):
    def column(slot, at):
        return jnp.where(slot == 2, at[2], 2 * at[1] + slot)

    blocks = BLOCKS // MIDDLE_GROUPS
    high = MIDDLE_GROUPS * SUB
    square = pl.BlockSpec((TILE, TILE), lambda slot, x, block, at: (0, 0))
    tri = pl.BlockSpec(
        (1, parts[0].shape[1], high, TILE), lambda slot, x, block, at: (slot, 0, x * blocks + block, 0)
    )
    state_spec = pl.BlockSpec(
        (MIDDLE_GROUPS, TILE, SUB * TILE),
        lambda slot, x, block, at: ((x * 3 + jnp.where(slot == 2, at[3], slot)) * blocks + block, 0, 0),
    )
    pairs = 6 * TILE * TILE
    return pl.pallas_call(
        middle_kernel,
        grid_spec=pltpu.PrefetchScalarGridSpec(
            num_scalar_prefetch=1,
            grid=(3, 2, blocks),
            in_specs=[
                state_spec,
                pl.BlockSpec(
                    (1, 1, high, TILE),
                    lambda slot, x, block, at: (2 * x + at[0], column(slot, at), block, 0),
                ),
            ]
            + [square] * 9
            + [
                pl.BlockSpec(
                    (1, 2 * TILE, TILE),
                    lambda slot, x, block, at: (jnp.where(slot == 2, 1, 0), 0, 0),
                )
            ]
            + [tri] * len(parts),
            out_specs=[
                pl.BlockSpec(
                    (1, TILE, high, TILE), lambda slot, x, block, at: (slot, 0, x * blocks + block, 0)
                ),
                pl.BlockSpec(
                    (MIDDLE_GROUPS, TILE, SUB * TILE),
                    lambda slot, x, block, at: (
                        jnp.where(slot == 2, x * blocks + block, 2 * blocks), 0, 0,
                    ),
                ),
            ],
            scratch_shapes=[pltpu.VMEM((TILE * PITCH, TILE), jnp.float32)] * 2,
        ),
        out_shape=(
            jax.ShapeDtypeStruct((3, TILE, 2 * TILE, TILE), jnp.bfloat16),
            jax.ShapeDtypeStruct((2 * BLOCKS + MIDDLE_GROUPS, TILE, SUB * TILE), jnp.bfloat16),
        ),
        compiler_params=pltpu.CompilerParams(
            dimension_semantics=("arbitrary",) * 3, vmem_limit_bytes=VMEM_LIMIT
        ),
        cost_estimate=pl.CostEstimate(
            flops=pairs * TILE * 1024, bytes_accessed=pairs * 1024, transcendentals=pairs * TILE * 2
        ),
        name="middle",
    )(at, states, mask, *fixed, *parts)


CHANNELS = 8


def incoming_kernel(at, pairs, keep, send):
    core = at[0]
    for d in range(CHANNELS):
        right = pairs[2, d]
        keep[d] = lax.dot_general(
            pairs[core, d], right, TN, preferred_element_type=jnp.float32
        ).astype(jnp.bfloat16)
        send[d] = lax.dot_general(
            pairs[1 - core, d], right, TN, preferred_element_type=jnp.float32
        ).astype(jnp.bfloat16)


def incoming(at, pairs):
    out_spec = pl.BlockSpec((CHANNELS, TILE, TILE), lambda d, at: (d, 0, 0))
    return pl.pallas_call(
        incoming_kernel,
        grid_spec=pltpu.PrefetchScalarGridSpec(
            num_scalar_prefetch=1,
            grid=(TILE // CHANNELS,),
            in_specs=[pl.BlockSpec((3, CHANNELS, 2 * TILE, TILE), lambda d, at: (0, d, 0, 0))],
            out_specs=[out_spec, out_spec],
        ),
        out_shape=(
            jax.ShapeDtypeStruct((TILE, TILE, TILE), jnp.bfloat16),
            jax.ShapeDtypeStruct((TILE, TILE, TILE), jnp.bfloat16),
        ),
        compiler_params=pltpu.CompilerParams(
            dimension_semantics=("arbitrary",), vmem_limit_bytes=VMEM_LIMIT
        ),
        cost_estimate=pl.CostEstimate(
            flops=TILE * 512 * 256 * TILE, bytes_accessed=36 * 2**20, transcendentals=0
        ),
        name="incoming",
    )(at, pairs)


def leave_kernel(at, kept, got, state, centre, gain1, bias1, gain_out, bias_out, proj, gate, result, turn):
    @pl.loop(0, GROUPS)
    def _(group):
        for d in range(TILE):
            turn[d * PITCH : d * PITCH + SUB, :] = kept[d, rows_of(group), :].astype(jnp.float32) + got[
                d, rows_of(group), :
            ].astype(jnp.float32)
        changed = []
        for first in range(0, SUB, CHUNK):
            before = state[group, :, first * TILE : (first + CHUNK) * TILE]
            gate_value = jnp.tanh(product(gate[...], norm_channels(before, centre, gain1, bias1)))
            triangle = chunk_of(turn, first).astype(jnp.bfloat16)
            out = product(proj[...], norm_channels(triangle, centre, gain_out, bias_out))
            changed.append(
                (before.astype(jnp.float32) + (out * gate_value + out)).astype(jnp.bfloat16)
            )
        result[rows_of(group)] = jnp.concatenate([chunk.T for chunk in changed], axis=0).reshape(
            SUB, TILE, TILE
        )


def leave(at, kept, got, states, *fixed):
    blocks = BLOCKS // GROUPS
    square = pl.BlockSpec((TILE, TILE), lambda block, at: (0, 0))
    tri = pl.BlockSpec((TILE, GROUPS * SUB, TILE), lambda block, at: (0, block, 0))
    return pl.pallas_call(
        leave_kernel,
        grid_spec=pltpu.PrefetchScalarGridSpec(
            num_scalar_prefetch=1,
            grid=(blocks,),
            in_specs=[
                tri,
                tri,
                pl.BlockSpec((GROUPS, TILE, SUB * TILE), lambda block, at: (at[1] * blocks + block, 0, 0)),
            ]
            + [square] * 7,
            out_specs=pl.BlockSpec((GROUPS * SUB, TILE, TILE), lambda block, at: (block, 0, 0)),
            scratch_shapes=[pltpu.VMEM((TILE * PITCH, TILE), jnp.float32)],
        ),
        out_shape=jax.ShapeDtypeStruct((TILE, TILE, TILE), jnp.bfloat16),
        compiler_params=pltpu.CompilerParams(
            dimension_semantics=("arbitrary",), vmem_limit_bytes=VMEM_LIMIT
        ),
        cost_estimate=pl.CostEstimate(
            flops=TILE**3 * 512, bytes_accessed=20 * 2**20, transcendentals=TILE**3
        ),
        name="leave",
    )(at, kept, got, states, *fixed)


def on_device_ring(
    pair_state,
    pair_mask,
    norm_in_gain,
    norm_in_bias,
    proj_in,
    gate_in,
    norm_out_gain,
    norm_out_bias,
    proj_out,
    gate_out,
):
    row = lax.axis_index("row")
    z = lax.axis_index("col")
    x, core = row // 2, row % 2
    place = jnp.where(x == 0, z, 7 - z)

    def device(position, which):
        on_x, on_z = (0, position) if position < 4 else (1, 7 - position)
        return (2 * on_x + which) * 4 + on_z

    up = [(device(p, w), device((p + 1) % 8, w)) for p in range(8) for w in range(2)]
    down = [(target, source) for source, target in up]
    swap = [(device(p, w), device(p, 1 - w)) for p in range(8) for w in range(2)]

    own_mask = pair_mask.astype(jnp.bfloat16)
    sib_mask = lax.ppermute(own_mask, BOTH, swap)
    masks = jnp.where(core == 0, jnp.stack([own_mask, sib_mask]), jnp.stack([sib_mask, own_mask]))

    half = TILE // 2
    ours = core * half
    theirs = half - ours

    def halved(matrix, start, width):
        return (0.5 * lax.dynamic_slice_in_dim(matrix, start, width, axis=1)).T

    enter_weights = jnp.concatenate(
        [halved(m[0], side + ours, half) for m in (proj_in, gate_in) for side in (0, TILE)], axis=0
    )
    middle_weights = jnp.stack(
        [
            jnp.concatenate([halved(m[1], side, TILE) for m in (proj_in, gate_in)], axis=0)
            for side in (0, TILE)
        ]
    )
    identity = jnp.eye(TILE, dtype=jnp.bfloat16)
    both = jnp.concatenate([identity - jnp.bfloat16(1.0 / TILE), identity], axis=0)
    def reordered(values):
        return jnp.concatenate(
            [lax.dynamic_slice_in_dim(values, start, half, axis=0) for start in (ours, theirs)], axis=0
        )

    def columns(values):
        return jnp.broadcast_to(values[:, None], (TILE, TILE))

    gain_in = [columns(norm_in_gain[u]) for u in range(2)]
    bias_in = [columns(norm_in_bias[u]) for u in range(2)]

    def project(held, offset, own, sib, mask, first_block):
        there = lax.rem(place + offset, 8)
        there_x = there // 4
        there_z = jnp.where(there_x == 0, there, 7 - there)
        last = lax.rem(z, 2)
        slot = jnp.where(there_z // 2 == x, lax.rem(there_z, 2), jnp.where(there_z == z, 2, -1))
        at = jnp.stack(
            [
                there_x,
                there_z,
                last,
                (there_x == x).astype(jnp.int32),
                (last == core).astype(jnp.int32),
                jnp.where(slot < 0, -1, 3 * there_x + slot),
            ]
        ).astype(jnp.int32)
        fixed = (both, gain_in[0], bias_in[0], enter_weights)
        return enter(own, sib, first_block, at, mask, *fixed, held)

    def hop(values, pairs):
        return [lax.ppermute(value, BOTH, pairs) for value in values]

    held = project(None, 0, pair_state, lax.ppermute(pair_state, BOTH, swap), masks, 0)
    below = hop([masks, pair_state], up)
    above = hop([masks, pair_state], down)
    part = TILE // 2
    middle_fixed = [
        both[:TILE],
        gain_in[0],
        bias_in[0],
        columns(reordered(norm_out_gain[0])),
        columns(reordered(norm_out_bias[0])),
        0.5 * reordered(proj_out[0]).T,
        0.5 * gate_out[0].T,
        gain_in[1],
        bias_in[1],
        middle_weights,
    ]
    leave_fixed = [
        both[:TILE],
        gain_in[1],
        bias_in[1],
        columns(norm_out_gain[1]),
        columns(norm_out_bias[1]),
        0.5 * proj_out[1].T,
        0.5 * gate_out[1].T,
    ]
    for step in range(1, 4):
        below, above, held, middle_fixed, leave_fixed = lax.optimization_barrier(
            (below, above, held, middle_fixed, leave_fixed)
        )
        now_below, now_above = below, above
        if step < 3:
            below = hop(now_below, up)
            above = hop(now_above, down)
        else:
            below = hop([now_below[0], now_below[1][:part]], up)
            above = hop([now_above[1][part:]], down)
        for offset, (mask, tile) in ((8 - step, now_below), (step, now_above)):
            held = project(held, offset, tile, lax.ppermute(tile, BOTH, swap), mask, 0)
    below, above, held = lax.optimization_barrier((below, above, held))
    held = project(held, 4, below[1], lax.ppermute(below[1], BOTH, swap), below[0], 0)
    held = project(held, 4, above[0], lax.ppermute(above[0], BOTH, swap), below[0], part // (GROUPS * SUB))
    states, *lefts, right, mask = held

    third = jnp.where(z // 2 == x, lax.rem(z, 2), 2)
    at_tri = jnp.stack([core, third]).astype(jnp.int32)
    kept, got = [], []
    for n in range(PARTS):
        if n >= 2:
            at_tri, got[n - 2] = lax.optimization_barrier((at_tri, got[n - 2]))
        stays, leaves = outgoing(at_tri, lefts, right, n)
        kept.append(stays)
        got.append(lax.ppermute(leaves, BOTH, swap))
    parts = kept + got
    at = jnp.stack([core, x, z, third]).astype(jnp.int32)
    pairs, states1 = middle(at, states, mask, middle_fixed, parts)
    kept1, sent1 = incoming(at, pairs)
    got1 = lax.ppermute(sent1, BOTH, swap)
    return leave(at, kept1, got1, states1, *leave_fixed)


def on_device_exchange(
    pair_state,
    pair_mask,
    norm_in_gain,
    norm_in_bias,
    proj_in,
    gate_in,
    norm_out_gain,
    norm_out_bias,
    proj_out,
    gate_out,
):
    mask_weight = pair_mask.astype(jnp.float32)[None]
    current = pair_state
    for update in range(2):
        normed = norm_last(
            current.astype(jnp.float32), norm_in_gain[update], norm_in_bias[update]
        ).astype(jnp.bfloat16)
        projected = jnp.einsum(
            "rcd,de->erc", normed, alternate(proj_in[update]), preferred_element_type=jnp.float32
        )
        gate_logit = jnp.einsum(
            "rcd,de->erc", normed, alternate(gate_in[update]), preferred_element_type=jnp.float32
        )
        paired = (projected * jax.nn.sigmoid(gate_logit) * mask_weight).astype(jnp.bfloat16)
        arrived = spread(paired)
        doubled, total_rows, total_cols = arrived.shape
        pair_count = doubled // 2
        arrived = arrived.reshape(pair_count, 2, total_rows, total_cols)
        left_side = arrived[:, 0]
        right_side = arrived[:, 1]
        pattern = "dik,djk->dij" if update == 0 else "dki,dkj->dij"
        triangle_out = jnp.einsum(
            pattern, left_side, right_side, preferred_element_type=jnp.float32
        ).astype(jnp.bfloat16)
        returned = gather_back(triangle_out)
        normed_out = norm_first(
            returned.astype(jnp.float32), norm_out_gain[update], norm_out_bias[update]
        ).astype(jnp.bfloat16)
        gate_value = jax.nn.sigmoid(
            jnp.einsum("rcd,df->rcf", normed, gate_out[update], preferred_element_type=jnp.float32)
        )
        change = (
            jnp.einsum(
                "erc,ef->rcf", normed_out, proj_out[update], preferred_element_type=jnp.float32
            )
            * gate_value
        )
        current = (current.astype(jnp.float32) + change).astype(jnp.bfloat16)
    return current


def on_device(pair_state, *others):
    square = pair_state.shape == (TILE, TILE, TILE)
    if square and lax.axis_size("row") == 4 and lax.axis_size("col") == 4:
        return on_device_ring(pair_state, *others)
    return on_device_exchange(pair_state, *others)


def solution(mesh):
    return jax.shard_map(
        on_device,
        mesh=mesh,
        in_specs=(
            P(("ens", "row"), "col", None),
            P(("ens", "row"), "col"),
            P(),
            P(),
            P(),
            P(),
            P(),
            P(),
            P(),
            P(),
        ),
        out_specs=P(("ens", "row"), "col", None),
        check_vma=False,
    )
```

```python
import jax
import jax.numpy as jnp
from jax import lax
from jax.experimental import pallas as pl
from jax.experimental.pallas import tpu as pltpu
from jax.sharding import PartitionSpec as P

epsilon = 1e-05


def norm_last(values, norm_gain, norm_bias):
    centre = jnp.mean(values, axis=-1, keepdims=True)
    variance = jnp.mean(jnp.square(values - centre), axis=-1, keepdims=True)
    return (values - centre) * lax.rsqrt(variance + epsilon) * norm_gain + norm_bias


def norm_first(values, norm_gain, norm_bias):
    centre = jnp.mean(values, axis=0, keepdims=True)
    variance = jnp.mean(jnp.square(values - centre), axis=0, keepdims=True)
    return (values - centre) * lax.rsqrt(variance + epsilon) * norm_gain[:, None, None] + norm_bias[
        :, None, None
    ]


def alternate(matrix):
    in_width, out_width = matrix.shape
    half_width = out_width // 2
    return matrix.reshape(in_width, 2, half_width).transpose(0, 2, 1).reshape(in_width, out_width)


def spread(paired):
    arrived = lax.all_to_all(paired, ("row", "col"), split_axis=0, concat_axis=1, tiled=True)
    n_row = lax.axis_size("row")
    n_col = lax.axis_size("col")
    channels, stacked, tile_cols = arrived.shape
    tile_rows = stacked // (n_row * n_col)
    arrived = arrived.reshape(channels, n_row, n_col, tile_rows, tile_cols).transpose(0, 1, 3, 2, 4)
    return arrived.reshape(channels, n_row * tile_rows, n_col * tile_cols)


def gather_back(triangle_out):
    n_row = lax.axis_size("row")
    n_col = lax.axis_size("col")
    channels, total_rows, total_cols = triangle_out.shape
    tile_rows = total_rows // n_row
    tile_cols = total_cols // n_col
    pieces = triangle_out.reshape(channels, n_row, tile_rows, n_col, tile_cols).transpose(
        1, 3, 0, 2, 4
    )
    pieces = pieces.reshape(n_row * n_col * channels, tile_rows, tile_cols)
    return lax.all_to_all(pieces, ("row", "col"), split_axis=0, concat_axis=0, tiled=True)


TILE = 128
SUB = 16
BLOCKS = TILE // SUB
CHUNK = 2
PITCH = SUB + 1
GROUPS = 2
MIDDLE_GROUPS = 4
VMEM_LIMIT = 40 * 1024 * 1024
BOTH = ("row", "col")
NT = (((1,), (1,)), ((), ()))
TN = (((0,), (0,)), ((), ()))


def channels_first(rows, matrix):
    return lax.dot_general(matrix, rows, NT, preferred_element_type=jnp.float32)


def norm_apart(apart, gain, bias):
    variance = jnp.mean(apart * apart, axis=0, keepdims=True)
    wide_gain = jnp.concatenate([gain[...]] * CHUNK, axis=1)
    wide_bias = jnp.concatenate([bias[...]] * CHUNK, axis=1)
    return (apart * lax.rsqrt(variance + epsilon) * wide_gain + wide_bias).astype(jnp.bfloat16)


def norm_channels(values, gain, bias):
    return norm_apart(values - jnp.mean(values, axis=0, keepdims=True), gain, bias)


def product(matrix, values):
    return jnp.dot(matrix, values, preferred_element_type=jnp.float32)


def gated(weights, normed):
    both = product(weights, normed)
    half = both.shape[0] // 2
    return both[:half] * jnp.tanh(both[half:]) + both[:half]


def turn_masked(chunks, mask_rows, turn):
    count = chunks[0].shape[0]
    for r in range(SUB):
        lanes = slice(r % CHUNK * TILE, (r % CHUNK + 1) * TILE)
        turn[pl.ds(r, count, stride=PITCH), :] = chunks[r // CHUNK][:, lanes] * mask_rows[r : r + 1, :]


def chunk_of(turn, first):
    return jnp.concatenate([turn[pl.ds(first + r, TILE, stride=PITCH), :] for r in range(CHUNK)], axis=1)


def rows_of(group):
    return pl.ds(pl.multiple_of(group * SUB, SUB), SUB)


def unturn(turn, places, group):
    for n, (out, d) in enumerate(places):
        out[0, d, rows_of(group), :] = turn[n * PITCH : n * PITCH + SUB, :].astype(jnp.bfloat16)


def enter_kernel(at, own, sib, mask, both, gain, bias, weights, *rest):
    state_out, left_low, left_high, right_out, mask_out, turn = rest[-6:]
    step = pl.program_id(0)
    use_own = (step == 1) == (at[4] == 1)
    mask_out[0, 0] = mask[0]

    def finish(group, paired):
        turn_masked(paired, mask[0, rows_of(group), :].astype(jnp.float32), turn)
        unturn(turn, [(out, d) for out in (left_low, left_high, right_out) for d in range(out.shape[1])], group)

    def turned_chunks(tile, group, matrix):
        rows = tile[rows_of(group)].reshape(SUB * TILE, TILE)
        size = CHUNK * TILE
        return [channels_first(rows[n * size : (n + 1) * size], matrix) for n in range(SUB // CHUNK)]

    @pl.when(use_own)
    def _():
        @pl.loop(0, GROUPS)
        def _(group):
            chunks = turned_chunks(own, group, both[...])
            paired = [gated(weights[...], norm_apart(chunk[:TILE], gain, bias)) for chunk in chunks]
            state_out[group] = jnp.concatenate(
                [chunk[TILE:].astype(jnp.bfloat16) for chunk in chunks], axis=1
            )
            finish(group, paired)

    @pl.when(jnp.logical_not(use_own))
    def _():
        @pl.loop(0, GROUPS)
        def _(group):
            chunks = turned_chunks(sib, group, both[:TILE])
            finish(group, [gated(weights[...], norm_apart(chunk, gain, bias)) for chunk in chunks])


def enter(own, sib, first_block, at, mask, both, gain, bias, weights, held):
    n_block = own.shape[0] // (GROUPS * SUB)
    blocks = TILE // (GROUPS * SUB)
    high = GROUPS * SUB
    full = pl.BlockSpec(memory_space=pl.ANY)

    def core_of(step, at):
        return jnp.where(step == 1, at[2], 1 - at[2])

    def is_own(step, at):
        return (step == 1) == (at[4] == 1)

    def own_map(step, block, at):
        return (jnp.where(is_own(step, at), block, jnp.where(step == 0, 0, n_block - 1)), 0, 0)

    def sib_map(step, block, at):
        return (jnp.where(is_own(step, at), jnp.where(step == 0, 0, n_block - 1), block), 0, 0)

    def mask_map(step, block, at):
        return (core_of(step, at), first_block + block, 0)

    def mask_out_map(step, block, at):
        return (2 * at[0] + core_of(step, at), at[1], first_block + block, 0)

    def state_map(step, block, at):
        kept = jnp.where(is_own(step, at), block, jnp.where(step == 0, 0, n_block - 1))
        return (jnp.where(at[5] < 0, 6 * blocks, at[5] * blocks + first_block + kept), 0, 0)

    def left_map(step, block, at):
        return (at[1], 0, (2 * at[0] + core_of(step, at)) * blocks + first_block + block, 0)

    def right_map(step, block, at):
        slot = jnp.where(at[3] == 1, core_of(step, at), 2)
        return (at[1], 0, slot * blocks + first_block + block, 0)

    half = weights.shape[0] // 4
    same = lambda step, block, at: (0, 0)
    shapes = (
        jax.ShapeDtypeStruct((6 * BLOCKS + GROUPS, TILE, SUB * TILE), jnp.bfloat16),
        jax.ShapeDtypeStruct((4, half // 2, 4 * TILE, TILE), jnp.bfloat16),
        jax.ShapeDtypeStruct((4, half // 2, 4 * TILE, TILE), jnp.bfloat16),
        jax.ShapeDtypeStruct((4, half, 3 * TILE, TILE), jnp.bfloat16),
        jax.ShapeDtypeStruct((4, 4, TILE, TILE), jnp.bfloat16),
    )
    in_specs = [
        pl.BlockSpec((high, TILE, TILE), own_map),
        pl.BlockSpec((high, TILE, TILE), sib_map),
        pl.BlockSpec((1, high, TILE), mask_map),
        pl.BlockSpec((2 * TILE, TILE), same),
        pl.BlockSpec((TILE, TILE), same),
        pl.BlockSpec((TILE, TILE), same),
        pl.BlockSpec((4 * half, TILE), same),
    ]
    operands = [own, sib, mask, both, gain, bias, weights]
    aliases = {}
    if held is not None:
        aliases = {len(operands) + 1 + n: n for n in range(5)}
        operands += list(held)
        in_specs += [full] * 5
    pairs = 2 * own.shape[0] * TILE
    return pl.pallas_call(
        enter_kernel,
        grid_spec=pltpu.PrefetchScalarGridSpec(
            num_scalar_prefetch=1,
            grid=(2, n_block),
            in_specs=in_specs,
            out_specs=[
                pl.BlockSpec((GROUPS, TILE, SUB * TILE), state_map),
                pl.BlockSpec((1, half // 2, high, TILE), left_map),
                pl.BlockSpec((1, half // 2, high, TILE), left_map),
                pl.BlockSpec((1, half, high, TILE), right_map),
                pl.BlockSpec((1, 1, high, TILE), mask_out_map),
            ],
            scratch_shapes=[pltpu.VMEM((2 * half * PITCH, TILE), jnp.float32)],
        ),
        out_shape=shapes,
        input_output_aliases=aliases,
        compiler_params=pltpu.CompilerParams(
            dimension_semantics=("arbitrary", "arbitrary"), vmem_limit_bytes=VMEM_LIMIT
        ),
        cost_estimate=pl.CostEstimate(
            flops=pairs * TILE * 1024, bytes_accessed=pairs * 1024, transcendentals=pairs * TILE
        ),
        name="enter",
    )(at, *operands)


def outgoing_kernel(at, left, right, keep, send):
    core = at[0]
    third = pl.multiple_of(at[1] * TILE, TILE)

    def wide(ref, d, start, count):
        return jnp.concatenate([ref[k, d, pl.ds(start, count), :] for k in range(4)], axis=1)

    blocks = [2 * x + which for which in (core, 1 - core) for x in range(2)]
    for d in range(TOGETHER):
        columns = jnp.concatenate(
            [wide(right, d, 0, 2 * TILE), wide(right, d, third, TILE)], axis=0
        )
        rows = jnp.concatenate(
            [wide(left, d, pl.multiple_of(block * TILE, TILE), TILE) for block in blocks], axis=0
        )
        sums = lax.dot_general(rows, columns, NT, preferred_element_type=jnp.float32)
        for slot in range(3):
            lanes = slice(slot * TILE, (slot + 1) * TILE)
            keep[slot, d] = sums[: 2 * TILE, lanes].astype(jnp.bfloat16)
            send[slot, d] = sums[2 * TILE :, lanes].astype(jnp.bfloat16)


TOGETHER = 4
PARTS = 2


def outgoing(at, lefts, right, part):
    count = right.shape[1] // PARTS
    steps = count // TOGETHER
    first = part * steps
    left = lefts[part * len(lefts) // PARTS]
    left_first = part % (PARTS // len(lefts)) * steps
    out = jax.ShapeDtypeStruct((3, count, 2 * TILE, TILE), jnp.bfloat16)
    return pl.pallas_call(
        outgoing_kernel,
        grid_spec=pltpu.PrefetchScalarGridSpec(
            num_scalar_prefetch=1,
            grid=(steps,),
            in_specs=[
                pl.BlockSpec((4, TOGETHER, 4 * TILE, TILE), lambda d, at: (0, left_first + d, 0, 0)),
                pl.BlockSpec((4, TOGETHER, 3 * TILE, TILE), lambda d, at: (0, first + d, 0, 0)),
            ],
            out_specs=[pl.BlockSpec((3, TOGETHER, 2 * TILE, TILE), lambda d, at: (0, d, 0, 0))] * 2,
        ),
        out_shape=(out, out),
        compiler_params=pltpu.CompilerParams(
            dimension_semantics=("arbitrary",), vmem_limit_bytes=VMEM_LIMIT
        ),
        cost_estimate=pl.CostEstimate(
            flops=count * 512 * 384 * 1024, bytes_accessed=count * 1300 * 1024, transcendentals=0
        ),
        name="outgoing",
    )(at, left, right)


def middle_kernel(
    at, state, mask, gain0, bias0, gain_out, bias_out, proj, gate, gain1, bias1, weights, *rest
):
    parts, (pairs_out, state_out, turn, turn_out) = rest[:-4], rest[-4:]

    @pl.loop(0, MIDDLE_GROUPS)
    def _(group):
        for n, (part, d) in enumerate((part, d) for part in parts for d in range(part.shape[1])):
            turn[n * PITCH : n * PITCH + SUB, :] = part[0, d, rows_of(group), :].astype(jnp.float32)
        changed, paired = [], []
        for first in range(0, SUB, CHUNK):
            before = state[group, :, first * TILE : (first + CHUNK) * TILE].astype(jnp.float32)
            gate_value = jnp.tanh(product(gate[...], norm_channels(before, gain0, bias0)))
            out = product(proj[...], norm_channels(chunk_of(turn, first), gain_out, bias_out))
            changed.append((before + (out * gate_value + out)).astype(jnp.bfloat16))
            normed1 = norm_channels(changed[-1].astype(jnp.float32), gain1, bias1)
            paired.append(gated(weights[0], normed1))
        state_out[group] = jnp.concatenate(changed, axis=1)
        turn_masked(paired, mask[0, 0, rows_of(group), :].astype(jnp.float32), turn_out)
        unturn(turn_out, [(pairs_out, d) for d in range(TILE)], group)


def middle(at, states, mask, fixed, parts):
    def column(slot, at):
        return jnp.where(slot == 2, at[2], 2 * at[1] + slot)

    blocks = BLOCKS // MIDDLE_GROUPS
    high = MIDDLE_GROUPS * SUB
    square = pl.BlockSpec((TILE, TILE), lambda slot, x, block, at: (0, 0))
    tri = pl.BlockSpec(
        (1, parts[0].shape[1], high, TILE), lambda slot, x, block, at: (slot, 0, x * blocks + block, 0)
    )
    state_spec = pl.BlockSpec(
        (MIDDLE_GROUPS, TILE, SUB * TILE),
        lambda slot, x, block, at: ((x * 3 + jnp.where(slot == 2, at[3], slot)) * blocks + block, 0, 0),
    )
    pairs = 6 * TILE * TILE
    return pl.pallas_call(
        middle_kernel,
        grid_spec=pltpu.PrefetchScalarGridSpec(
            num_scalar_prefetch=1,
            grid=(3, 2, blocks),
            in_specs=[
                state_spec,
                pl.BlockSpec(
                    (1, 1, high, TILE),
                    lambda slot, x, block, at: (2 * x + at[0], column(slot, at), block, 0),
                ),
            ]
            + [square] * 8
            + [
                pl.BlockSpec(
                    (1, 2 * TILE, TILE),
                    lambda slot, x, block, at: (jnp.where(slot == 2, 1, 0), 0, 0),
                )
            ]
            + [tri] * len(parts),
            out_specs=[
                pl.BlockSpec(
                    (1, TILE, high, TILE), lambda slot, x, block, at: (slot, 0, x * blocks + block, 0)
                ),
                pl.BlockSpec(
                    (MIDDLE_GROUPS, TILE, SUB * TILE),
                    lambda slot, x, block, at: (
                        jnp.where(slot == 2, x * blocks + block, 2 * blocks), 0, 0,
                    ),
                ),
            ],
            scratch_shapes=[pltpu.VMEM((TILE * PITCH, TILE), jnp.float32)] * 2,
        ),
        out_shape=(
            jax.ShapeDtypeStruct((3, TILE, 2 * TILE, TILE), jnp.bfloat16),
            jax.ShapeDtypeStruct((2 * BLOCKS + MIDDLE_GROUPS, TILE, SUB * TILE), jnp.bfloat16),
        ),
        compiler_params=pltpu.CompilerParams(
            dimension_semantics=("arbitrary",) * 3, vmem_limit_bytes=VMEM_LIMIT
        ),
        cost_estimate=pl.CostEstimate(
            flops=pairs * TILE * 1024, bytes_accessed=pairs * 1024, transcendentals=pairs * TILE * 2
        ),
        name="middle",
    )(at, states, mask, *fixed, *parts)


CHANNELS = 16


def incoming_kernel(at, pairs, keep, send):
    core = at[0]
    for d in range(CHANNELS):
        right = pairs[2, d]
        keep[d] = lax.dot_general(
            pairs[core, d], right, TN, preferred_element_type=jnp.float32
        ).astype(jnp.bfloat16)
        send[d] = lax.dot_general(
            pairs[1 - core, d], right, TN, preferred_element_type=jnp.float32
        ).astype(jnp.bfloat16)


def incoming(at, pairs):
    out_spec = pl.BlockSpec((CHANNELS, TILE, TILE), lambda d, at: (d, 0, 0))
    return pl.pallas_call(
        incoming_kernel,
        grid_spec=pltpu.PrefetchScalarGridSpec(
            num_scalar_prefetch=1,
            grid=(TILE // CHANNELS,),
            in_specs=[pl.BlockSpec((3, CHANNELS, 2 * TILE, TILE), lambda d, at: (0, d, 0, 0))],
            out_specs=[out_spec, out_spec],
        ),
        out_shape=(
            jax.ShapeDtypeStruct((TILE, TILE, TILE), jnp.bfloat16),
            jax.ShapeDtypeStruct((TILE, TILE, TILE), jnp.bfloat16),
        ),
        compiler_params=pltpu.CompilerParams(
            dimension_semantics=("arbitrary",), vmem_limit_bytes=VMEM_LIMIT
        ),
        cost_estimate=pl.CostEstimate(
            flops=TILE * 512 * 256 * TILE, bytes_accessed=36 * 2**20, transcendentals=0
        ),
        name="incoming",
    )(at, pairs)


def leave_kernel(at, kept, got, state, gain1, bias1, gain_out, bias_out, proj, gate, result, turn):
    @pl.loop(0, GROUPS)
    def _(group):
        for d in range(TILE):
            turn[d * PITCH : d * PITCH + SUB, :] = kept[d, rows_of(group), :].astype(jnp.float32) + got[
                d, rows_of(group), :
            ].astype(jnp.float32)
        changed = []
        for first in range(0, SUB, CHUNK):
            before = state[group, :, first * TILE : (first + CHUNK) * TILE].astype(jnp.float32)
            gate_value = jnp.tanh(product(gate[...], norm_channels(before, gain1, bias1)))
            out = product(proj[...], norm_channels(chunk_of(turn, first), gain_out, bias_out))
            changed.append((before + (out * gate_value + out)).astype(jnp.bfloat16))
        result[rows_of(group)] = jnp.concatenate([chunk.T for chunk in changed], axis=0).reshape(
            SUB, TILE, TILE
        )


def leave(at, kept, got, states, *fixed):
    blocks = BLOCKS // GROUPS
    square = pl.BlockSpec((TILE, TILE), lambda block, at: (0, 0))
    tri = pl.BlockSpec((TILE, GROUPS * SUB, TILE), lambda block, at: (0, block, 0))
    return pl.pallas_call(
        leave_kernel,
        grid_spec=pltpu.PrefetchScalarGridSpec(
            num_scalar_prefetch=1,
            grid=(blocks,),
            in_specs=[
                tri,
                tri,
                pl.BlockSpec((GROUPS, TILE, SUB * TILE), lambda block, at: (at[1] * blocks + block, 0, 0)),
            ]
            + [square] * 6,
            out_specs=pl.BlockSpec((GROUPS * SUB, TILE, TILE), lambda block, at: (block, 0, 0)),
            scratch_shapes=[pltpu.VMEM((TILE * PITCH, TILE), jnp.float32)],
        ),
        out_shape=jax.ShapeDtypeStruct((TILE, TILE, TILE), jnp.bfloat16),
        compiler_params=pltpu.CompilerParams(
            dimension_semantics=("arbitrary",), vmem_limit_bytes=VMEM_LIMIT
        ),
        cost_estimate=pl.CostEstimate(
            flops=TILE**3 * 512, bytes_accessed=20 * 2**20, transcendentals=TILE**3
        ),
        name="leave",
    )(at, kept, got, states, *fixed)


def on_device_ring(
    pair_state,
    pair_mask,
    norm_in_gain,
    norm_in_bias,
    proj_in,
    gate_in,
    norm_out_gain,
    norm_out_bias,
    proj_out,
    gate_out,
):
    row = lax.axis_index("row")
    z = lax.axis_index("col")
    x, core = row // 2, row % 2
    place = jnp.where(x == 0, z, 7 - z)

    def device(position, which):
        on_x, on_z = (0, position) if position < 4 else (1, 7 - position)
        return (2 * on_x + which) * 4 + on_z

    up = [(device(p, w), device((p + 1) % 8, w)) for p in range(8) for w in range(2)]
    down = [(target, source) for source, target in up]
    swap = [(device(p, w), device(p, 1 - w)) for p in range(8) for w in range(2)]

    own_mask = pair_mask.astype(jnp.bfloat16)
    sib_mask = lax.ppermute(own_mask, BOTH, swap)
    masks = jnp.where(core == 0, jnp.stack([own_mask, sib_mask]), jnp.stack([sib_mask, own_mask]))

    half = TILE // 2
    ours = core * half
    theirs = half - ours

    def halved(matrix, start, width):
        return (0.5 * lax.dynamic_slice_in_dim(matrix, start, width, axis=1)).T

    enter_weights = jnp.concatenate(
        [halved(m[0], side + ours, half) for m in (proj_in, gate_in) for side in (0, TILE)], axis=0
    )
    middle_weights = jnp.stack(
        [
            jnp.concatenate([halved(m[1], side, TILE) for m in (proj_in, gate_in)], axis=0)
            for side in (0, TILE)
        ]
    )
    identity = jnp.eye(TILE, dtype=jnp.bfloat16)
    both = jnp.concatenate([identity - jnp.bfloat16(1.0 / TILE), identity], axis=0)
    def reordered(values):
        return jnp.concatenate(
            [lax.dynamic_slice_in_dim(values, start, half, axis=0) for start in (ours, theirs)], axis=0
        )

    def columns(values):
        return jnp.broadcast_to(values[:, None], (TILE, TILE))

    gain_in = [columns(norm_in_gain[u]) for u in range(2)]
    bias_in = [columns(norm_in_bias[u]) for u in range(2)]

    def project(held, offset, own, sib, mask, first_block):
        there = lax.rem(place + offset, 8)
        there_x = there // 4
        there_z = jnp.where(there_x == 0, there, 7 - there)
        last = lax.rem(z, 2)
        slot = jnp.where(there_z // 2 == x, lax.rem(there_z, 2), jnp.where(there_z == z, 2, -1))
        at = jnp.stack(
            [
                there_x,
                there_z,
                last,
                (there_x == x).astype(jnp.int32),
                (last == core).astype(jnp.int32),
                jnp.where(slot < 0, -1, 3 * there_x + slot),
            ]
        ).astype(jnp.int32)
        fixed = (both, gain_in[0], bias_in[0], enter_weights)
        return enter(own, sib, first_block, at, mask, *fixed, held)

    def hop(values, pairs):
        return [lax.ppermute(value, BOTH, pairs) for value in values]

    held = project(None, 0, pair_state, lax.ppermute(pair_state, BOTH, swap), masks, 0)
    below = hop([masks, pair_state], up)
    above = hop([masks, pair_state], down)
    part = TILE // 2
    middle_fixed = [
        gain_in[0],
        bias_in[0],
        columns(reordered(norm_out_gain[0])),
        columns(reordered(norm_out_bias[0])),
        0.5 * reordered(proj_out[0]).T,
        0.5 * gate_out[0].T,
        gain_in[1],
        bias_in[1],
        middle_weights,
    ]
    leave_fixed = [
        gain_in[1],
        bias_in[1],
        columns(norm_out_gain[1]),
        columns(norm_out_bias[1]),
        0.5 * proj_out[1].T,
        0.5 * gate_out[1].T,
    ]
    for step in range(1, 4):
        below, above, held, middle_fixed, leave_fixed = lax.optimization_barrier(
            (below, above, held, middle_fixed, leave_fixed)
        )
        now_below, now_above = below, above
        if step < 3:
            below = hop(now_below, up)
            above = hop(now_above, down)
        else:
            below = hop([now_below[0], now_below[1][:part]], up)
            above = hop([now_above[1][part:]], down)
        for offset, (mask, tile) in ((8 - step, now_below), (step, now_above)):
            held = project(held, offset, tile, lax.ppermute(tile, BOTH, swap), mask, 0)
    below, above, held = lax.optimization_barrier((below, above, held))
    held = project(held, 4, below[1], lax.ppermute(below[1], BOTH, swap), below[0], 0)
    held = project(held, 4, above[0], lax.ppermute(above[0], BOTH, swap), below[0], part // (GROUPS * SUB))
    states, *lefts, right, mask = held

    third = jnp.where(z // 2 == x, lax.rem(z, 2), 2)
    at_tri = jnp.stack([core, third]).astype(jnp.int32)
    kept, got = [], []
    for n in range(PARTS):
        if n >= 2:
            at_tri, got[n - 2] = lax.optimization_barrier((at_tri, got[n - 2]))
        stays, leaves = outgoing(at_tri, lefts, right, n)
        kept.append(stays)
        got.append(lax.ppermute(leaves, BOTH, swap))
    parts = kept + got
    at = jnp.stack([core, x, z, third]).astype(jnp.int32)
    pairs, states1 = middle(at, states, mask, middle_fixed, parts)
    kept1, sent1 = incoming(at, pairs)
    got1 = lax.ppermute(sent1, BOTH, swap)
    return leave(at, kept1, got1, states1, *leave_fixed)


def on_device_exchange(
    pair_state,
    pair_mask,
    norm_in_gain,
    norm_in_bias,
    proj_in,
    gate_in,
    norm_out_gain,
    norm_out_bias,
    proj_out,
    gate_out,
):
    mask_weight = pair_mask.astype(jnp.float32)[None]
    current = pair_state
    for update in range(2):
        normed = norm_last(
            current.astype(jnp.float32), norm_in_gain[update], norm_in_bias[update]
        ).astype(jnp.bfloat16)
        projected = jnp.einsum(
            "rcd,de->erc", normed, alternate(proj_in[update]), preferred_element_type=jnp.float32
        )
        gate_logit = jnp.einsum(
            "rcd,de->erc", normed, alternate(gate_in[update]), preferred_element_type=jnp.float32
        )
        paired = (projected * jax.nn.sigmoid(gate_logit) * mask_weight).astype(jnp.bfloat16)
        arrived = spread(paired)
        doubled, total_rows, total_cols = arrived.shape
        pair_count = doubled // 2
        arrived = arrived.reshape(pair_count, 2, total_rows, total_cols)
        left_side = arrived[:, 0]
        right_side = arrived[:, 1]
        pattern = "dik,djk->dij" if update == 0 else "dki,dkj->dij"
        triangle_out = jnp.einsum(
            pattern, left_side, right_side, preferred_element_type=jnp.float32
        ).astype(jnp.bfloat16)
        returned = gather_back(triangle_out)
        normed_out = norm_first(
            returned.astype(jnp.float32), norm_out_gain[update], norm_out_bias[update]
        ).astype(jnp.bfloat16)
        gate_value = jax.nn.sigmoid(
            jnp.einsum("rcd,df->rcf", normed, gate_out[update], preferred_element_type=jnp.float32)
        )
        change = (
            jnp.einsum(
                "erc,ef->rcf", normed_out, proj_out[update], preferred_element_type=jnp.float32
            )
            * gate_value
        )
        current = (current.astype(jnp.float32) + change).astype(jnp.bfloat16)
    return current


def on_device(pair_state, *others):
    square = pair_state.shape == (TILE, TILE, TILE)
    if square and lax.axis_size("row") == 4 and lax.axis_size("col") == 4:
        return on_device_ring(pair_state, *others)
    return on_device_exchange(pair_state, *others)


def solution(mesh):
    return jax.shard_map(
        on_device,
        mesh=mesh,
        in_specs=(
            P(("ens", "row"), "col", None),
            P(("ens", "row"), "col"),
            P(),
            P(),
            P(),
            P(),
            P(),
            P(),
            P(),
            P(),
        ),
        out_specs=P(("ens", "row"), "col", None),
        check_vma=False,
    )
```

```python
import jax
import jax.numpy as jnp
from jax import lax
from jax.experimental import pallas as pl
from jax.experimental.pallas import tpu as pltpu
from jax.sharding import PartitionSpec as P

epsilon = 1e-05


def norm_last(values, norm_gain, norm_bias):
    centre = jnp.mean(values, axis=-1, keepdims=True)
    variance = jnp.mean(jnp.square(values - centre), axis=-1, keepdims=True)
    return (values - centre) * lax.rsqrt(variance + epsilon) * norm_gain + norm_bias


def norm_first(values, norm_gain, norm_bias):
    centre = jnp.mean(values, axis=0, keepdims=True)
    variance = jnp.mean(jnp.square(values - centre), axis=0, keepdims=True)
    return (values - centre) * lax.rsqrt(variance + epsilon) * norm_gain[:, None, None] + norm_bias[
        :, None, None
    ]


def alternate(matrix):
    in_width, out_width = matrix.shape
    half_width = out_width // 2
    return matrix.reshape(in_width, 2, half_width).transpose(0, 2, 1).reshape(in_width, out_width)


def spread(paired):
    arrived = lax.all_to_all(paired, ("row", "col"), split_axis=0, concat_axis=1, tiled=True)
    n_row = lax.axis_size("row")
    n_col = lax.axis_size("col")
    channels, stacked, tile_cols = arrived.shape
    tile_rows = stacked // (n_row * n_col)
    arrived = arrived.reshape(channels, n_row, n_col, tile_rows, tile_cols).transpose(0, 1, 3, 2, 4)
    return arrived.reshape(channels, n_row * tile_rows, n_col * tile_cols)


def gather_back(triangle_out):
    n_row = lax.axis_size("row")
    n_col = lax.axis_size("col")
    channels, total_rows, total_cols = triangle_out.shape
    tile_rows = total_rows // n_row
    tile_cols = total_cols // n_col
    pieces = triangle_out.reshape(channels, n_row, tile_rows, n_col, tile_cols).transpose(
        1, 3, 0, 2, 4
    )
    pieces = pieces.reshape(n_row * n_col * channels, tile_rows, tile_cols)
    return lax.all_to_all(pieces, ("row", "col"), split_axis=0, concat_axis=0, tiled=True)


TILE = 128
SUB = 16
BLOCKS = TILE // SUB
CHUNK = 1
PITCH = SUB + 1
GROUPS = 2
MIDDLE_GROUPS = 4
VMEM_LIMIT = 40 * 1024 * 1024
BOTH = ("row", "col")
NT = (((1,), (1,)), ((), ()))
TN = (((0,), (0,)), ((), ()))


def channels_first(rows, matrix):
    return lax.dot_general(matrix, rows, NT, preferred_element_type=jnp.float32)


def norm_apart(apart, gain, bias):
    variance = jnp.mean(apart * apart, axis=0, keepdims=True)
    wide_gain = jnp.concatenate([gain[...]] * CHUNK, axis=1)
    wide_bias = jnp.concatenate([bias[...]] * CHUNK, axis=1)
    return (apart * lax.rsqrt(variance + epsilon) * wide_gain + wide_bias).astype(jnp.bfloat16)


def norm_channels(values, gain, bias):
    return norm_apart(values - jnp.mean(values, axis=0, keepdims=True), gain, bias)


def product(matrix, values):
    return jnp.dot(matrix, values, preferred_element_type=jnp.float32)


def gated(weights, normed):
    both = product(weights, normed)
    half = both.shape[0] // 2
    return both[:half] * jnp.tanh(both[half:]) + both[:half]


def turn_masked(chunks, mask_rows, turn):
    count = chunks[0].shape[0]
    for r in range(SUB):
        lanes = slice(r % CHUNK * TILE, (r % CHUNK + 1) * TILE)
        turn[pl.ds(r, count, stride=PITCH), :] = chunks[r // CHUNK][:, lanes] * mask_rows[r : r + 1, :]


def chunk_of(turn, first):
    return jnp.concatenate([turn[pl.ds(first + r, TILE, stride=PITCH), :] for r in range(CHUNK)], axis=1)


def rows_of(group):
    return pl.ds(pl.multiple_of(group * SUB, SUB), SUB)


def unturn(turn, places, group):
    for n, (out, d) in enumerate(places):
        out[0, d, rows_of(group), :] = turn[n * PITCH : n * PITCH + SUB, :].astype(jnp.bfloat16)


def enter_kernel(at, own, sib, mask, both, gain, bias, weights, *rest):
    state_out, left_low, left_high, right_out, mask_out, turn = rest[-6:]
    step = pl.program_id(0)
    use_own = (step == 1) == (at[4] == 1)
    mask_out[0, 0] = mask[0]

    def finish(group, paired):
        turn_masked(paired, mask[0, rows_of(group), :].astype(jnp.float32), turn)
        unturn(turn, [(out, d) for out in (left_low, left_high, right_out) for d in range(out.shape[1])], group)

    def turned_chunks(tile, group, matrix):
        rows = tile[rows_of(group)].reshape(SUB * TILE, TILE)
        size = CHUNK * TILE
        return [channels_first(rows[n * size : (n + 1) * size], matrix) for n in range(SUB // CHUNK)]

    @pl.when(use_own)
    def _():
        @pl.loop(0, GROUPS)
        def _(group):
            chunks = turned_chunks(own, group, both[...])
            paired = [gated(weights[...], norm_apart(chunk[:TILE], gain, bias)) for chunk in chunks]
            state_out[group] = jnp.concatenate(
                [chunk[TILE:].astype(jnp.bfloat16) for chunk in chunks], axis=1
            )
            finish(group, paired)

    @pl.when(jnp.logical_not(use_own))
    def _():
        @pl.loop(0, GROUPS)
        def _(group):
            chunks = turned_chunks(sib, group, both[:TILE])
            finish(group, [gated(weights[...], norm_apart(chunk, gain, bias)) for chunk in chunks])


def enter(own, sib, first_block, at, mask, both, gain, bias, weights, held):
    n_block = own.shape[0] // (GROUPS * SUB)
    blocks = TILE // (GROUPS * SUB)
    high = GROUPS * SUB
    full = pl.BlockSpec(memory_space=pl.ANY)

    def core_of(step, at):
        return jnp.where(step == 1, at[2], 1 - at[2])

    def is_own(step, at):
        return (step == 1) == (at[4] == 1)

    def own_map(step, block, at):
        return (jnp.where(is_own(step, at), block, jnp.where(step == 0, 0, n_block - 1)), 0, 0)

    def sib_map(step, block, at):
        return (jnp.where(is_own(step, at), jnp.where(step == 0, 0, n_block - 1), block), 0, 0)

    def mask_map(step, block, at):
        return (core_of(step, at), first_block + block, 0)

    def mask_out_map(step, block, at):
        return (2 * at[0] + core_of(step, at), at[1], first_block + block, 0)

    def state_map(step, block, at):
        kept = jnp.where(is_own(step, at), block, jnp.where(step == 0, 0, n_block - 1))
        return (jnp.where(at[5] < 0, 6 * blocks, at[5] * blocks + first_block + kept), 0, 0)

    def left_map(step, block, at):
        return (at[1], 0, (2 * at[0] + core_of(step, at)) * blocks + first_block + block, 0)

    def right_map(step, block, at):
        slot = jnp.where(at[3] == 1, core_of(step, at), 2)
        return (at[1], 0, slot * blocks + first_block + block, 0)

    half = weights.shape[0] // 4
    same = lambda step, block, at: (0, 0)
    shapes = (
        jax.ShapeDtypeStruct((6 * BLOCKS + GROUPS, TILE, SUB * TILE), jnp.bfloat16),
        jax.ShapeDtypeStruct((4, half // 2, 4 * TILE, TILE), jnp.bfloat16),
        jax.ShapeDtypeStruct((4, half // 2, 4 * TILE, TILE), jnp.bfloat16),
        jax.ShapeDtypeStruct((4, half, 3 * TILE, TILE), jnp.bfloat16),
        jax.ShapeDtypeStruct((4, 4, TILE, TILE), jnp.bfloat16),
    )
    in_specs = [
        pl.BlockSpec((high, TILE, TILE), own_map),
        pl.BlockSpec((high, TILE, TILE), sib_map),
        pl.BlockSpec((1, high, TILE), mask_map),
        pl.BlockSpec((2 * TILE, TILE), same),
        pl.BlockSpec((TILE, TILE), same),
        pl.BlockSpec((TILE, TILE), same),
        pl.BlockSpec((4 * half, TILE), same),
    ]
    operands = [own, sib, mask, both, gain, bias, weights]
    aliases = {}
    if held is not None:
        aliases = {len(operands) + 1 + n: n for n in range(5)}
        operands += list(held)
        in_specs += [full] * 5
    pairs = 2 * own.shape[0] * TILE
    return pl.pallas_call(
        enter_kernel,
        grid_spec=pltpu.PrefetchScalarGridSpec(
            num_scalar_prefetch=1,
            grid=(2, n_block),
            in_specs=in_specs,
            out_specs=[
                pl.BlockSpec((GROUPS, TILE, SUB * TILE), state_map),
                pl.BlockSpec((1, half // 2, high, TILE), left_map),
                pl.BlockSpec((1, half // 2, high, TILE), left_map),
                pl.BlockSpec((1, half, high, TILE), right_map),
                pl.BlockSpec((1, 1, high, TILE), mask_out_map),
            ],
            scratch_shapes=[pltpu.VMEM((2 * half * PITCH, TILE), jnp.float32)],
        ),
        out_shape=shapes,
        input_output_aliases=aliases,
        compiler_params=pltpu.CompilerParams(
            dimension_semantics=("arbitrary", "arbitrary"), vmem_limit_bytes=VMEM_LIMIT
        ),
        cost_estimate=pl.CostEstimate(
            flops=pairs * TILE * 1024, bytes_accessed=pairs * 1024, transcendentals=pairs * TILE
        ),
        name="enter",
    )(at, *operands)


def outgoing_kernel(at, left, right, keep, send):
    core = at[0]
    third = pl.multiple_of(at[1] * TILE, TILE)

    def wide(ref, d, start, count):
        return jnp.concatenate([ref[k, d, pl.ds(start, count), :] for k in range(4)], axis=1)

    blocks = [2 * x + which for which in (core, 1 - core) for x in range(2)]
    for d in range(TOGETHER):
        columns = jnp.concatenate(
            [wide(right, d, 0, 2 * TILE), wide(right, d, third, TILE)], axis=0
        )
        rows = jnp.concatenate(
            [wide(left, d, pl.multiple_of(block * TILE, TILE), TILE) for block in blocks], axis=0
        )
        sums = lax.dot_general(rows, columns, NT, preferred_element_type=jnp.float32)
        for slot in range(3):
            lanes = slice(slot * TILE, (slot + 1) * TILE)
            keep[slot, d] = sums[: 2 * TILE, lanes].astype(jnp.bfloat16)
            send[slot, d] = sums[2 * TILE :, lanes].astype(jnp.bfloat16)


TOGETHER = 4
PARTS = 2


def outgoing(at, lefts, right, part):
    count = right.shape[1] // PARTS
    steps = count // TOGETHER
    first = part * steps
    left = lefts[part * len(lefts) // PARTS]
    left_first = part % (PARTS // len(lefts)) * steps
    out = jax.ShapeDtypeStruct((3, count, 2 * TILE, TILE), jnp.bfloat16)
    return pl.pallas_call(
        outgoing_kernel,
        grid_spec=pltpu.PrefetchScalarGridSpec(
            num_scalar_prefetch=1,
            grid=(steps,),
            in_specs=[
                pl.BlockSpec((4, TOGETHER, 4 * TILE, TILE), lambda d, at: (0, left_first + d, 0, 0)),
                pl.BlockSpec((4, TOGETHER, 3 * TILE, TILE), lambda d, at: (0, first + d, 0, 0)),
            ],
            out_specs=[pl.BlockSpec((3, TOGETHER, 2 * TILE, TILE), lambda d, at: (0, d, 0, 0))] * 2,
        ),
        out_shape=(out, out),
        compiler_params=pltpu.CompilerParams(
            dimension_semantics=("arbitrary",), vmem_limit_bytes=VMEM_LIMIT
        ),
        cost_estimate=pl.CostEstimate(
            flops=count * 512 * 384 * 1024, bytes_accessed=count * 1300 * 1024, transcendentals=0
        ),
        name="outgoing",
    )(at, left, right)


def middle_kernel(
    at, state, mask, gain0, bias0, gain_out, bias_out, proj, gate, gain1, bias1, weights, *rest
):
    parts, (pairs_out, state_out, turn, turn_out) = rest[:-4], rest[-4:]

    @pl.loop(0, MIDDLE_GROUPS)
    def _(group):
        for n, (part, d) in enumerate((part, d) for part in parts for d in range(part.shape[1])):
            turn[n * PITCH : n * PITCH + SUB, :] = part[0, d, rows_of(group), :].astype(jnp.float32)
        changed, paired = [], []
        for first in range(0, SUB, CHUNK):
            before = state[group, :, first * TILE : (first + CHUNK) * TILE].astype(jnp.float32)
            gate_value = jnp.tanh(product(gate[...], norm_channels(before, gain0, bias0)))
            out = product(proj[...], norm_channels(chunk_of(turn, first), gain_out, bias_out))
            changed.append((before + (out * gate_value + out)).astype(jnp.bfloat16))
            normed1 = norm_channels(changed[-1].astype(jnp.float32), gain1, bias1)
            paired.append(gated(weights[0], normed1))
        state_out[group] = jnp.concatenate(changed, axis=1)
        turn_masked(paired, mask[0, 0, rows_of(group), :].astype(jnp.float32), turn_out)
        unturn(turn_out, [(pairs_out, d) for d in range(TILE)], group)


def middle(at, states, mask, fixed, parts):
    def column(slot, at):
        return jnp.where(slot == 2, at[2], 2 * at[1] + slot)

    blocks = BLOCKS // MIDDLE_GROUPS
    high = MIDDLE_GROUPS * SUB
    square = pl.BlockSpec((TILE, TILE), lambda slot, x, block, at: (0, 0))
    tri = pl.BlockSpec(
        (1, parts[0].shape[1], high, TILE), lambda slot, x, block, at: (slot, 0, x * blocks + block, 0)
    )
    state_spec = pl.BlockSpec(
        (MIDDLE_GROUPS, TILE, SUB * TILE),
        lambda slot, x, block, at: ((x * 3 + jnp.where(slot == 2, at[3], slot)) * blocks + block, 0, 0),
    )
    pairs = 6 * TILE * TILE
    return pl.pallas_call(
        middle_kernel,
        grid_spec=pltpu.PrefetchScalarGridSpec(
            num_scalar_prefetch=1,
            grid=(3, 2, blocks),
            in_specs=[
                state_spec,
                pl.BlockSpec(
                    (1, 1, high, TILE),
                    lambda slot, x, block, at: (2 * x + at[0], column(slot, at), block, 0),
                ),
            ]
            + [square] * 8
            + [
                pl.BlockSpec(
                    (1, 2 * TILE, TILE),
                    lambda slot, x, block, at: (jnp.where(slot == 2, 1, 0), 0, 0),
                )
            ]
            + [tri] * len(parts),
            out_specs=[
                pl.BlockSpec(
                    (1, TILE, high, TILE), lambda slot, x, block, at: (slot, 0, x * blocks + block, 0)
                ),
                pl.BlockSpec(
                    (MIDDLE_GROUPS, TILE, SUB * TILE),
                    lambda slot, x, block, at: (
                        jnp.where(slot == 2, x * blocks + block, 2 * blocks), 0, 0,
                    ),
                ),
            ],
            scratch_shapes=[pltpu.VMEM((TILE * PITCH, TILE), jnp.float32)] * 2,
        ),
        out_shape=(
            jax.ShapeDtypeStruct((3, TILE, 2 * TILE, TILE), jnp.bfloat16),
            jax.ShapeDtypeStruct((2 * BLOCKS + MIDDLE_GROUPS, TILE, SUB * TILE), jnp.bfloat16),
        ),
        compiler_params=pltpu.CompilerParams(
            dimension_semantics=("arbitrary",) * 3, vmem_limit_bytes=VMEM_LIMIT
        ),
        cost_estimate=pl.CostEstimate(
            flops=pairs * TILE * 1024, bytes_accessed=pairs * 1024, transcendentals=pairs * TILE * 2
        ),
        name="middle",
    )(at, states, mask, *fixed, *parts)


CHANNELS = 16


def incoming_kernel(at, pairs, keep, send):
    core = at[0]
    for d in range(CHANNELS):
        right = pairs[2, d]
        keep[d] = lax.dot_general(
            pairs[core, d], right, TN, preferred_element_type=jnp.float32
        ).astype(jnp.bfloat16)
        send[d] = lax.dot_general(
            pairs[1 - core, d], right, TN, preferred_element_type=jnp.float32
        ).astype(jnp.bfloat16)


def incoming(at, pairs):
    out_spec = pl.BlockSpec((CHANNELS, TILE, TILE), lambda d, at: (d, 0, 0))
    return pl.pallas_call(
        incoming_kernel,
        grid_spec=pltpu.PrefetchScalarGridSpec(
            num_scalar_prefetch=1,
            grid=(TILE // CHANNELS,),
            in_specs=[pl.BlockSpec((3, CHANNELS, 2 * TILE, TILE), lambda d, at: (0, d, 0, 0))],
            out_specs=[out_spec, out_spec],
        ),
        out_shape=(
            jax.ShapeDtypeStruct((TILE, TILE, TILE), jnp.bfloat16),
            jax.ShapeDtypeStruct((TILE, TILE, TILE), jnp.bfloat16),
        ),
        compiler_params=pltpu.CompilerParams(
            dimension_semantics=("arbitrary",), vmem_limit_bytes=VMEM_LIMIT
        ),
        cost_estimate=pl.CostEstimate(
            flops=TILE * 512 * 256 * TILE, bytes_accessed=36 * 2**20, transcendentals=0
        ),
        name="incoming",
    )(at, pairs)


def leave_kernel(at, kept, got, state, gain1, bias1, gain_out, bias_out, proj, gate, result, turn):
    @pl.loop(0, GROUPS)
    def _(group):
        for d in range(TILE):
            turn[d * PITCH : d * PITCH + SUB, :] = kept[d, rows_of(group), :].astype(jnp.float32) + got[
                d, rows_of(group), :
            ].astype(jnp.float32)
        changed = []
        for first in range(0, SUB, CHUNK):
            before = state[group, :, first * TILE : (first + CHUNK) * TILE].astype(jnp.float32)
            gate_value = jnp.tanh(product(gate[...], norm_channels(before, gain1, bias1)))
            out = product(proj[...], norm_channels(chunk_of(turn, first), gain_out, bias_out))
            changed.append((before + (out * gate_value + out)).astype(jnp.bfloat16))
        result[rows_of(group)] = jnp.concatenate([chunk.T for chunk in changed], axis=0).reshape(
            SUB, TILE, TILE
        )


def leave(at, kept, got, states, *fixed):
    blocks = BLOCKS // GROUPS
    square = pl.BlockSpec((TILE, TILE), lambda block, at: (0, 0))
    tri = pl.BlockSpec((TILE, GROUPS * SUB, TILE), lambda block, at: (0, block, 0))
    return pl.pallas_call(
        leave_kernel,
        grid_spec=pltpu.PrefetchScalarGridSpec(
            num_scalar_prefetch=1,
            grid=(blocks,),
            in_specs=[
                tri,
                tri,
                pl.BlockSpec((GROUPS, TILE, SUB * TILE), lambda block, at: (at[1] * blocks + block, 0, 0)),
            ]
            + [square] * 6,
            out_specs=pl.BlockSpec((GROUPS * SUB, TILE, TILE), lambda block, at: (block, 0, 0)),
            scratch_shapes=[pltpu.VMEM((TILE * PITCH, TILE), jnp.float32)],
        ),
        out_shape=jax.ShapeDtypeStruct((TILE, TILE, TILE), jnp.bfloat16),
        compiler_params=pltpu.CompilerParams(
            dimension_semantics=("arbitrary",), vmem_limit_bytes=VMEM_LIMIT
        ),
        cost_estimate=pl.CostEstimate(
            flops=TILE**3 * 512, bytes_accessed=20 * 2**20, transcendentals=TILE**3
        ),
        name="leave",
    )(at, kept, got, states, *fixed)


def on_device_ring(
    pair_state,
    pair_mask,
    norm_in_gain,
    norm_in_bias,
    proj_in,
    gate_in,
    norm_out_gain,
    norm_out_bias,
    proj_out,
    gate_out,
):
    row = lax.axis_index("row")
    z = lax.axis_index("col")
    x, core = row // 2, row % 2
    place = jnp.where(x == 0, z, 7 - z)

    def device(position, which):
        on_x, on_z = (0, position) if position < 4 else (1, 7 - position)
        return (2 * on_x + which) * 4 + on_z

    up = [(device(p, w), device((p + 1) % 8, w)) for p in range(8) for w in range(2)]
    down = [(target, source) for source, target in up]
    swap = [(device(p, w), device(p, 1 - w)) for p in range(8) for w in range(2)]

    own_mask = pair_mask.astype(jnp.bfloat16)
    sib_mask = lax.ppermute(own_mask, BOTH, swap)
    masks = jnp.where(core == 0, jnp.stack([own_mask, sib_mask]), jnp.stack([sib_mask, own_mask]))

    half = TILE // 2
    ours = core * half
    theirs = half - ours

    def halved(matrix, start, width):
        return (0.5 * lax.dynamic_slice_in_dim(matrix, start, width, axis=1)).T

    enter_weights = jnp.concatenate(
        [halved(m[0], side + ours, half) for m in (proj_in, gate_in) for side in (0, TILE)], axis=0
    )
    middle_weights = jnp.stack(
        [
            jnp.concatenate([halved(m[1], side, TILE) for m in (proj_in, gate_in)], axis=0)
            for side in (0, TILE)
        ]
    )
    identity = jnp.eye(TILE, dtype=jnp.bfloat16)
    both = jnp.concatenate([identity - jnp.bfloat16(1.0 / TILE), identity], axis=0)
    def reordered(values):
        return jnp.concatenate(
            [lax.dynamic_slice_in_dim(values, start, half, axis=0) for start in (ours, theirs)], axis=0
        )

    def columns(values):
        return jnp.broadcast_to(values[:, None], (TILE, TILE))

    gain_in = [columns(norm_in_gain[u]) for u in range(2)]
    bias_in = [columns(norm_in_bias[u]) for u in range(2)]

    def project(held, offset, own, sib, mask, first_block):
        there = lax.rem(place + offset, 8)
        there_x = there // 4
        there_z = jnp.where(there_x == 0, there, 7 - there)
        last = lax.rem(z, 2)
        slot = jnp.where(there_z // 2 == x, lax.rem(there_z, 2), jnp.where(there_z == z, 2, -1))
        at = jnp.stack(
            [
                there_x,
                there_z,
                last,
                (there_x == x).astype(jnp.int32),
                (last == core).astype(jnp.int32),
                jnp.where(slot < 0, -1, 3 * there_x + slot),
            ]
        ).astype(jnp.int32)
        fixed = (both, gain_in[0], bias_in[0], enter_weights)
        return enter(own, sib, first_block, at, mask, *fixed, held)

    def hop(values, pairs):
        return [lax.ppermute(value, BOTH, pairs) for value in values]

    held = project(None, 0, pair_state, lax.ppermute(pair_state, BOTH, swap), masks, 0)
    below = hop([masks, pair_state], up)
    above = hop([masks, pair_state], down)
    part = TILE // 2
    middle_fixed = [
        gain_in[0],
        bias_in[0],
        columns(reordered(norm_out_gain[0])),
        columns(reordered(norm_out_bias[0])),
        0.5 * reordered(proj_out[0]).T,
        0.5 * gate_out[0].T,
        gain_in[1],
        bias_in[1],
        middle_weights,
    ]
    leave_fixed = [
        gain_in[1],
        bias_in[1],
        columns(norm_out_gain[1]),
        columns(norm_out_bias[1]),
        0.5 * proj_out[1].T,
        0.5 * gate_out[1].T,
    ]
    for step in range(1, 4):
        below, above, held, middle_fixed, leave_fixed = lax.optimization_barrier(
            (below, above, held, middle_fixed, leave_fixed)
        )
        now_below, now_above = below, above
        if step < 3:
            below = hop(now_below, up)
            above = hop(now_above, down)
        else:
            below = hop([now_below[0], now_below[1][:part]], up)
            above = hop([now_above[1][part:]], down)
        for offset, (mask, tile) in ((8 - step, now_below), (step, now_above)):
            held = project(held, offset, tile, lax.ppermute(tile, BOTH, swap), mask, 0)
    below, above, held = lax.optimization_barrier((below, above, held))
    held = project(held, 4, below[1], lax.ppermute(below[1], BOTH, swap), below[0], 0)
    held = project(held, 4, above[0], lax.ppermute(above[0], BOTH, swap), below[0], part // (GROUPS * SUB))
    states, *lefts, right, mask = held

    third = jnp.where(z // 2 == x, lax.rem(z, 2), 2)
    at_tri = jnp.stack([core, third]).astype(jnp.int32)
    kept, got = [], []
    for n in range(PARTS):
        if n >= 2:
            at_tri, got[n - 2] = lax.optimization_barrier((at_tri, got[n - 2]))
        stays, leaves = outgoing(at_tri, lefts, right, n)
        kept.append(stays)
        got.append(lax.ppermute(leaves, BOTH, swap))
    parts = kept + got
    at = jnp.stack([core, x, z, third]).astype(jnp.int32)
    pairs, states1 = middle(at, states, mask, middle_fixed, parts)
    kept1, sent1 = incoming(at, pairs)
    got1 = lax.ppermute(sent1, BOTH, swap)
    return leave(at, kept1, got1, states1, *leave_fixed)


def on_device_exchange(
    pair_state,
    pair_mask,
    norm_in_gain,
    norm_in_bias,
    proj_in,
    gate_in,
    norm_out_gain,
    norm_out_bias,
    proj_out,
    gate_out,
):
    mask_weight = pair_mask.astype(jnp.float32)[None]
    current = pair_state
    for update in range(2):
        normed = norm_last(
            current.astype(jnp.float32), norm_in_gain[update], norm_in_bias[update]
        ).astype(jnp.bfloat16)
        projected = jnp.einsum(
            "rcd,de->erc", normed, alternate(proj_in[update]), preferred_element_type=jnp.float32
        )
        gate_logit = jnp.einsum(
            "rcd,de->erc", normed, alternate(gate_in[update]), preferred_element_type=jnp.float32
        )
        paired = (projected * jax.nn.sigmoid(gate_logit) * mask_weight).astype(jnp.bfloat16)
        arrived = spread(paired)
        doubled, total_rows, total_cols = arrived.shape
        pair_count = doubled // 2
        arrived = arrived.reshape(pair_count, 2, total_rows, total_cols)
        left_side = arrived[:, 0]
        right_side = arrived[:, 1]
        pattern = "dik,djk->dij" if update == 0 else "dki,dkj->dij"
        triangle_out = jnp.einsum(
            pattern, left_side, right_side, preferred_element_type=jnp.float32
        ).astype(jnp.bfloat16)
        returned = gather_back(triangle_out)
        normed_out = norm_first(
            returned.astype(jnp.float32), norm_out_gain[update], norm_out_bias[update]
        ).astype(jnp.bfloat16)
        gate_value = jax.nn.sigmoid(
            jnp.einsum("rcd,df->rcf", normed, gate_out[update], preferred_element_type=jnp.float32)
        )
        change = (
            jnp.einsum(
                "erc,ef->rcf", normed_out, proj_out[update], preferred_element_type=jnp.float32
            )
            * gate_value
        )
        current = (current.astype(jnp.float32) + change).astype(jnp.bfloat16)
    return current


def on_device(pair_state, *others):
    square = pair_state.shape == (TILE, TILE, TILE)
    if square and lax.axis_size("row") == 4 and lax.axis_size("col") == 4:
        return on_device_ring(pair_state, *others)
    return on_device_exchange(pair_state, *others)


def solution(mesh):
    return jax.shard_map(
        on_device,
        mesh=mesh,
        in_specs=(
            P(("ens", "row"), "col", None),
            P(("ens", "row"), "col"),
            P(),
            P(),
            P(),
            P(),
            P(),
            P(),
            P(),
            P(),
        ),
        out_specs=P(("ens", "row"), "col", None),
        check_vma=False,
    )
```
